32 devices in a mesh: groups: 2 (over y), dom: 4 (over z), sub: 2 (over x), inner: 2 (over core).
Axes of the slice: x: 2, y: 2, z: 4, core: 2. Of those that a mesh axis runs over, the one named last changes fastest.
Arguments:
- node_state: bfloat16 [8192, 128], P(('groups', 'dom', 'sub')), parts along dimension 0, may hold values from -6 to 6
- edge_state: bfloat16 [49152, 128], P(('groups', 'dom', 'sub', 'inner')), parts along dimension 0, may hold values from -6 to 6
- edge_count: int32 [32], P(('groups', 'dom', 'sub', 'inner')), parts along dimension 0, may hold values from 768 to 1536, as said below
- block_start: int32 [192], P(('groups', 'dom', 'sub', 'inner')), parts along dimension 0, may hold values from 0 to 384, as said below
- edge_offset: int32 [49152], P(('groups', 'dom', 'sub', 'inner')), parts along dimension 0, may hold values from 0 to 127
- edge_other: int32 [49152], P(('groups', 'dom', 'sub', 'inner')), parts along dimension 0, may hold values from 0 to 2047, as said below
- send_index: int32 [4096], P(('groups', 'dom', 'sub')), parts along dimension 0, may hold values from 0 to 511, as said below
- edge_entry: bfloat16 [384, 128], replicated, may hold values from -0.3125 to 0.3125
- edge_middle: bfloat16 [128, 128], replicated, may hold values from -0.5 to 0.5
- edge_outlet: bfloat16 [128, 128], replicated, may hold values from -0.5 to 0.5
- edge_gain: float32 [128], replicated, may hold values from 0.1 to 1.9
- node_entry: bfloat16 [256, 128], replicated, may hold values from -0.375 to 0.375
- node_middle: bfloat16 [128, 128], replicated, may hold values from -0.5 to 0.5
- node_outlet: bfloat16 [128, 128], replicated, may hold values from -0.5 to 0.5
- node_gain: float32 [128], replicated, may hold values from 0.1 to 1.9
- node_cotangent: bfloat16 [8192, 128], P(('groups', 'dom', 'sub')), parts along dimension 0, may hold values from -6 to 6
- edge_cotangent: bfloat16 [49152, 128], P(('groups', 'dom', 'sub', 'inner')), parts along dimension 0, may hold values from -6 to 6
Outputs:
- new_nodes: bfloat16 [8192, 128], P(('groups', 'dom', 'sub')), parts along dimension 0
- new_edges: bfloat16 [49152, 128], P(('groups', 'dom', 'sub', 'inner')), parts along dimension 0
- node_adjoint: bfloat16 [8192, 128], P(('groups', 'dom', 'sub')), parts along dimension 0
- edge_adjoint: bfloat16 [49152, 128], P(('groups', 'dom', 'sub', 'inner')), parts along dimension 0
- edge_gradient: float32 [1280, 128], P('groups'), parts along dimension 0
- node_gradient: float32 [1024, 128], P('groups'), parts along dimension 0
- gain_gradient: float32 [4, 128], P('groups'), parts along dimension 0
The draws below stay inside these ranges and needn't reach their ends.
There are 2 independent parts, one for each index of `groups`. The reference program is written for one: setup_inputs(seed, part) draws one part's arguments, and reference() takes and returns one part's arrays. A program takes and returns all parts, laid end to end along the dimension named above; an argument that names none is the same for every part. Nothing has to cross between parts.
Inputs may be any that keep to these rules, and one draw needn't show every extreme that they name: `edge_count`: number of live slots at the head of each shard; some shard is full and some holds exactly half. `block_start`: each incidence block's window of 128 rows lies inside its node block. `edge_other`: values of 512 or more name border slot s = value - 512 of the slab below (r = 0), the own slab (r = 1) or the slab above (r = 2); the first slab never names r = 0 and the last never r = 2. `send_index`: the 256 rows of one block are distinct.
All inputs are finite; a program needn't handle non-finite values.
Results may differ from the reference program's by a relative error of at most 0.013.
Values may be sent and summed in bfloat16 or wider, within the bound.
No kernel may reach another device: no remote copies, remote signals or barrier semaphores. Data moves between devices by JAX's collectives and lax.ppermute only.
A program may use at most 64 MiB of HBM per device.

```python
import math
import jax
import jax.numpy as jnp
from jax import lax

H = 128
NODE_DEV = 512
EDGE_DEV = 1536
SEND = 256
WINDOW = 128
EBLK = 256
NODE_BLOCKS = 8
SHARDS = 16
NODES = 4096
EDGES = 24576
INC_BLOCKS = 96
N_DOM = 4
N_SUB = 2
N_INNER = 2


def draw_edge_count(key, part):
    key = jax.random.fold_in(key, 3)
    counts = jax.random.randint(key, (SHARDS,), EDGE_DEV // 2, EDGE_DEV + 1)
    counts = counts.at[0].set(EDGE_DEV).at[1].set(EDGE_DEV // 2)
    return counts.astype(jnp.int32)


def draw_block_start(key, part):
    key = jax.random.fold_in(key, 5)
    starts = jax.random.randint(key, (INC_BLOCKS,), 0, NODE_DEV - WINDOW + 1)
    starts = starts.at[0].set(0).at[1].set(NODE_DEV - WINDOW)
    return starts.astype(jnp.int32)


def draw_edge_offset(key, part):
    key = jax.random.fold_in(key, 7)
    offsets = jax.random.randint(key, (EDGES,), 0, WINDOW)
    offsets = offsets.at[0].set(0).at[1].set(WINDOW - 1)
    return offsets.astype(jnp.int32)


def draw_edge_other(key, part):
    key = jax.random.fold_in(key, 11)
    key_slot, key_local, key_pick = jax.random.split(key, 3)
    positions = jnp.arange(EDGES, dtype=jnp.int32)
    within = positions % EDGE_DEV
    slab_id = positions // EDGE_DEV // (N_SUB * N_INNER)
    layer_slots = N_SUB * SEND
    lowest = jnp.where(slab_id > 0, 0, layer_slots)
    highest = jnp.where(slab_id < N_DOM - 1, 3 * layer_slots, 2 * layer_slots)
    raw_slot = jax.random.randint(key_slot, (EDGES,), 0, 1 << 24)
    halo_value = NODE_DEV + lowest + raw_slot % (highest - lowest)
    local_value = jax.random.randint(key_local, (EDGES,), 0, NODE_DEV)
    chosen = jax.random.randint(key_pick, (EDGES,), 0, 4) == 0
    values = jnp.where(chosen, halo_value, local_value)
    values = jnp.where(within == 0, 0, values)
    values = jnp.where(within == 1, NODE_DEV + highest - 1, values)
    return values.astype(jnp.int32)


def draw_send_index(key, part):
    key = jax.random.fold_in(key, 13)
    block_keys = jax.random.split(key, NODE_BLOCKS)
    chosen = jax.vmap(lambda block_key: jax.random.permutation(block_key, NODE_DEV)[:SEND])(block_keys)
    chosen = chosen.astype(jnp.int32)
    anchor = jnp.where(jnp.arange(NODE_BLOCKS, dtype=jnp.int32) % 2 == 0, 0, NODE_DEV - 1)
    values = (chosen - chosen[:, :1] + anchor[:, None]) % NODE_DEV
    return values.reshape(-1).astype(jnp.int32)


def level_of(own_key, extent, pieces, low, high):
    level = 1.0
    for axis_at, parts in pieces:
        heights = jax.random.uniform(jax.random.fold_in(jax.random.fold_in(own_key, 6), axis_at), (parts,), jnp.float32, low / len(pieces), high / len(pieces))
        level = level * jnp.repeat(jnp.exp(heights), extent[axis_at] // parts).reshape((-1,) + (1,) * (len(extent) - 1 - axis_at))
    return level


def bell_draw(key, extent, deviation, most, cuts=(), kind=jnp.bfloat16):
    loudness = level_of(key, extent, cuts, -0.22, 0.18) if cuts else 1.0
    result = jax.random.normal(key, extent, jnp.float32) * deviation * loudness
    return jnp.minimum(jnp.maximum(result, -most), most).astype(kind)


def setup_inputs(seed: int = 0, part: int = 0) -> dict:
    key_list = jax.random.split(jax.random.key(seed), 18)
    part_keys = jax.random.split(jax.random.fold_in(key_list[17], part), 18)
    node_state = bell_draw(part_keys[0], (NODES, H), 1.0, 6.0, ((0, 8),))
    edge_state = bell_draw(part_keys[1], (EDGES, H), 1.0, 6.0, ((0, 16),))
    edge_count = draw_edge_count(jax.random.fold_in(jax.random.fold_in(key_list[17], part), 71), part)
    block_start = draw_block_start(jax.random.fold_in(jax.random.fold_in(key_list[17], part), 71), part)
    edge_offset = draw_edge_offset(jax.random.fold_in(jax.random.fold_in(key_list[17], part), 71), part)
    edge_other = draw_edge_other(jax.random.fold_in(jax.random.fold_in(key_list[17], part), 71), part)
    send_index = draw_send_index(jax.random.fold_in(jax.random.fold_in(key_list[17], part), 71), part)
    edge_entry = bell_draw(key_list[7], (3 * H, H), (3 * H) ** -0.5, 0.3125)
    edge_middle = bell_draw(key_list[8], (H, H), H ** -0.5, 0.5)
    edge_outlet = bell_draw(key_list[9], (H, H), H ** -0.5, 0.5)
    edge_gain = jnp.clip(1.0 + 0.18 * jax.random.normal(key_list[10], (H,), jnp.float32), 0.1, 1.9)
    node_entry = bell_draw(key_list[11], (2 * H, H), (2 * H) ** -0.5, 0.375)
    node_middle = bell_draw(key_list[12], (H, H), H ** -0.5, 0.5)
    node_outlet = bell_draw(key_list[13], (H, H), H ** -0.5, 0.5)
    node_gain = jnp.clip(1.0 + 0.18 * jax.random.normal(key_list[14], (H,), jnp.float32), 0.1, 1.9)
    node_cotangent = bell_draw(part_keys[15], (NODES, H), 1.0, 6.0, ((0, 8),))
    edge_cotangent = bell_draw(part_keys[16], (EDGES, H), 1.0, 6.0, ((0, 16),))
    return dict(node_state=node_state, edge_state=edge_state, edge_count=edge_count, block_start=block_start, edge_offset=edge_offset, edge_other=edge_other, send_index=send_index, edge_entry=edge_entry, edge_middle=edge_middle, edge_outlet=edge_outlet, edge_gain=edge_gain, node_entry=node_entry, node_middle=node_middle, node_outlet=node_outlet, node_gain=node_gain, node_cotangent=node_cotangent, edge_cotangent=edge_cotangent)


EPS = 1e-05

def silu_pair(pre_act):
    logistic = jax.nn.sigmoid(pre_act)
    return (pre_act * logistic, logistic * (1.0 + pre_act * (1.0 - logistic)))

def matmul(left, right):
    return jnp.dot(left, right, preferred_element_type=jnp.float32)

def contract(left, right):
    return jnp.dot(left.T, right, preferred_element_type=jnp.float32)

def transposed(left, right):
    return jnp.dot(left, right.T, preferred_element_type=jnp.float32)

def mlp_forward(inputs, entry_weight, middle_weight, outlet_weight):
    first_act, first_slope = silu_pair(matmul(inputs, entry_weight))
    first_hidden = first_act.astype(jnp.bfloat16)
    second_act, second_slope = silu_pair(matmul(first_hidden, middle_weight))
    second_hidden = second_act.astype(jnp.bfloat16)
    output_pre = matmul(second_hidden, outlet_weight)
    centred = output_pre - lax.optimization_barrier(jnp.mean(output_pre, axis=-1, keepdims=True))
    inverse = lax.rsqrt(lax.optimization_barrier(jnp.mean(centred * centred, axis=-1, keepdims=True)) + EPS)
    normed = centred * inverse
    return (normed, (first_hidden, second_hidden, first_slope, second_slope, inverse))

def mlp_backward(upstream, inputs, entry_weight, middle_weight, outlet_weight, gain_vec, normed, saved):
    first_hidden, second_hidden, first_slope, second_slope, inverse = saved
    gain_grad = lax.optimization_barrier(jnp.sum(upstream * normed, axis=0))
    scaled = upstream * gain_vec
    output_grad = inverse * (scaled - lax.optimization_barrier(jnp.mean(scaled, axis=-1, keepdims=True)) - normed * lax.optimization_barrier(jnp.mean(scaled * normed, axis=-1, keepdims=True)))
    output_grad = output_grad.astype(jnp.bfloat16)
    outlet_grad = contract(second_hidden, output_grad)
    second_grad = (transposed(output_grad, outlet_weight) * second_slope).astype(jnp.bfloat16)
    middle_grad = contract(first_hidden, second_grad)
    first_grad = (transposed(second_grad, middle_weight) * first_slope).astype(jnp.bfloat16)
    entry_grad = contract(inputs, first_grad)
    input_grad = transposed(first_grad, entry_weight)
    return (input_grad, (entry_grad, middle_grad, outlet_grad, gain_grad))

def round_trip(values):
    return lax.optimization_barrier(values.astype(jnp.bfloat16)).astype(jnp.float32)

def reference(node_state, edge_state, edge_count, block_start, edge_offset, edge_other, send_index, edge_entry, edge_middle, edge_outlet, edge_gain, node_entry, node_middle, node_outlet, node_gain, node_cotangent, edge_cotangent):
    positions = jnp.arange(EDGES, dtype=jnp.int32)
    shard_id = positions // EDGE_DEV
    node_block = shard_id // N_INNER
    slab_id = node_block // N_SUB
    is_live = (positions % EDGE_DEV < edge_count[shard_id]).astype(jnp.float32)[:, None]
    near_end = node_block * NODE_DEV + block_start[positions // EBLK] + edge_offset
    halo_slot = edge_other - NODE_DEV
    layer_slots = N_SUB * SEND
    offset_slab = halo_slot // layer_slots
    peer_sub = halo_slot // SEND % N_SUB
    peer_block = (slab_id + offset_slab - 1) * N_SUB + peer_sub
    lookup = jnp.clip(peer_block * SEND + halo_slot % SEND, 0, NODE_BLOCKS * SEND - 1).astype(jnp.int32)
    remote_end = peer_block * NODE_DEV + send_index[lookup]
    far_end = jnp.where(edge_other < NODE_DEV, node_block * NODE_DEV + edge_other, remote_end).astype(jnp.int32)
    node_float = node_state.astype(jnp.float32)
    near_rows = node_float[near_end].astype(jnp.bfloat16)
    far_rows = node_float[far_end].astype(jnp.bfloat16)
    edge_inputs = jnp.concatenate([edge_state, near_rows, far_rows], axis=1)
    edge_normed, edge_saved = mlp_forward(edge_inputs, edge_entry, edge_middle, edge_outlet)
    new_edges = (edge_state.astype(jnp.float32) + is_live * edge_gain * edge_normed).astype(jnp.bfloat16)
    messages = new_edges.astype(jnp.float32) * is_live
    totals = jnp.zeros((NODES, H), jnp.float32).at[near_end].add(messages).at[far_end].add(messages)
    node_inputs = jnp.concatenate([node_state, totals.astype(jnp.bfloat16)], axis=1)
    node_normed, node_saved = mlp_forward(node_inputs, node_entry, node_middle, node_outlet)
    new_nodes = (node_float + node_gain * node_normed).astype(jnp.bfloat16)
    node_upstream = node_cotangent.astype(jnp.float32)
    node_input_grad, node_weight_grads = mlp_backward(node_upstream, node_inputs, node_entry, node_middle, node_outlet, node_gain, node_normed, node_saved)
    pull_rows = round_trip(node_input_grad[:, H:])
    edge_upstream = edge_cotangent.astype(jnp.float32) + is_live * (pull_rows[near_end] + pull_rows[far_end])
    edge_input_grad, edge_weight_grads = mlp_backward(is_live * edge_upstream, edge_inputs, edge_entry, edge_middle, edge_outlet, edge_gain, edge_normed, edge_saved)
    edge_adjoint = (edge_upstream + edge_input_grad[:, :H]).astype(jnp.bfloat16)
    near_grad = round_trip(edge_input_grad[:, H:2 * H])
    far_grad = round_trip(edge_input_grad[:, 2 * H:])
    node_sums = node_upstream + node_input_grad[:, :H]
    node_sums = node_sums.at[near_end].add(near_grad).at[far_end].add(far_grad)
    node_adjoint = node_sums.astype(jnp.bfloat16)
    edge_scale = 1.0 / math.sqrt(EDGES)
    node_scale = 1.0 / math.sqrt(NODES)
    edge_gradient = jnp.concatenate(list(edge_weight_grads[:3]), axis=0) * edge_scale
    node_gradient = jnp.concatenate(list(node_weight_grads[:3]), axis=0) * node_scale
    gain_gradient = jnp.stack([edge_weight_grads[3] * edge_scale, node_weight_grads[3] * node_scale])
    return (new_nodes, new_edges, node_adjoint, edge_adjoint, edge_gradient, node_gradient, gain_gradient)
```

```python
import math

import jax
import jax.numpy as jnp
from jax import lax
from jax.experimental import pallas as pl
from jax.experimental.pallas import tpu as pltpu
from jax.sharding import PartitionSpec as P

EPS = 1e-05
BF = jnp.bfloat16
F32 = jnp.float32
AXES = ("dom", "sub", "inner")
VMEM_LIMIT = 48 * 1024 * 1024


def mm(left, right):
    return jnp.dot(left, right, preferred_element_type=F32)


def mm_tn(left, right):
    return lax.dot_general(left, right, (((0,), (0,)), ((), ())), preferred_element_type=F32)


def mm_nt(left, right):
    return lax.dot_general(left, right, (((1,), (1,)), ((), ())), preferred_element_type=F32)


def silu_pair(pre_act):
    logistic = jax.nn.sigmoid(pre_act)
    act = pre_act * logistic
    return act, logistic + act * (1.0 - logistic)


def layer_norm(output_pre):
    centred = output_pre - jnp.mean(output_pre, axis=-1, keepdims=True)
    inverse = lax.rsqrt(jnp.mean(centred * centred, axis=-1, keepdims=True) + EPS)
    return centred * inverse, inverse


def norm_backward(scaled, normed, inverse):
    return inverse * (
        scaled
        - jnp.mean(scaled, axis=-1, keepdims=True)
        - normed * jnp.mean(scaled * normed, axis=-1, keepdims=True)
    )


def hot_rows(index_row, rows, base=0):
    place = lax.broadcasted_iota(jnp.int32, (rows, index_row.shape[1]), 0) + base
    return jnp.where(place == index_row, 1.0, 0.0).astype(BF)


def hot_cols(index_col, cols, base=0):
    place = lax.broadcasted_iota(jnp.int32, (index_col.shape[0], cols), 1) + base
    return jnp.where(place == index_col, 1.0, 0.0).astype(BF)


def column(row):
    wide = jnp.broadcast_to(row, (8, row.shape[1]))
    return jnp.transpose(wide)[:, :1]


class Layout:
    def __init__(self, nodes, send):
        self.nodes, self.send = nodes, send
        self.sub = lax.axis_size("sub")
        self.dom = lax.axis_size("dom")
        self.groups = [(a, x) for a in range(3) for x in range(self.sub)]
        self.remote = self.groups[1:]
        self.halo = len(self.remote) * send

    def place(self, other):
        d, t = lax.axis_index("dom"), lax.axis_index("sub")
        slot = jnp.maximum(other - self.nodes, 0)
        layer = slot // (self.sub * self.send)
        rest = slot - layer * (self.sub * self.send)
        peer = rest // self.send
        k = rest - peer * self.send
        upper = (layer == 2).astype(jnp.int32)
        even = 1 - lax.rem(d, 2)
        swap = jnp.where(layer == 1, 0, jnp.where(upper == even, 1, 2))
        row = self.nodes + (swap * self.sub + (peer ^ t)) * self.send + k
        return jnp.where(other < self.nodes, other, row)

    def exchange(self, arrays):
        inner = lax.axis_size("inner")
        out = []
        for (a, x), value in zip(self.remote, arrays):
            pairs = []
            for d in range(self.dom):
                other = d if a == 0 else (d ^ 1 if a == 1 else ((d + 1) ^ 1) - 1)
                if not 0 <= other < self.dom:
                    continue
                for t in range(self.sub):
                    for i in range(inner):
                        pairs.append(
                            (
                                (d * self.sub + t) * inner + i,
                                (other * self.sub + (t ^ x)) * inner + i,
                            )
                        )
            out.append(lax.ppermute(value, AXES, pairs))
        return out


def swap_axis(value, axis, mask):
    count = lax.axis_size(axis)
    return lax.ppermute(value, axis, [(j, j ^ mask) for j in range(count)])


def call(body, outs, *args, smem=(), scratch=(), flops=0):
    specs = [
        pl.BlockSpec(memory_space=pltpu.SMEM if j in smem else pltpu.VMEM)
        for j in range(len(args))
    ]
    size = sum(math.prod(a.shape) * a.dtype.itemsize for a in (*args, *outs))
    return pl.pallas_call(
        body,
        out_shape=outs,
        in_specs=specs,
        out_specs=[pl.BlockSpec(memory_space=pltpu.VMEM) for _ in outs],
        scratch_shapes=list(scratch),
        compiler_params=pltpu.CompilerParams(vmem_limit_bytes=VMEM_LIMIT),
        cost_estimate=pl.CostEstimate(flops=flops, bytes_accessed=size, transcendentals=0),
    )(*args)


def shape(rows, cols, dtype):
    return jax.ShapeDtypeStruct((rows, cols), dtype)


def border_kernel(send_ref, table_ref, out_ref):
    hot = hot_rows(send_ref[...], table_ref.shape[0])
    out_ref[...] = mm_tn(hot, table_ref[...]).astype(BF)


def near_row(offset_ref, start_ref, b):
    return offset_ref[b : b + 1, :] + start_ref[b]


def live_column(count_ref, b, size):
    return lax.broadcasted_iota(jnp.int32, (size, 1), 0) + b * size < count_ref[0]


def per_device(
    node_state,
    edge_state,
    edge_count,
    block_start,
    edge_offset,
    edge_other,
    send_index,
    edge_entry,
    edge_middle,
    edge_outlet,
    edge_gain,
    node_entry,
    node_middle,
    node_outlet,
    node_gain,
    node_cotangent,
    edge_cotangent,
):
    nodes, feat = node_state.shape
    edges = edge_state.shape[0]
    blocks = block_start.shape[0]
    size = edges // blocks
    send = send_index.shape[0]
    lay = Layout(nodes, send)
    remote = len(lay.remote)
    halo_base = nodes + send
    f = feat

    offset = edge_offset.reshape(blocks, size)
    other = edge_other.reshape(blocks, size)
    sends = send_index.reshape(1, send)
    gain_e = edge_gain.reshape(1, f)
    gain_n = node_gain.reshape(1, f)

    (border,) = call(border_kernel, [shape(send, f, BF)], sends, node_state)
    halo = lay.exchange([border] * remote)

    def edge_local(
        off_ref, oth_ref, start_ref, node_ref, border_ref, edge_ref, entry_ref,
        near_ref, far_ref, pre_ref, place_ref,
    ):
        place_ref[...] = lay.place(oth_ref[...])
        for b in range(blocks):
            rows = pl.ds(b * size, size)
            near = hot_cols(column(near_row(off_ref, start_ref, b)), nodes)
            near = mm(near, node_ref[...]).astype(BF)
            far = hot_cols(column(place_ref[b : b + 1, :]), nodes + send)
            far = mm(far[:, :nodes], node_ref[...]) + mm(far[:, nodes:], border_ref[...])
            near_ref[rows, :] = near
            far_ref[rows, :] = far.astype(BF)
            pre_ref[rows, :] = mm(edge_ref[rows, :], entry_ref[:f, :]) + mm(
                near, entry_ref[f : 2 * f, :]
            )

    near_rows, far_own, pre_own, place = call(
        edge_local,
        [
            shape(edges, f, BF),
            shape(edges, f, BF),
            shape(edges, f, F32),
            shape(blocks, size, jnp.int32),
        ],
        offset, other, block_start, node_state, border, edge_state, edge_entry,
        smem=(2,),
        flops=2 * edges * f * (2 * nodes + send + 2 * f),
    )

    def edge_forward(*refs):
        (place_ref, count_ref, edge_ref, far_own_ref, pre_ref, entry_ref, middle_ref,
         outlet_ref, gain_ref) = refs[:9]
        halo_refs = refs[9 : 9 + remote]
        (new_ref, message_ref, far_ref, h1_ref, h2_ref, s1_ref, s2_ref, normed_ref,
         inverse_ref) = refs[9 + remote : 18 + remote]
        slot_refs = refs[18 + remote : 18 + 2 * remote]
        table, sums = refs[18 + 2 * remote :]
        for j in range(remote):
            table[pl.ds(j * send, send), :] = halo_refs[j][...]
        for b in range(blocks):
            rows = pl.ds(b * size, size)
            place_b = place_ref[b : b + 1, :]
            hot = hot_cols(column(place_b), lay.halo, halo_base)
            far = (mm(hot, table[...]) + far_own_ref[rows, :].astype(F32)).astype(BF)
            far_ref[rows, :] = far
            act, slope = silu_pair(pre_ref[rows, :] + mm(far, entry_ref[2 * f :, :]))
            h1 = act.astype(BF)
            h1_ref[rows, :] = h1
            s1_ref[rows, :] = slope
            act, slope = silu_pair(mm(h1, middle_ref[...]))
            h2 = act.astype(BF)
            h2_ref[rows, :] = h2
            s2_ref[rows, :] = slope
            normed, inverse = layer_norm(mm(h2, outlet_ref[...]))
            normed_ref[rows, :] = normed
            inverse_ref[rows, :] = inverse
            live = jnp.where(live_column(count_ref, b, size), 1.0, 0.0)
            state = edge_ref[rows, :].astype(F32)
            new = (state + live * gain_ref[...] * normed).astype(BF)
            new_ref[rows, :] = new
            message = (new.astype(F32) * live).astype(BF)
            message_ref[rows, :] = message
            part = mm(hot_rows(place_b, lay.halo, halo_base), message)
            if b == 0:
                sums[...] = part
            else:
                sums[...] += part
        for j in range(remote):
            slot_refs[j][...] = sums[pl.ds(j * send, send), :].astype(BF)

    edge_outs = call(
        edge_forward,
        [
            shape(edges, f, BF),
            shape(edges, f, BF),
            shape(edges, f, BF),
            shape(edges, f, BF),
            shape(edges, f, BF),
            shape(edges, f, F32),
            shape(edges, f, F32),
            shape(edges, f, F32),
            shape(edges, 1, F32),
        ]
        + [shape(send, f, BF)] * remote,
        place, edge_count, edge_state, far_own, pre_own, edge_entry, edge_middle, edge_outlet,
        gain_e, *halo,
        smem=(1,),
        scratch=[pltpu.VMEM((lay.halo, f), BF), pltpu.VMEM((lay.halo, f), F32)],
        flops=2 * edges * f * (2 * lay.halo + 3 * f),
    )
    new_edges, message, far_rows, h1, h2, s1, s2, normed, inverse = edge_outs[:9]
    received = lay.exchange(edge_outs[9:])

    def local_sums(off_ref, place_ref, start_ref, send_ref, near_ref, far_ref, out_ref):
        slot = jnp.zeros((send, f), F32)
        total = jnp.zeros((nodes, f), F32)
        for b in range(blocks):
            rows = pl.ds(b * size, size)
            place_b = place_ref[b : b + 1, :]
            total += mm(hot_rows(near_row(off_ref, start_ref, b), nodes), near_ref[rows, :])
            hot = hot_rows(place_b, nodes + send)
            total += mm(hot[:nodes], far_ref[rows, :])
            slot += mm(hot[nodes:], far_ref[rows, :])
        out_ref[...] = total + mm(hot_rows(send_ref[...], nodes), slot.astype(BF))

    def gather_back(near, far):
        (out,) = call(
            local_sums,
            [shape(nodes, f, F32)],
            offset, place, block_start, sends, near, far,
            smem=(2,),
            flops=2 * edges * f * (2 * nodes + send),
        )
        return out

    def join_kernel(send_ref, own_ref, *refs):
        hot = hot_rows(send_ref[...], nodes)
        total = own_ref[...]
        for ref in refs[:-1]:
            total += mm(hot, ref[...])
        refs[-1][...] = total.astype(BF)

    def join(own, arrived):
        (out,) = call(
            join_kernel, [shape(nodes, f, BF)], sends, own, *arrived,
            flops=2 * nodes * send * f * remote,
        )
        return out, swap_axis(out, "inner", 1)

    part, part_other = join(gather_back(message, message), received)

    def node_kernel(
        part_ref, other_ref, node_ref, cot_ref, send_ref, entry_ref, middle_ref, outlet_ref,
        gain_ref, new_ref, pulls_ref, border_ref, direct_ref, weight_ref, gain_grad_ref,
    ):
        totals = (part_ref[...].astype(F32) + other_ref[...].astype(F32)).astype(BF)
        state = node_ref[...]
        act, s1n = silu_pair(mm(state, entry_ref[:f, :]) + mm(totals, entry_ref[f:, :]))
        h1n = act.astype(BF)
        act, s2n = silu_pair(mm(h1n, middle_ref[...]))
        h2n = act.astype(BF)
        normed_n, inverse_n = layer_norm(mm(h2n, outlet_ref[...]))
        new_ref[...] = (state.astype(F32) + gain_ref[...] * normed_n).astype(BF)
        up = cot_ref[...].astype(F32)
        og = norm_backward(up * gain_ref[...], normed_n, inverse_n).astype(BF)
        second = (mm_nt(og, outlet_ref[...]) * s2n).astype(BF)
        first = (mm_nt(second, middle_ref[...]) * s1n).astype(BF)
        pulls = mm_nt(first, entry_ref[f:, :]).astype(BF)
        pulls_ref[...] = pulls
        border_ref[...] = mm_tn(hot_rows(send_ref[...], nodes), pulls).astype(BF)
        direct_ref[...] = up + mm_nt(first, entry_ref[:f, :])
        weight_ref[:f, :] = mm_tn(state, first)
        weight_ref[f : 2 * f, :] = mm_tn(totals, first)
        weight_ref[2 * f : 3 * f, :] = mm_tn(h1n, second)
        weight_ref[3 * f :, :] = mm_tn(h2n, og)
        gain_grad_ref[...] = jnp.sum(up * normed_n, axis=0, keepdims=True)

    own_new, pulls, pull_border, direct, node_weights, node_gain_grad = call(
        node_kernel,
        [
            shape(nodes, f, BF),
            shape(nodes, f, BF),
            shape(send, f, BF),
            shape(nodes, f, F32),
            shape(4 * f, f, F32),
            shape(1, f, F32),
        ],
        part, part_other, node_state, node_cotangent, sends, node_entry, node_middle,
        node_outlet, gain_n,
        flops=2 * nodes * f * f * 12,
    )
    pull_halo = lay.exchange([pull_border] * remote)

    def pull_local(
        off_ref, place_ref, start_ref, count_ref, pulls_ref, border_ref, cot_ref, up_ref
    ):
        for b in range(blocks):
            rows = pl.ds(b * size, size)
            near = hot_cols(column(near_row(off_ref, start_ref, b)), nodes)
            far = hot_cols(column(place_ref[b : b + 1, :]), nodes + send)
            got = mm(near + far[:, :nodes], pulls_ref[...]) + mm(far[:, nodes:], border_ref[...])
            live = jnp.where(live_column(count_ref, b, size), 1.0, 0.0)
            up_ref[rows, :] = cot_ref[rows, :].astype(F32) + live * got

    (up_own,) = call(
        pull_local,
        [shape(edges, f, F32)],
        offset, place, block_start, edge_count, pulls, pull_border, edge_cotangent,
        smem=(2, 3),
        flops=2 * edges * f * (nodes + send),
    )

    def edge_backward(*refs):
        (place_ref, count_ref, up_own_ref, normed_ref, inverse_ref, s1_ref, s2_ref, entry_ref,
         middle_ref, outlet_ref, gain_ref) = refs[:11]
        halo_refs = refs[11 : 11 + remote]
        (adjoint_ref, near_ref, far_ref, first_ref, second_ref, og_ref, gain_grad_ref) = refs[
            11 + remote : 18 + remote
        ]
        slot_refs = refs[18 + remote : 18 + 2 * remote]
        table, sums = refs[18 + 2 * remote :]
        for j in range(remote):
            table[pl.ds(j * send, send), :] = halo_refs[j][...]
        gain_sum = jnp.zeros((1, f), F32)
        for b in range(blocks):
            rows = pl.ds(b * size, size)
            place_b = place_ref[b : b + 1, :]
            live = jnp.where(live_column(count_ref, b, size), 1.0, 0.0)
            hot = hot_cols(column(place_b), lay.halo, halo_base)
            up = up_own_ref[rows, :] + live * mm(hot, table[...])
            into = live * up
            normed_b = normed_ref[rows, :]
            gain_sum += jnp.sum(into * normed_b, axis=0, keepdims=True)
            og = norm_backward(into * gain_ref[...], normed_b, inverse_ref[rows, :]).astype(BF)
            og_ref[rows, :] = og
            second = (mm_nt(og, outlet_ref[...]) * s2_ref[rows, :]).astype(BF)
            second_ref[rows, :] = second
            first = (mm_nt(second, middle_ref[...]) * s1_ref[rows, :]).astype(BF)
            first_ref[rows, :] = first
            adjoint_ref[rows, :] = (up + mm_nt(first, entry_ref[:f, :])).astype(BF)
            near_ref[rows, :] = mm_nt(first, entry_ref[f : 2 * f, :]).astype(BF)
            far = mm_nt(first, entry_ref[2 * f :, :]).astype(BF)
            far_ref[rows, :] = far
            part = mm(hot_rows(place_b, lay.halo, halo_base), far)
            if b == 0:
                sums[...] = part
            else:
                sums[...] += part
        gain_grad_ref[...] = gain_sum
        for j in range(remote):
            slot_refs[j][...] = sums[pl.ds(j * send, send), :].astype(BF)

    back_outs = call(
        edge_backward,
        [shape(edges, f, BF)] * 6 + [shape(1, f, F32)] + [shape(send, f, BF)] * remote,
        place, edge_count, up_own, normed, inverse, s1, s2, edge_entry, edge_middle, edge_outlet,
        gain_e, *pull_halo,
        smem=(1,),
        scratch=[pltpu.VMEM((lay.halo, f), BF), pltpu.VMEM((lay.halo, f), F32)],
        flops=2 * edges * f * (2 * lay.halo + 5 * f),
    )
    edge_adjoint, near_grad, far_grad, first_grad, second_grad, output_grad = back_outs[:6]
    edge_gain_grad = back_outs[6]
    back_received = lay.exchange(back_outs[7:])

    subs = lax.axis_size("sub")
    doms = lax.axis_size("dom")
    inners = lax.axis_size("inner")
    weight_rows = 9 * f + 16
    unit = 16 * inners * subs
    weight_rows = -(-weight_rows // unit) * unit
    half = weight_rows // 2
    piece = half // subs
    block_total = doms * subs
    edge_scale = 1.0 / math.sqrt(edges * block_total * inners)
    node_scale = 1.0 / math.sqrt(nodes * block_total)

    def weight_kernel(
        edge_ref, near_ref, far_ref, h1_ref, h2_ref, first_ref, second_ref, og_ref, node_ref,
        edge_gain_ref, node_gain_ref, keep_ref, give_ref, acc,
    ):
        first = first_ref[...]
        acc[:f, :] = mm_tn(edge_ref[...], first).astype(BF)
        acc[f : 2 * f, :] = mm_tn(near_ref[...], first).astype(BF)
        acc[2 * f : 3 * f, :] = mm_tn(far_ref[...], first).astype(BF)
        acc[3 * f : 4 * f, :] = mm_tn(h1_ref[...], second_ref[...]).astype(BF)
        acc[4 * f : 5 * f, :] = mm_tn(h2_ref[...], og_ref[...]).astype(BF)
        acc[5 * f : 9 * f, :] = (node_ref[...] * 0.5).astype(BF)
        row = lax.broadcasted_iota(jnp.int32, (weight_rows - 9 * f, f), 0)
        gains = jnp.where(row == 0, edge_gain_ref[...], 0.0)
        gains = jnp.where(row == 1, node_gain_ref[...] * 0.5, gains)
        acc[9 * f :, :] = gains.astype(BF)
        me = lax.axis_index("inner")
        keep_ref[...] = acc[pl.ds(pl.multiple_of(me * half, 16), half), :]
        give_ref[...] = acc[pl.ds(pl.multiple_of((1 - me) * half, 16), half), :]

    keep, give = call(
        weight_kernel,
        [shape(half, f, BF)] * 2,
        edge_state, near_rows, far_rows, h1, h2, first_grad, second_grad, output_grad,
        node_weights, edge_gain_grad, node_gain_grad,
        scratch=[pltpu.VMEM((weight_rows, f), BF)],
        flops=2 * edges * f * f * 5,
    )

    def split_kernel(keep_ref, got_ref, *refs):
        out_refs, acc = refs[:-1], refs[-1]
        acc[...] = (keep_ref[...].astype(F32) + got_ref[...].astype(F32)).astype(BF)
        t = lax.axis_index("sub")
        for x in range(subs):
            out_refs[x][...] = acc[pl.ds(pl.multiple_of((t ^ x) * piece, 16), piece), :]

    pieces = call(
        split_kernel,
        [shape(piece, f, BF)] * subs,
        keep, swap_axis(give, "inner", 1),
        scratch=[pltpu.VMEM((half, f), BF)],
    )
    arrived = [pieces[0]] + [swap_axis(pieces[x], "sub", x) for x in range(1, subs)]

    def add_all(values):
        values = [v.astype(F32) for v in values]
        while len(values) > 1:
            values = [values[j] + values[j + 1] for j in range(0, len(values), 2)]
        return values[0]

    total = add_all(arrived)
    stride = 1
    while stride < doms:
        step = 4 if stride * 4 <= doms else 2
        sent = total.astype(BF)
        total = add_all(
            [sent] + [swap_axis(sent, "dom", stride * m) for m in range(1, step)]
        )
        stride *= step
    sent = total.astype(BF)
    own_pieces = [sent] + [swap_axis(sent, "sub", x) for x in range(1, subs)]

    def order_kernel(*refs):
        t = lax.axis_index("sub")
        for x in range(subs):
            refs[-1][pl.ds(pl.multiple_of((t ^ x) * piece, 16), piece), :] = refs[x][...]

    (own_half,) = call(order_kernel, [shape(half, f, BF)], *own_pieces)
    other_half = swap_axis(own_half, "inner", 1)

    def finish_kernel(own_ref, other_ref, edge_ref, node_ref, gain_ref, acc):
        me = lax.axis_index("inner")
        acc[pl.ds(pl.multiple_of(me * half, 16), half), :] = own_ref[...]
        acc[pl.ds(pl.multiple_of((1 - me) * half, 16), half), :] = other_ref[...]
        edge_ref[...] = acc[: 5 * f, :].astype(F32) * edge_scale
        node_ref[...] = acc[5 * f : 9 * f, :].astype(F32) * node_scale
        tail = acc[9 * f : 9 * f + 16, :].astype(F32)
        gain_ref[0:1, :] = tail[0:1, :] * edge_scale
        gain_ref[1:2, :] = tail[1:2, :] * node_scale

    edge_gradient, node_gradient, gain_gradient = call(
        finish_kernel,
        [shape(5 * f, f, F32), shape(4 * f, f, F32), shape(2, f, F32)],
        own_half, other_half,
        scratch=[pltpu.VMEM((weight_rows, f), BF)],
    )

    back, back_other = join(gather_back(near_grad, far_grad), back_received)
    node_adjoint = (back.astype(F32) + back_other.astype(F32) + direct).astype(BF)
    return (
        own_new,
        new_edges,
        node_adjoint,
        edge_adjoint,
        edge_gradient,
        node_gradient,
        gain_gradient,
    )


def solution(mesh):
    nodes = P(("groups", "dom", "sub"), None)
    edges = P(("groups", "dom", "sub", "inner"), None)
    slots = P(("groups", "dom", "sub", "inner"))
    return jax.shard_map(
        per_device,
        mesh=mesh,
        in_specs=(
            nodes,
            edges,
            slots,
            slots,
            slots,
            slots,
            P(("groups", "dom", "sub")),
            P(),
            P(),
            P(),
            P(),
            P(),
            P(),
            P(),
            P(),
            nodes,
            edges,
        ),
        out_specs=(
            nodes,
            edges,
            nodes,
            edges,
            P("groups", None),
            P("groups", None),
            P("groups", None),
        ),
        check_vma=False,
    )
```

```python
import math

import jax
import jax.numpy as jnp
from jax import lax
from jax.experimental import pallas as pl
from jax.experimental.pallas import tpu as pltpu
from jax.sharding import PartitionSpec as P

EPS = 1e-05
BF = jnp.bfloat16
F32 = jnp.float32
AXES = ("dom", "sub", "inner")
VMEM_LIMIT = 16 * 1024 * 1024


def mm(left, right):
    return jnp.dot(left, right, preferred_element_type=F32)


def mm_tn(left, right):
    return lax.dot_general(left, right, (((0,), (0,)), ((), ())), preferred_element_type=F32)


def mm_nt(left, right):
    return lax.dot_general(left, right, (((1,), (1,)), ((), ())), preferred_element_type=F32)


def silu_pair(pre_act):
    logistic = jax.nn.sigmoid(pre_act)
    act = pre_act * logistic
    return act, logistic + act * (1.0 - logistic)


def layer_norm(output_pre):
    centred = output_pre - jnp.mean(output_pre, axis=-1, keepdims=True)
    inverse = lax.rsqrt(jnp.mean(centred * centred, axis=-1, keepdims=True) + EPS)
    return centred * inverse, inverse


def norm_backward(scaled, normed, inverse):
    return inverse * (
        scaled
        - jnp.mean(scaled, axis=-1, keepdims=True)
        - normed * jnp.mean(scaled * normed, axis=-1, keepdims=True)
    )


def hot_rows(index_row, rows):
    place = lax.broadcasted_iota(jnp.int32, (rows, index_row.shape[1]), 0)
    return jnp.where(place == index_row, 1.0, 0.0).astype(BF)


def folded_hot(index_row, rows):
    return hot_rows(jnp.where(index_row >= rows, index_row - rows, index_row), rows)


def fold(table):
    rows = table.shape[0] // 2
    return jnp.concatenate([table[:rows], table[rows:]], axis=1)


def unfold(table):
    f = table.shape[1] // 2
    return jnp.concatenate([table[:, :f], table[:, f:]], axis=0)


def gather_folded(index_row, index_col, table):
    rows, f = table.shape[0], table.shape[1] // 2
    got = mm_tn(folded_hot(index_row, rows), table)
    return jnp.where(index_col >= rows, got[:, f:], got[:, :f])


def halves(values, index_col, rows):
    upper = index_col >= rows
    zero = jnp.zeros_like(values)
    return jnp.concatenate(
        [jnp.where(upper, zero, values), jnp.where(upper, values, zero)], axis=1
    ).astype(BF)


def column(row):
    wide = jnp.broadcast_to(row, (8, row.shape[1]))
    return jnp.transpose(wide)[:, :1]


class Layout:
    def __init__(self, nodes, send):
        self.nodes, self.send = nodes, send
        self.sub = lax.axis_size("sub")
        self.dom = lax.axis_size("dom")
        across = range(1, self.sub)
        self.remote = [(2, 0), (1, 0)]
        self.remote += [(0, x) for x in across]
        self.remote += [(2, x) for x in across] + [(1, x) for x in across]
        self.halo = len(self.remote) * send

    def place(self, other):
        d, t = lax.axis_index("dom"), lax.axis_index("sub")
        slot = jnp.maximum(other - self.nodes, 0)
        layer = slot // (self.sub * self.send)
        rest = slot - layer * (self.sub * self.send)
        peer = rest // self.send
        k = rest - peer * self.send
        upper = (layer == 2).astype(jnp.int32)
        even = 1 - lax.rem(d, 2)
        x = peer ^ t
        across = self.sub - 1
        aside = jnp.where(layer == 1, 0, jnp.where(upper == even, 2, 1))
        place = jnp.where(x > 0, 2 + aside * across + x, aside)
        row = self.nodes + place * self.send + k
        return jnp.where(other < self.nodes, other, row)

    def exchange(self, arrays):
        inner = lax.axis_size("inner")
        out = []
        for (a, x), value in zip(self.remote, arrays):
            pairs = []
            for d in range(self.dom):
                other = d if a == 0 else (d ^ 1 if a == 1 else ((d + 1) ^ 1) - 1)
                if not 0 <= other < self.dom:
                    continue
                for t in range(self.sub):
                    for i in range(inner):
                        pairs.append(
                            (
                                (d * self.sub + t) * inner + i,
                                (other * self.sub + (t ^ x)) * inner + i,
                            )
                        )
            out.append(lax.ppermute(value, AXES, pairs))
        return out


def swap_axis(value, axis, mask):
    count = lax.axis_size(axis)
    return lax.ppermute(value, axis, [(j, j ^ mask) for j in range(count)])


def call(body, outs, *args, smem=(), scratch=(), flops=0):
    specs = [
        pl.BlockSpec(memory_space=pltpu.SMEM if j in smem else pltpu.VMEM)
        for j in range(len(args))
    ]
    size = sum(math.prod(a.shape) * a.dtype.itemsize for a in (*args, *outs))
    return pl.pallas_call(
        body,
        out_shape=outs,
        in_specs=specs,
        out_specs=[pl.BlockSpec(memory_space=pltpu.VMEM) for _ in outs],
        scratch_shapes=list(scratch),
        compiler_params=pltpu.CompilerParams(vmem_limit_bytes=VMEM_LIMIT),
        cost_estimate=pl.CostEstimate(flops=flops, bytes_accessed=size, transcendentals=0),
    )(*args)


def shape(rows, cols, dtype):
    return jax.ShapeDtypeStruct((rows, cols), dtype)


def border_kernel(send_ref, table_ref, out_ref):
    hot = hot_rows(send_ref[...], table_ref.shape[0])
    out_ref[...] = mm_tn(hot, table_ref[...]).astype(BF)


def live_column(count_ref, b, size):
    row = lax.broadcasted_iota(jnp.int32, (size, 1), 0) + b * size
    return jnp.where(row < count_ref[0], 1.0, 0.0)


def whole_row(ref):
    return jnp.concatenate([ref[b : b + 1, :] for b in range(ref.shape[0])], axis=1)


def per_device(
    node_state,
    edge_state,
    edge_count,
    block_start,
    edge_offset,
    edge_other,
    send_index,
    edge_entry,
    edge_middle,
    edge_outlet,
    edge_gain,
    node_entry,
    node_middle,
    node_outlet,
    node_gain,
    node_cotangent,
    edge_cotangent,
):
    nodes, feat = node_state.shape
    edges = edge_state.shape[0]
    blocks = block_start.shape[0]
    size = edges // blocks
    send = send_index.shape[0]
    lay = Layout(nodes, send)
    remote = len(lay.remote)
    own = nodes + send
    half_near, half_own, half_halo = nodes // 2, own // 2, lay.halo // 2
    f = feat

    sends = send_index.reshape(1, send)
    gain_e = edge_gain.reshape(1, f)
    gain_n = node_gain.reshape(1, f)

    (border,) = call(border_kernel, [shape(send, f, BF)], sends, node_state)
    halo = lay.exchange([border] * remote)

    def edge_local(
        off_ref, oth_ref, start_ref, node_ref, border_ref, edge_ref, entry_ref,
        near_ref, far_ref, pre_ref, place_ref, spot_ref,
    ):
        near_table = fold(node_ref[...])
        own_table = fold(jnp.concatenate([node_ref[...], border_ref[...]], axis=0))
        for b in range(blocks):
            rows = pl.ds(b * size, size)
            spot = off_ref[rows].reshape(1, size) + start_ref[b]
            place = lay.place(oth_ref[rows].reshape(1, size))
            spot_ref[b : b + 1, :] = spot
            place_ref[b : b + 1, :] = place
            near = gather_folded(spot, column(spot), near_table).astype(BF)
            near_ref[rows, :] = near
            far_ref[rows, :] = gather_folded(place, column(place), own_table).astype(BF)
            pre_ref[rows, :] = mm(edge_ref[rows, :], entry_ref[:f, :]) + mm(
                near, entry_ref[f : 2 * f, :]
            )

    near_rows, far_own, pre_own, place, spot = call(
        edge_local,
        [
            shape(edges, f, BF),
            shape(edges, f, BF),
            shape(edges, f, F32),
            shape(blocks, size, jnp.int32),
            shape(blocks, size, jnp.int32),
        ],
        edge_offset, edge_other, block_start, node_state, border, edge_state, edge_entry,
        smem=(2,),
        flops=2 * edges * f * (nodes + own + 2 * f),
    )

    def edge_forward(*refs):
        (place_ref, count_ref, edge_ref, far_own_ref, pre_ref, entry_ref, middle_ref,
         outlet_ref, gain_ref) = refs[:9]
        halo_refs = refs[9 : 9 + remote]
        (message_ref, far_ref, h1_ref, h2_ref, s1_ref, s2_ref, out_ref) = refs[
            9 + remote : 16 + remote
        ]
        slot_refs = refs[16 + remote : 16 + 2 * remote]
        table, pairs = refs[16 + 2 * remote :]
        for j in range(remote):
            table[pl.ds(j * send, send), :] = halo_refs[j][...]
        folded = fold(table[...])
        for b in range(blocks):
            rows = pl.ds(b * size, size)
            slot = place_ref[b : b + 1, :] - own
            slot_col = column(slot)
            far = gather_folded(slot, slot_col, folded)
            far = (far + far_own_ref[rows, :].astype(F32)).astype(BF)
            far_ref[rows, :] = far
            act, slope = silu_pair(pre_ref[rows, :] + mm(far, entry_ref[2 * f :, :]))
            h1 = act.astype(BF)
            h1_ref[rows, :] = h1
            s1_ref[rows, :] = slope
            act, slope = silu_pair(mm(h1, middle_ref[...]))
            h2 = act.astype(BF)
            h2_ref[rows, :] = h2
            s2_ref[rows, :] = slope
            output_pre = mm(h2, outlet_ref[...])
            out_ref[rows, :] = output_pre
            normed, _ = layer_norm(output_pre)
            live = live_column(count_ref, b, size)
            state = edge_ref[rows, :].astype(F32)
            new = (state + live * gain_ref[...] * normed).astype(BF)
            message = new.astype(F32) * live
            message_ref[rows, :] = message.astype(BF)
            pairs[rows, :] = halves(message, slot_col, half_halo)
        hot = folded_hot(whole_row(place_ref) - own, half_halo)
        sums = unfold(mm(hot, pairs[...]).astype(BF))
        for j in range(remote):
            slot_refs[j][...] = sums[j * send : (j + 1) * send]

    edge_outs = call(
        edge_forward,
        [shape(edges, f, BF)] * 4
        + [shape(edges, f, F32)] * 3
        + [shape(send, f, BF)] * remote,
        place, edge_count, edge_state, far_own, pre_own, edge_entry, edge_middle, edge_outlet,
        gain_e, *halo,
        smem=(1,),
        scratch=[pltpu.VMEM((lay.halo, f), BF), pltpu.VMEM((edges, 2 * f), BF)],
        flops=2 * edges * f * (2 * lay.halo + 3 * f),
    )
    message, far_rows, h1, h2, s1, s2, out_pre = edge_outs[:7]
    received = lay.exchange(edge_outs[7:])

    def local_sums(spot_ref, place_ref, send_ref, near_pairs, far_pairs):
        total = unfold(mm(folded_hot(whole_row(spot_ref), half_near), near_pairs[...]))
        sums = unfold(mm(folded_hot(whole_row(place_ref), half_own), far_pairs[...]))
        slot = sums[nodes:].astype(BF)
        return total + sums[:nodes] + mm(hot_rows(send_ref[...], nodes), slot)

    pair_scratch = [pltpu.VMEM((edges, 2 * f), BF), pltpu.VMEM((edges, 2 * f), BF)]

    def message_sums(
        spot_ref, place_ref, send_ref, count_ref, edge_ref, message_ref, new_ref, out_ref,
        near_pairs, far_pairs,
    ):
        for b in range(blocks):
            rows = pl.ds(b * size, size)
            message = message_ref[rows, :].astype(F32)
            live = live_column(count_ref, b, size) > 0.0
            new_ref[rows, :] = jnp.where(live, message, edge_ref[rows, :].astype(F32)).astype(BF)
            near_pairs[rows, :] = halves(message, column(spot_ref[b : b + 1, :]), half_near)
            far_pairs[rows, :] = halves(message, column(place_ref[b : b + 1, :]), half_own)
        out_ref[...] = local_sums(spot_ref, place_ref, send_ref, near_pairs, far_pairs)

    new_edges, message_part = call(
        message_sums,
        [shape(edges, f, BF), shape(nodes, f, F32)],
        spot, place, sends, edge_count, edge_state, message,
        smem=(3,),
        scratch=pair_scratch,
        flops=2 * edges * f * (nodes + own),
    )

    def join_kernel(send_ref, own_ref, *refs):
        hot = hot_rows(send_ref[...], nodes)
        total = own_ref[...]
        for ref in refs[:-1]:
            total += mm(hot, ref[...])
        refs[-1][...] = total.astype(BF)

    def join(part, arrived):
        (out,) = call(
            join_kernel, [shape(nodes, f, BF)], sends, part, *arrived,
            flops=2 * nodes * send * f * remote,
        )
        return out, swap_axis(out, "inner", 1)

    part, part_other = join(message_part, received)

    def node_kernel(
        part_ref, other_ref, node_ref, cot_ref, send_ref, entry_ref, middle_ref, outlet_ref,
        gain_ref, new_ref, pulls_ref, border_ref, direct_ref, totals_ref, h1_ref, h2_ref,
        first_ref, second_ref, og_ref, gain_grad_ref,
    ):
        totals = (part_ref[...].astype(F32) + other_ref[...].astype(F32)).astype(BF)
        totals_ref[...] = totals
        state = node_ref[...]
        act, slope1 = silu_pair(mm(state, entry_ref[:f, :]) + mm(totals, entry_ref[f:, :]))
        h1n = act.astype(BF)
        h1_ref[...] = h1n
        act, slope2 = silu_pair(mm(h1n, middle_ref[...]))
        h2n = act.astype(BF)
        h2_ref[...] = h2n
        normed, inverse = layer_norm(mm(h2n, outlet_ref[...]))
        new_ref[...] = (state.astype(F32) + gain_ref[...] * normed).astype(BF)
        up = cot_ref[...].astype(F32)
        gain_grad_ref[...] = jnp.sum(up * normed, axis=0, keepdims=True)
        og = norm_backward(up * gain_ref[...], normed, inverse).astype(BF)
        og_ref[...] = og
        second = (mm_nt(og, outlet_ref[...]) * slope2).astype(BF)
        second_ref[...] = second
        first = (mm_nt(second, middle_ref[...]) * slope1).astype(BF)
        first_ref[...] = first
        pulls = mm_nt(first, entry_ref[f:, :]).astype(BF)
        pulls_ref[...] = pulls
        border_ref[...] = mm_tn(hot_rows(send_ref[...], nodes), pulls).astype(BF)
        direct_ref[...] = up + mm_nt(first, entry_ref[:f, :])

    node_outs = call(
        node_kernel,
        [
            shape(nodes, f, BF),
            shape(nodes, f, BF),
            shape(send, f, BF),
            shape(nodes, f, F32),
        ]
        + [shape(nodes, f, BF)] * 6
        + [shape(1, f, F32)],
        part, part_other, node_state, node_cotangent, sends, node_entry, node_middle,
        node_outlet, gain_n,
        flops=2 * nodes * f * f * 8,
    )
    own_new, pulls, pull_border, direct = node_outs[:4]
    node_saved, node_gain_grad = node_outs[4:10], node_outs[10]
    pull_halo = lay.exchange([pull_border] * remote)

    def pull_local(
        spot_ref, place_ref, count_ref, pulls_ref, border_ref, cot_ref, node_ref, totals_ref,
        h1_ref, h2_ref, first_ref, second_ref, og_ref, up_ref, weight_ref,
    ):
        near_table = fold(pulls_ref[...])
        own_table = fold(jnp.concatenate([pulls_ref[...], border_ref[...]], axis=0))
        for b in range(blocks):
            rows = pl.ds(b * size, size)
            spot = spot_ref[b : b + 1, :]
            place = place_ref[b : b + 1, :]
            got = gather_folded(spot, column(spot), near_table)
            got += gather_folded(place, column(place), own_table)
            live = live_column(count_ref, b, size)
            up_ref[rows, :] = cot_ref[rows, :].astype(F32) + live * got
        first = first_ref[...]
        weight_ref[:f, :] = (0.5 * mm_tn(node_ref[...], first)).astype(BF)
        weight_ref[f : 2 * f, :] = (0.5 * mm_tn(totals_ref[...], first)).astype(BF)
        weight_ref[2 * f : 3 * f, :] = (0.5 * mm_tn(h1_ref[...], second_ref[...])).astype(BF)
        weight_ref[3 * f :, :] = (0.5 * mm_tn(h2_ref[...], og_ref[...])).astype(BF)

    up_own, node_weights = call(
        pull_local,
        [shape(edges, f, F32), shape(4 * f, f, BF)],
        spot, place, edge_count, pulls, pull_border, edge_cotangent, node_state, *node_saved,
        smem=(2,),
        flops=2 * edges * f * (nodes + own) + 8 * nodes * f * f,
    )

    subs = lax.axis_size("sub")
    doms = lax.axis_size("dom")
    inners = lax.axis_size("inner")
    unit = 16 * inners * subs
    weight_rows = -(-(9 * f + 16) // unit) * unit
    half = weight_rows // 2
    piece = half // subs
    block_total = doms * subs
    edge_scale = 1.0 / math.sqrt(edges * block_total * inners)
    node_scale = 1.0 / math.sqrt(nodes * block_total)

    def edge_backward(*refs):
        (place_ref, count_ref, up_own_ref, out_pre_ref, s1_ref, s2_ref, h1_ref, h2_ref, edge_ref,
         near_ref, far_ref, middle_ref, outlet_ref, gain_ref, node_ref, node_gain_ref) = refs[:16]
        halo_refs = refs[16 : 16 + remote]
        up_ref, first_ref, keep_ref, give_ref, table, second, output, acc = refs[16 + remote :]
        for j in range(remote):
            table[pl.ds(j * send, send), :] = halo_refs[j][...]
        folded = fold(table[...])
        gain_sum = jnp.zeros((1, f), F32)
        for b in range(blocks):
            rows = pl.ds(b * size, size)
            live = live_column(count_ref, b, size)
            slot = place_ref[b : b + 1, :] - own
            up = up_own_ref[rows, :] + live * gather_folded(slot, column(slot), folded)
            up_ref[rows, :] = up
            into = live * up
            normed, inverse = layer_norm(out_pre_ref[rows, :])
            gain_sum += jnp.sum(into * normed, axis=0, keepdims=True)
            og = norm_backward(into * gain_ref[...], normed, inverse).astype(BF)
            output[rows, :] = og
            second_b = (mm_nt(og, outlet_ref[...]) * s2_ref[rows, :]).astype(BF)
            second[rows, :] = second_b
            first_ref[rows, :] = (mm_nt(second_b, middle_ref[...]) * s1_ref[rows, :]).astype(BF)
        first = first_ref[...]
        acc[:f, :] = mm_tn(edge_ref[...], first).astype(BF)
        acc[f : 2 * f, :] = mm_tn(near_ref[...], first).astype(BF)
        acc[2 * f : 3 * f, :] = mm_tn(far_ref[...], first).astype(BF)
        acc[3 * f : 4 * f, :] = mm_tn(h1_ref[...], second[...]).astype(BF)
        acc[4 * f : 5 * f, :] = mm_tn(h2_ref[...], output[...]).astype(BF)
        acc[5 * f : 9 * f, :] = node_ref[...]
        row = lax.broadcasted_iota(jnp.int32, (weight_rows - 9 * f, f), 0)
        gains = jnp.where(row == 0, gain_sum, 0.0)
        gains = jnp.where(row == 1, node_gain_ref[...] * 0.5, gains)
        acc[9 * f :, :] = gains.astype(BF)
        me = lax.axis_index("inner")
        keep_ref[...] = acc[pl.ds(pl.multiple_of(me * half, 16), half), :]
        give_ref[...] = acc[pl.ds(pl.multiple_of((1 - me) * half, 16), half), :]

    up, first_grad, keep, give = call(
        edge_backward,
        [shape(edges, f, F32), shape(edges, f, BF), shape(half, f, BF), shape(half, f, BF)],
        place, edge_count, up_own, out_pre, s1, s2, h1, h2, edge_state, near_rows, far_rows,
        edge_middle, edge_outlet, gain_e, node_weights, node_gain_grad, *pull_halo,
        smem=(1,),
        scratch=[
            pltpu.VMEM((lay.halo, f), BF),
            pltpu.VMEM((edges, f), BF),
            pltpu.VMEM((edges, f), BF),
            pltpu.VMEM((weight_rows, f), BF),
        ],
        flops=2 * edges * f * (lay.halo + 7 * f),
    )
    got = swap_axis(give, "inner", 1)

    def far_slots(place_ref, first_ref, entry_ref, far_ref, *refs):
        slot_refs, pairs = refs[:-1], refs[-1]
        for b in range(blocks):
            rows = pl.ds(b * size, size)
            far = mm_nt(first_ref[rows, :], entry_ref[2 * f :, :])
            far_ref[rows, :] = far.astype(BF)
            pairs[rows, :] = halves(far, column(place_ref[b : b + 1, :] - own), half_halo)
        hot = folded_hot(whole_row(place_ref) - own, half_halo)
        sums = unfold(mm(hot, pairs[...]).astype(BF))
        for j in range(remote):
            slot_refs[j][...] = sums[j * send : (j + 1) * send]

    far_outs = call(
        far_slots,
        [shape(edges, f, BF)] + [shape(send, f, BF)] * remote,
        place, first_grad, edge_entry,
        scratch=[pltpu.VMEM((edges, 2 * f), BF)],
        flops=2 * edges * f * (lay.halo + f),
    )
    far_grad = far_outs[0]
    back_received = lay.exchange(far_outs[1:])

    def grad_sums(
        spot_ref, place_ref, send_ref, up_ref, first_ref, far_ref, entry_ref, adjoint_ref,
        out_ref, near_pairs, far_pairs,
    ):
        for b in range(blocks):
            rows = pl.ds(b * size, size)
            first = first_ref[rows, :]
            adjoint_ref[rows, :] = (up_ref[rows, :] + mm_nt(first, entry_ref[:f, :])).astype(BF)
            near = mm_nt(first, entry_ref[f : 2 * f, :])
            far = far_ref[rows, :].astype(F32)
            near_pairs[rows, :] = halves(near, column(spot_ref[b : b + 1, :]), half_near)
            far_pairs[rows, :] = halves(far, column(place_ref[b : b + 1, :]), half_own)
        out_ref[...] = local_sums(spot_ref, place_ref, send_ref, near_pairs, far_pairs)

    edge_adjoint, grad_part = call(
        grad_sums,
        [shape(edges, f, BF), shape(nodes, f, F32)],
        spot, place, sends, up, first_grad, far_grad, edge_entry,
        scratch=pair_scratch,
        flops=2 * edges * f * (nodes + own + 2 * f),
    )

    def split_kernel(keep_ref, got_ref, *refs):
        out_refs, acc = refs[:-1], refs[-1]
        acc[...] = (keep_ref[...].astype(F32) + got_ref[...].astype(F32)).astype(BF)
        t = lax.axis_index("sub")
        for x in range(subs):
            out_refs[x][...] = acc[pl.ds(pl.multiple_of((t ^ x) * piece, 16), piece), :]

    pieces = call(
        split_kernel,
        [shape(piece, f, BF)] * subs,
        keep, got,
        scratch=[pltpu.VMEM((half, f), BF)],
    )
    arrived = [pieces[0]] + [swap_axis(pieces[x], "sub", x) for x in range(1, subs)]

    def add_all(values):
        values = [v.astype(F32) for v in values]
        while len(values) > 1:
            values = [values[j] + values[j + 1] for j in range(0, len(values), 2)]
        return values[0]

    total = add_all(arrived)
    stride = 1
    while stride < doms:
        step = 4 if stride * 4 <= doms else 2
        sent = total.astype(BF)
        total = add_all(
            [sent] + [swap_axis(sent, "dom", stride * m) for m in range(1, step)]
        )
        stride *= step
    sent = total.astype(BF)
    own_pieces = [sent] + [swap_axis(sent, "sub", x) for x in range(1, subs)]

    def order_kernel(*refs):
        t = lax.axis_index("sub")
        for x in range(subs):
            refs[-1][pl.ds(pl.multiple_of((t ^ x) * piece, 16), piece), :] = refs[x][...]

    (own_half,) = call(order_kernel, [shape(half, f, BF)], *own_pieces)
    other_half = swap_axis(own_half, "inner", 1)

    def finish_kernel(own_ref, other_ref, edge_ref, node_ref, gain_ref, acc):
        me = lax.axis_index("inner")
        acc[pl.ds(pl.multiple_of(me * half, 16), half), :] = own_ref[...]
        acc[pl.ds(pl.multiple_of((1 - me) * half, 16), half), :] = other_ref[...]
        edge_ref[...] = acc[: 5 * f, :].astype(F32) * edge_scale
        node_ref[...] = acc[5 * f : 9 * f, :].astype(F32) * node_scale
        tail = acc[9 * f : 9 * f + 16, :].astype(F32)
        gain_ref[0:1, :] = tail[0:1, :] * edge_scale
        gain_ref[1:2, :] = tail[1:2, :] * node_scale

    edge_gradient, node_gradient, gain_gradient = call(
        finish_kernel,
        [shape(5 * f, f, F32), shape(4 * f, f, F32), shape(2, f, F32)],
        own_half, other_half,
        scratch=[pltpu.VMEM((weight_rows, f), BF)],
    )

    back, back_other = join(grad_part, back_received)
    node_adjoint = (back.astype(F32) + back_other.astype(F32) + direct).astype(BF)
    return (
        own_new,
        new_edges,
        node_adjoint,
        edge_adjoint,
        edge_gradient,
        node_gradient,
        gain_gradient,
    )


def solution(mesh):
    nodes = P(("groups", "dom", "sub"), None)
    edges = P(("groups", "dom", "sub", "inner"), None)
    slots = P(("groups", "dom", "sub", "inner"))
    return jax.shard_map(
        per_device,
        mesh=mesh,
        in_specs=(
            nodes,
            edges,
            slots,
            slots,
            slots,
            slots,
            P(("groups", "dom", "sub")),
            P(),
            P(),
            P(),
            P(),
            P(),
            P(),
            P(),
            P(),
            nodes,
            edges,
        ),
        out_specs=(
            nodes,
            edges,
            nodes,
            edges,
            P("groups", None),
            P("groups", None),
            P("groups", None),
        ),
        check_vma=False,
    )
```

```python
import math

import jax
import jax.numpy as jnp
from jax import lax
from jax.experimental import pallas as pl
from jax.experimental.pallas import tpu as pltpu
from jax.sharding import PartitionSpec as P

EPS = 1e-05
BF = jnp.bfloat16
F32 = jnp.float32
AXES = ("dom", "sub", "inner")
VMEM_LIMIT = 16 * 1024 * 1024


def mm(left, right):
    return jnp.dot(left, right, preferred_element_type=F32)


def mm_tn(left, right):
    return lax.dot_general(left, right, (((0,), (0,)), ((), ())), preferred_element_type=F32)


def mm_nt(left, right):
    return lax.dot_general(left, right, (((1,), (1,)), ((), ())), preferred_element_type=F32)


def silu_pair(pre_act):
    logistic = jax.nn.sigmoid(pre_act)
    act = pre_act * logistic
    return act, logistic + act * (1.0 - logistic)


def layer_norm(output_pre):
    centred = output_pre - jnp.mean(output_pre, axis=-1, keepdims=True)
    inverse = lax.rsqrt(jnp.mean(centred * centred, axis=-1, keepdims=True) + EPS)
    return centred * inverse, inverse


def norm_backward(scaled, normed, inverse):
    return inverse * (
        scaled
        - jnp.mean(scaled, axis=-1, keepdims=True)
        - normed * jnp.mean(scaled * normed, axis=-1, keepdims=True)
    )


def hot_rows(index_row, rows):
    place = lax.broadcasted_iota(jnp.int32, (rows, index_row.shape[1]), 0)
    return jnp.where(place == index_row, 1.0, 0.0).astype(BF)


def folded_hot(index_row, rows):
    return hot_rows(jnp.where(index_row >= rows, index_row - rows, index_row), rows)


def fold(table):
    rows = table.shape[0] // 2
    return jnp.concatenate([table[:rows], table[rows:]], axis=1)


def unfold(table):
    f = table.shape[1] // 2
    return jnp.concatenate([table[:, :f], table[:, f:]], axis=0)


def gather_folded(index_row, index_col, table):
    rows, f = table.shape[0], table.shape[1] // 2
    got = mm_tn(folded_hot(index_row, rows), table)
    return jnp.where(index_col >= rows, got[:, f:], got[:, :f])


def halves(values, index_col, rows):
    upper = index_col >= rows
    zero = jnp.zeros_like(values)
    return jnp.concatenate(
        [jnp.where(upper, zero, values), jnp.where(upper, values, zero)], axis=1
    ).astype(BF)


def column(row):
    wide = jnp.broadcast_to(row, (8, row.shape[1]))
    return jnp.transpose(wide)[:, :1]


class Layout:
    def __init__(self, nodes, send):
        self.nodes, self.send = nodes, send
        self.sub = lax.axis_size("sub")
        self.dom = lax.axis_size("dom")
        self.halo = (3 * self.sub - 1) * send

    def place(self, other):
        d, t, core = (lax.axis_index(name) for name in AXES)
        slot = jnp.maximum(other - self.nodes, 0)
        layer = slot // (self.sub * self.send)
        rest = slot - layer * (self.sub * self.send)
        peer = rest // self.send
        k = rest - peer * self.send
        upper = (layer == 2).astype(jnp.int32)
        even = 1 - lax.rem(d, 2)
        x = peer ^ t
        side = jnp.where(upper == even, 0, 1)
        mine = side == ((core + x) & 1)
        group = jnp.where(mine, 1 + x, 2 * self.sub + x)
        group = jnp.where(layer == 1, jnp.where(x > 0, self.sub + x, 0), group)
        row = self.nodes + group * self.send + k
        return jnp.where(other < self.nodes, other, row)

    def permute(self, value, x, across):
        inner = lax.axis_size("inner")
        pairs = []
        for d in range(self.dom):
            for t in range(self.sub):
                for i in range(inner):
                    other = d if not across else (((d + 1) ^ 1) - 1 if (i + x) & 1 else d ^ 1)
                    if 0 <= other < self.dom:
                        source = (d * self.sub + t) * inner + i
                        pairs.append((source, (other * self.sub + (t ^ x)) * inner + i))
        return lax.ppermute(value, AXES, pairs)

    def fetch(self, border):
        mine = [self.permute(border, x, True) for x in range(self.sub)]
        own = [self.permute(border, x, False) for x in range(1, self.sub)]
        return mine + own + [swap_axis(value, "inner", 1) for value in mine]

    def give_back(self, mine, own, theirs):
        got = swap_axis(theirs, "inner", 1)
        send = self.send

        def add_kernel(mine_ref, got_ref, *outs):
            total = (mine_ref[...] + got_ref[...].astype(F32)).astype(BF)
            for x, out in enumerate(outs):
                out[...] = total[x * send : (x + 1) * send]

        rows = [shape(send, mine.shape[1], BF)] * self.sub
        sums = call(add_kernel, rows, mine, got)
        arrived = [self.permute(value, x, True) for x, value in enumerate(sums)]
        return arrived + [self.permute(value, x + 1, False) for x, value in enumerate(own)]

    def slot_shapes(self, f):
        block = self.sub * self.send
        own = [shape(self.send, f, BF)] * (self.sub - 1)
        return [shape(block, f, F32)] + own + [shape(block, f, BF)]

    def store_slots(self, sums, refs):
        block, send = self.sub * self.send, self.send
        refs[0][...] = sums[:block]
        for j in range(self.sub - 1):
            refs[1 + j][...] = sums[block + j * send : block + (j + 1) * send].astype(BF)
        refs[-1][...] = sums[self.halo - block :].astype(BF)


def swap_axis(value, axis, mask):
    count = lax.axis_size(axis)
    return lax.ppermute(value, axis, [(j, j ^ mask) for j in range(count)])


def call(body, outs, *args, smem=(), hbm=(), scratch=(), flops=0, after=()):
    first, passed = len(args), len(after)
    specs = []
    for j in range(first):
        space = pltpu.SMEM if j in smem else pltpu.HBM if j in hbm else pltpu.VMEM
        specs.append(pl.BlockSpec(memory_space=space))
    anywhere = [pl.BlockSpec(memory_space=pl.ANY)] * passed
    size = sum(math.prod(a.shape) * a.dtype.itemsize for a in (*args, *outs))

    def inner(*refs):
        body(*refs[:first], *refs[first + passed : first + passed + len(outs)],
             *refs[first + 2 * passed + len(outs) :])

    return pl.pallas_call(
        inner,
        out_shape=list(outs) + [jax.ShapeDtypeStruct(a.shape, a.dtype) for a in after],
        in_specs=specs + anywhere,
        out_specs=[pl.BlockSpec(memory_space=pltpu.VMEM) for _ in outs] + anywhere,
        scratch_shapes=list(scratch),
        input_output_aliases={first + j: len(outs) + j for j in range(passed)},
        compiler_params=pltpu.CompilerParams(vmem_limit_bytes=VMEM_LIMIT),
        cost_estimate=pl.CostEstimate(flops=flops, bytes_accessed=size, transcendentals=0),
    )(*args, *after)


def shape(rows, cols, dtype):
    return jax.ShapeDtypeStruct((rows, cols), dtype)


def border_kernel(send_ref, table_ref, out_ref):
    hot = hot_rows(send_ref[...], table_ref.shape[0])
    out_ref[...] = mm_tn(hot, table_ref[...]).astype(BF)


def live_column(count_ref, b, size):
    row = lax.broadcasted_iota(jnp.int32, (size, 1), 0) + b * size
    return jnp.where(row < count_ref[0], 1.0, 0.0)


def whole_row(ref):
    return jnp.concatenate([ref[b : b + 1, :] for b in range(ref.shape[0])], axis=1)


def per_device(
    node_state,
    edge_state,
    edge_count,
    block_start,
    edge_offset,
    edge_other,
    send_index,
    edge_entry,
    edge_middle,
    edge_outlet,
    edge_gain,
    node_entry,
    node_middle,
    node_outlet,
    node_gain,
    node_cotangent,
    edge_cotangent,
):
    nodes, feat = node_state.shape
    edges = edge_state.shape[0]
    blocks = block_start.shape[0]
    size = edges // blocks
    send = send_index.shape[0]
    lay = Layout(nodes, send)
    remote = 3 * lay.sub - 1
    outward = lay.sub + 1
    own = nodes + send
    half_near, half_own, half_halo = nodes // 2, own // 2, lay.halo // 2
    f = feat

    sends = send_index.reshape(1, send)
    gain_e = edge_gain.reshape(1, f)
    gain_n = node_gain.reshape(1, f)

    (border,) = call(border_kernel, [shape(send, f, BF)], sends, node_state)
    halo = lay.fetch(border)

    def edge_local(
        off_ref, oth_ref, start_ref, node_ref, border_ref, near_ref, far_ref, place_ref, spot_ref
    ):
        near_table = fold(node_ref[...])
        own_table = fold(jnp.concatenate([node_ref[...], border_ref[...]], axis=0))
        for b in range(blocks):
            rows = pl.ds(b * size, size)
            spot = off_ref[rows].reshape(1, size) + start_ref[b]
            place = lay.place(oth_ref[rows].reshape(1, size))
            spot_ref[b : b + 1, :] = spot
            place_ref[b : b + 1, :] = place
            near_ref[rows, :] = gather_folded(spot, column(spot), near_table).astype(BF)
            far_ref[rows, :] = gather_folded(place, column(place), own_table).astype(BF)

    near_rows, far_own, place, spot = call(
        edge_local,
        [
            shape(edges, f, BF),
            shape(edges, f, BF),
            shape(blocks, size, jnp.int32),
            shape(blocks, size, jnp.int32),
        ],
        edge_offset, edge_other, block_start, node_state, border,
        smem=(2,),
        flops=2 * edges * f * (nodes + own),
    )

    def edge_forward(*refs):
        (place_ref, count_ref, edge_ref, far_own_ref, near_ref, entry_ref, middle_ref,
         outlet_ref, gain_ref) = refs[:9]
        halo_refs = refs[9 : 9 + remote]
        (message_ref, far_ref, h1_ref, h2_ref, s1_ref, s2_ref, out_ref) = refs[
            9 + remote : 16 + remote
        ]
        slot_refs = refs[16 + remote : 16 + remote + outward]
        table, pairs = refs[16 + remote + outward :]
        for j in range(remote):
            table[pl.ds(j * send, send), :] = halo_refs[j][...]
        folded = fold(table[...])
        for b in range(blocks):
            rows = pl.ds(b * size, size)
            slot = place_ref[b : b + 1, :] - own
            slot_col = column(slot)
            far = gather_folded(slot, slot_col, folded)
            far = (far + far_own_ref[rows, :].astype(F32)).astype(BF)
            far_ref[rows, :] = far
            inputs = jnp.concatenate([edge_ref[rows, :], near_ref[rows, :], far], axis=1)
            act, slope = silu_pair(mm(inputs, entry_ref[...]))
            h1 = act.astype(BF)
            h1_ref[rows, :] = h1
            s1_ref[rows, :] = slope
            act, slope = silu_pair(mm(h1, middle_ref[...]))
            h2 = act.astype(BF)
            h2_ref[rows, :] = h2
            s2_ref[rows, :] = slope
            output_pre = mm(h2, outlet_ref[...])
            out_ref[rows, :] = output_pre
            normed, _ = layer_norm(output_pre)
            live = live_column(count_ref, b, size)
            state = edge_ref[rows, :].astype(F32)
            new = (state + live * gain_ref[...] * normed).astype(BF)
            message = new.astype(F32) * live
            message_ref[rows, :] = message.astype(BF)
            pairs[rows, :] = halves(message, slot_col, half_halo)
        hot = folded_hot(whole_row(place_ref) - own, half_halo)
        lay.store_slots(unfold(mm(hot, pairs[...])), slot_refs)

    edge_outs = call(
        edge_forward,
        [shape(edges, f, BF)] * 4
        + [shape(edges, f, F32)] * 3
        + lay.slot_shapes(f),
        place, edge_count, edge_state, far_own, near_rows, edge_entry, edge_middle, edge_outlet,
        gain_e, *halo,
        smem=(1,),
        scratch=[pltpu.VMEM((lay.halo, f), BF), pltpu.VMEM((edges, 2 * f), BF)],
        flops=2 * edges * f * (2 * lay.halo + 5 * f),
    )
    message, far_rows, h1, h2, s1, s2, out_pre = edge_outs[:7]
    received = lay.give_back(edge_outs[7], edge_outs[8:-1], edge_outs[-1])

    def local_sums(spot_ref, place_ref, send_ref, near_pairs, far_pairs):
        total = unfold(mm(folded_hot(whole_row(spot_ref), half_near), near_pairs[...]))
        sums = unfold(mm(folded_hot(whole_row(place_ref), half_own), far_pairs[...]))
        slot = sums[nodes:].astype(BF)
        return total + sums[:nodes] + mm(hot_rows(send_ref[...], nodes), slot)

    pair_scratch = [pltpu.VMEM((edges, 2 * f), BF), pltpu.VMEM((edges, 2 * f), BF)]

    def message_sums(
        spot_ref, place_ref, send_ref, count_ref, edge_ref, message_ref, new_ref, out_ref,
        near_pairs, far_pairs,
    ):
        for b in range(blocks):
            rows = pl.ds(b * size, size)
            message = message_ref[rows, :].astype(F32)
            live = live_column(count_ref, b, size) > 0.0
            new_ref[rows, :] = jnp.where(live, message, edge_ref[rows, :].astype(F32)).astype(BF)
            near_pairs[rows, :] = halves(message, column(spot_ref[b : b + 1, :]), half_near)
            far_pairs[rows, :] = halves(message, column(place_ref[b : b + 1, :]), half_own)
        out_ref[...] = local_sums(spot_ref, place_ref, send_ref, near_pairs, far_pairs)

    new_edges, message_part = call(
        message_sums,
        [shape(edges, f, BF), shape(nodes, f, F32)],
        spot, place, sends, edge_count, edge_state, message,
        smem=(3,),
        scratch=pair_scratch,
        flops=2 * edges * f * (nodes + own),
    )

    def join_kernel(send_ref, own_ref, *refs):
        hot = hot_rows(send_ref[...], nodes)
        total = own_ref[...]
        for ref in refs[:-1]:
            total += mm(hot, ref[...])
        refs[-1][...] = total.astype(BF)

    def join(part, arrived):
        (out,) = call(
            join_kernel, [shape(nodes, f, BF)], sends, part, *arrived,
            flops=2 * nodes * send * f * len(arrived),
        )
        return out, swap_axis(out, "inner", 1)

    part, part_other = join(message_part, received)

    def node_kernel(
        part_ref, other_ref, node_ref, cot_ref, send_ref, entry_ref, middle_ref, outlet_ref,
        gain_ref, new_ref, pulls_ref, border_ref, direct_ref, totals_ref, h1_ref, h2_ref,
        first_ref, second_ref, og_ref, gain_grad_ref,
    ):
        totals = (part_ref[...].astype(F32) + other_ref[...].astype(F32)).astype(BF)
        totals_ref[...] = totals
        state = node_ref[...]
        act, slope1 = silu_pair(mm(state, entry_ref[:f, :]) + mm(totals, entry_ref[f:, :]))
        h1n = act.astype(BF)
        h1_ref[...] = h1n
        act, slope2 = silu_pair(mm(h1n, middle_ref[...]))
        h2n = act.astype(BF)
        h2_ref[...] = h2n
        normed, inverse = layer_norm(mm(h2n, outlet_ref[...]))
        new_ref[...] = (state.astype(F32) + gain_ref[...] * normed).astype(BF)
        up = cot_ref[...].astype(F32)
        gain_grad_ref[...] = jnp.sum(up * normed, axis=0, keepdims=True)
        og = norm_backward(up * gain_ref[...], normed, inverse).astype(BF)
        og_ref[...] = og
        second = (mm_nt(og, outlet_ref[...]) * slope2).astype(BF)
        second_ref[...] = second
        first = (mm_nt(second, middle_ref[...]) * slope1).astype(BF)
        first_ref[...] = first
        pulls = mm_nt(first, entry_ref[f:, :]).astype(BF)
        pulls_ref[...] = pulls
        border_ref[...] = mm_tn(hot_rows(send_ref[...], nodes), pulls).astype(BF)
        direct_ref[...] = up + mm_nt(first, entry_ref[:f, :])

    node_outs = call(
        node_kernel,
        [
            shape(nodes, f, BF),
            shape(nodes, f, BF),
            shape(send, f, BF),
            shape(nodes, f, F32),
        ]
        + [shape(nodes, f, BF)] * 6
        + [shape(1, f, F32)],
        part, part_other, node_state, node_cotangent, sends, node_entry, node_middle,
        node_outlet, gain_n,
        flops=2 * nodes * f * f * 8,
    )
    own_new, pulls, pull_border, direct = node_outs[:4]
    node_saved, node_gain_grad = node_outs[4:10], node_outs[10]
    pull_halo = lay.fetch(pull_border)

    def pull_local(
        spot_ref, place_ref, count_ref, pulls_ref, border_ref, cot_ref, node_ref, totals_ref,
        h1_ref, h2_ref, first_ref, second_ref, og_ref, up_ref, weight_ref,
    ):
        near_table = fold(pulls_ref[...])
        own_table = fold(jnp.concatenate([pulls_ref[...], border_ref[...]], axis=0))
        for b in range(blocks):
            rows = pl.ds(b * size, size)
            spot = spot_ref[b : b + 1, :]
            place = place_ref[b : b + 1, :]
            got = gather_folded(spot, column(spot), near_table)
            got += gather_folded(place, column(place), own_table)
            live = live_column(count_ref, b, size)
            up_ref[rows, :] = cot_ref[rows, :].astype(F32) + live * got
        first = first_ref[...]
        weight_ref[:f, :] = (0.5 * mm_tn(node_ref[...], first)).astype(BF)
        weight_ref[f : 2 * f, :] = (0.5 * mm_tn(totals_ref[...], first)).astype(BF)
        weight_ref[2 * f : 3 * f, :] = (0.5 * mm_tn(h1_ref[...], second_ref[...])).astype(BF)
        weight_ref[3 * f :, :] = (0.5 * mm_tn(h2_ref[...], og_ref[...])).astype(BF)

    up_own, node_weights = call(
        pull_local,
        [shape(edges, f, F32), shape(4 * f, f, BF)],
        spot, place, edge_count, pulls, pull_border, edge_cotangent, node_state, *node_saved,
        smem=(2,),
        flops=2 * edges * f * (nodes + own) + 8 * nodes * f * f,
    )

    subs = lax.axis_size("sub")
    doms = lax.axis_size("dom")
    inners = lax.axis_size("inner")
    unit = 16 * inners * subs
    weight_rows = -(-(9 * f + 16) // unit) * unit
    half = weight_rows // 2
    piece = half // subs
    block_total = doms * subs
    edge_scale = 1.0 / math.sqrt(edges * block_total * inners)
    node_scale = 1.0 / math.sqrt(nodes * block_total)

    def edge_backward(*refs):
        (place_ref, count_ref, up_own_ref, out_pre_ref, s1_ref, s2_ref, h1_ref, h2_ref, edge_ref,
         near_ref, far_ref, middle_ref, outlet_ref, gain_ref, node_ref, node_gain_ref) = refs[:16]
        halo_refs = refs[16 : 16 + remote]
        up_ref, first_ref, keep_ref, give_ref, table, second, output, acc = refs[16 + remote :]
        for j in range(remote):
            table[pl.ds(j * send, send), :] = halo_refs[j][...]
        folded = fold(table[...])
        gain_sum = jnp.zeros((1, f), F32)
        for b in range(blocks):
            rows = pl.ds(b * size, size)
            live = live_column(count_ref, b, size)
            slot = place_ref[b : b + 1, :] - own
            up = up_own_ref[rows, :] + live * gather_folded(slot, column(slot), folded)
            up_ref[rows, :] = up
            into = live * up
            normed, inverse = layer_norm(out_pre_ref[rows, :])
            gain_sum += jnp.sum(into * normed, axis=0, keepdims=True)
            og = norm_backward(into * gain_ref[...], normed, inverse).astype(BF)
            output[rows, :] = og
            second_b = (mm_nt(og, outlet_ref[...]) * s2_ref[rows, :]).astype(BF)
            second[rows, :] = second_b
            first_ref[rows, :] = (mm_nt(second_b, middle_ref[...]) * s1_ref[rows, :]).astype(BF)
        first = first_ref[...]
        acc[:f, :] = mm_tn(edge_ref[...], first).astype(BF)
        acc[f : 2 * f, :] = mm_tn(near_ref[...], first).astype(BF)
        acc[2 * f : 3 * f, :] = mm_tn(far_ref[...], first).astype(BF)
        acc[3 * f : 4 * f, :] = mm_tn(h1_ref[...], second[...]).astype(BF)
        acc[4 * f : 5 * f, :] = mm_tn(h2_ref[...], output[...]).astype(BF)
        acc[5 * f : 9 * f, :] = node_ref[...]
        row = lax.broadcasted_iota(jnp.int32, (weight_rows - 9 * f, f), 0)
        gains = jnp.where(row == 0, gain_sum, 0.0)
        gains = jnp.where(row == 1, node_gain_ref[...] * 0.5, gains)
        acc[9 * f :, :] = gains.astype(BF)
        me = lax.axis_index("inner")
        keep_ref[...] = acc[pl.ds(pl.multiple_of(me * half, 16), half), :]
        give_ref[...] = acc[pl.ds(pl.multiple_of((1 - me) * half, 16), half), :]

    up, first_grad, keep, give = call(
        edge_backward,
        [shape(edges, f, F32), shape(edges, f, BF), shape(half, f, BF), shape(half, f, BF)],
        place, edge_count, up_own, out_pre, s1, s2, h1, h2, edge_state, near_rows, far_rows,
        edge_middle, edge_outlet, gain_e, node_weights, node_gain_grad, *pull_halo,
        smem=(1,),
        scratch=[
            pltpu.VMEM((lay.halo, f), BF),
            pltpu.VMEM((edges, f), BF),
            pltpu.VMEM((edges, f), BF),
            pltpu.VMEM((weight_rows, f), BF),
        ],
        flops=2 * edges * f * (lay.halo + 7 * f),
    )
    got = swap_axis(give, "inner", 1)

    def far_slots(place_ref, first_ref, entry_ref, far_ref, *refs):
        slot_refs, pairs = refs[:-1], refs[-1]
        for b in range(blocks):
            rows = pl.ds(b * size, size)
            far = mm_nt(first_ref[rows, :], entry_ref[2 * f :, :])
            far_ref[rows, :] = far.astype(BF)
            pairs[rows, :] = halves(far, column(place_ref[b : b + 1, :] - own), half_halo)
        hot = folded_hot(whole_row(place_ref) - own, half_halo)
        lay.store_slots(unfold(mm(hot, pairs[...])), slot_refs)

    far_outs = call(
        far_slots,
        [shape(edges, f, BF)] + lay.slot_shapes(f),
        place, first_grad, edge_entry,
        scratch=[pltpu.VMEM((edges, 2 * f), BF)],
        flops=2 * edges * f * (lay.halo + f),
    )
    far_grad = far_outs[0]
    back = lay.give_back(far_outs[1], far_outs[2:-1], far_outs[-1])

    def split_kernel(keep_ref, got_ref, *refs):
        out_refs, acc = refs[:-1], refs[-1]
        acc[...] = (keep_ref[...].astype(F32) + got_ref[...].astype(F32)).astype(BF)
        t = lax.axis_index("sub")
        for x in range(subs):
            out_refs[x][...] = acc[pl.ds(pl.multiple_of((t ^ x) * piece, 16), piece), :]

    split = call(
        split_kernel,
        [shape(piece, f, BF)] * subs,
        keep, got,
        scratch=[pltpu.VMEM((half, f), BF)],
    )
    arrived = [split[0]] + [swap_axis(split[x], "sub", x) for x in range(1, subs)]

    def add_kernel(*refs):
        values = [ref[...].astype(F32) for ref in refs[:-1]]
        while len(values) > 1:
            values = [values[j] + values[j + 1] for j in range(0, len(values), 2)]
        refs[-1][...] = values[0].astype(BF)

    def add_all(values, after=()):
        out = call(add_kernel, [shape(piece, f, BF)], *values, after=after)
        return out[0], out[1:]

    total, _ = add_all(arrived)
    stride = 1
    while stride < doms:
        partner = swap_axis(total, "dom", stride)
        if stride == 1:
            total, (far_grad,) = add_all([total, partner], [far_grad])
        else:
            total, _ = add_all([total, partner])
        stride *= 2
    own_pieces = [total] + [swap_axis(total, "sub", x) for x in range(1, subs)]

    def grad_sums(
        spot_ref, place_ref, send_ref, up_ref, first_ref, far_ref, entry_ref, adjoint_ref,
        out_ref, near_pairs, far_pairs,
    ):
        for b in range(blocks):
            rows = pl.ds(b * size, size)
            first = first_ref[rows, :]
            adjoint_ref[rows, :] = (up_ref[rows, :] + mm_nt(first, entry_ref[:f, :])).astype(BF)
            near = mm_nt(first, entry_ref[f : 2 * f, :])
            far = far_ref[rows, :].astype(F32)
            near_pairs[rows, :] = halves(near, column(spot_ref[b : b + 1, :]), half_near)
            far_pairs[rows, :] = halves(far, column(place_ref[b : b + 1, :]), half_own)
        out_ref[...] = local_sums(spot_ref, place_ref, send_ref, near_pairs, far_pairs)

    edge_adjoint, grad_part = call(
        grad_sums,
        [shape(edges, f, BF), shape(nodes, f, F32)],
        spot, place, sends, up, first_grad, far_grad, edge_entry,
        scratch=pair_scratch,
        flops=2 * edges * f * (nodes + own + 2 * f),
    )

    def order_kernel(*refs):
        t = lax.axis_index("sub")
        for x in range(subs):
            refs[-1][pl.ds(pl.multiple_of((t ^ x) * piece, 16), piece), :] = refs[x][...]

    (own_half,) = call(order_kernel, [shape(half, f, BF)], *own_pieces)
    other_half = swap_axis(own_half, "inner", 1)

    def finish_kernel(own_ref, other_ref, edge_ref, node_ref, gain_ref, acc):
        me = lax.axis_index("inner")
        acc[pl.ds(pl.multiple_of(me * half, 16), half), :] = own_ref[...]
        acc[pl.ds(pl.multiple_of((1 - me) * half, 16), half), :] = other_ref[...]
        edge_ref[...] = acc[: 5 * f, :].astype(F32) * edge_scale
        node_ref[...] = acc[5 * f : 9 * f, :].astype(F32) * node_scale
        tail = acc[9 * f : 9 * f + 16, :].astype(F32)
        gain_ref[0:1, :] = tail[0:1, :] * edge_scale
        gain_ref[1:2, :] = tail[1:2, :] * node_scale

    edge_gradient, node_gradient, gain_gradient = call(
        finish_kernel,
        [shape(5 * f, f, F32), shape(4 * f, f, F32), shape(2, f, F32)],
        own_half, other_half,
        scratch=[pltpu.VMEM((weight_rows, f), BF)],
    )

    back_part, back_other = join(grad_part, back)
    node_adjoint = (back_part.astype(F32) + back_other.astype(F32) + direct).astype(BF)
    return (
        own_new,
        new_edges,
        node_adjoint,
        edge_adjoint,
        edge_gradient,
        node_gradient,
        gain_gradient,
    )


def solution(mesh):
    nodes = P(("groups", "dom", "sub"), None)
    edges = P(("groups", "dom", "sub", "inner"), None)
    slots = P(("groups", "dom", "sub", "inner"))
    return jax.shard_map(
        per_device,
        mesh=mesh,
        in_specs=(
            nodes,
            edges,
            slots,
            slots,
            slots,
            slots,
            P(("groups", "dom", "sub")),
            P(),
            P(),
            P(),
            P(),
            P(),
            P(),
            P(),
            P(),
            nodes,
            edges,
        ),
        out_specs=(
            nodes,
            edges,
            nodes,
            edges,
            P("groups", None),
            P("groups", None),
            P("groups", None),
        ),
        check_vma=False,
    )
```

```python
import math

import jax
import jax.numpy as jnp
from jax import lax
from jax.experimental import pallas as pl
from jax.experimental.pallas import tpu as pltpu
from jax.sharding import PartitionSpec as P

EPS = 1e-05
BF = jnp.bfloat16
F32 = jnp.float32
AXES = ("dom", "sub", "inner")
BACK_ORDER = (1, 0, 2)
VMEM_LIMIT = 16 * 1024 * 1024


def mm(left, right):
    return jnp.dot(left, right, preferred_element_type=F32)


def mm_tn(left, right):
    return lax.dot_general(left, right, (((0,), (0,)), ((), ())), preferred_element_type=F32)


def mm_nt(left, right):
    return lax.dot_general(left, right, (((1,), (1,)), ((), ())), preferred_element_type=F32)


def silu_pair(pre_act):
    logistic = jax.nn.sigmoid(pre_act)
    act = pre_act * logistic
    return act, logistic + act * (1.0 - logistic)


def layer_norm(output_pre):
    centred = output_pre - jnp.mean(output_pre, axis=-1, keepdims=True)
    inverse = lax.rsqrt(jnp.mean(centred * centred, axis=-1, keepdims=True) + EPS)
    return centred * inverse, inverse


def norm_backward(scaled, normed, inverse):
    return inverse * (
        scaled
        - jnp.mean(scaled, axis=-1, keepdims=True)
        - normed * jnp.mean(scaled * normed, axis=-1, keepdims=True)
    )


def hot_rows(index_row, rows):
    place = lax.broadcasted_iota(jnp.int32, (rows, index_row.shape[1]), 0)
    return jnp.where(place == index_row, 1.0, 0.0).astype(BF)


def folded_hot(index_row, rows):
    return hot_rows(jnp.where(index_row >= rows, index_row - rows, index_row), rows)


def fold(table):
    rows = table.shape[0] // 2
    return jnp.concatenate([table[:rows], table[rows:]], axis=1)


def unfold(table):
    f = table.shape[1] // 2
    return jnp.concatenate([table[:, :f], table[:, f:]], axis=0)


def gather_folded(index_row, index_col, table):
    rows, f = table.shape[0], table.shape[1] // 2
    got = mm_tn(folded_hot(index_row, rows), table)
    return jnp.where(index_col >= rows, got[:, f:], got[:, :f])


def halves(values, index_col, rows):
    upper = index_col >= rows
    zero = jnp.zeros_like(values)
    return jnp.concatenate(
        [jnp.where(upper, zero, values), jnp.where(upper, values, zero)], axis=1
    ).astype(BF)


def column(row):
    wide = jnp.broadcast_to(row, (8, row.shape[1]))
    return jnp.transpose(wide)[:, :1]


class Layout:
    def __init__(self, nodes, send):
        self.nodes, self.send = nodes, send
        self.sub = lax.axis_size("sub")
        self.dom = lax.axis_size("dom")
        self.halo = (3 * self.sub - 1) * send

    def place(self, other):
        d, t, core = (lax.axis_index(name) for name in AXES)
        slot = jnp.maximum(other - self.nodes, 0)
        layer = slot // (self.sub * self.send)
        rest = slot - layer * (self.sub * self.send)
        peer = rest // self.send
        k = rest - peer * self.send
        upper = (layer == 2).astype(jnp.int32)
        even = 1 - lax.rem(d, 2)
        x = peer ^ t
        pair = x >> 1
        near = upper == even
        mine = near == ((x & 1) == core)
        group = jnp.where(near, self.sub // 2 + pair, pair)
        group += jnp.where(mine, 1, 2 * self.sub)
        group = jnp.where(layer == 1, jnp.where(x > 0, self.sub + x, 0), group)
        row = self.nodes + group * self.send + k
        return jnp.where(other < self.nodes, other, row)

    def permute(self, value, layer, x):
        inner = lax.axis_size("inner")
        pairs = []
        for d in range(self.dom):
            other = (d, d ^ 1, ((d + 1) ^ 1) - 1)[layer]
            if not 0 <= other < self.dom:
                continue
            for t in range(self.sub):
                for i in range(inner):
                    source = (d * self.sub + t) * inner + i
                    pairs.append((source, (other * self.sub + (t ^ x[i])) * inner + i))
        return lax.ppermute(value, AXES, pairs)

    def swaps(self):
        pairs = range(0, self.sub, 2)
        steps = [(2, (x + 1, x)) for x in pairs] + [(1, (x, x + 1)) for x in pairs]
        return steps + [(0, (x, x)) for x in range(1, self.sub)]

    def fetch(self, border):
        got = [self.permute(border, layer, x) for layer, x in self.swaps()]
        return got + [swap_axis(value, "inner", 1) for value in got[: self.sub]]

    def give_back(self, mine, own, theirs):
        got = swap_axis(theirs, "inner", 1)
        send = self.send

        def add_kernel(mine_ref, got_ref, *outs):
            total = (mine_ref[...] + got_ref[...].astype(F32)).astype(BF)
            for x, out in enumerate(outs):
                out[...] = total[x * send : (x + 1) * send]

        rows = [shape(send, mine.shape[1], BF)] * self.sub
        sums = call(add_kernel, rows, mine, got)
        arrived = {}
        order = BACK_ORDER if self.sub == 2 else range(len(self.swaps()))
        for j in order:
            value = (*sums, *own)[j]
            arrived[j] = self.permute(value, *self.swaps()[j])
        return list(arrived.values())

    def slot_shapes(self, f):
        block = self.sub * self.send
        own = [shape(self.send, f, BF)] * (self.sub - 1)
        return [shape(block, f, F32)] + own + [shape(block, f, BF)]

    def store_slots(self, sums, refs):
        block, send = self.sub * self.send, self.send
        refs[0][...] = sums[:block]
        for j in range(self.sub - 1):
            refs[1 + j][...] = sums[block + j * send : block + (j + 1) * send].astype(BF)
        refs[-1][...] = sums[self.halo - block :].astype(BF)


def swap_axis(value, axis, mask):
    count = lax.axis_size(axis)
    return lax.ppermute(value, axis, [(j, j ^ mask) for j in range(count)])


def call(body, outs, *args, smem=(), hbm=(), scratch=(), flops=0, after=()):
    first, passed = len(args), len(after)
    specs = []
    for j in range(first):
        space = pltpu.SMEM if j in smem else pltpu.HBM if j in hbm else pltpu.VMEM
        specs.append(pl.BlockSpec(memory_space=space))
    anywhere = [pl.BlockSpec(memory_space=pl.ANY)] * passed
    size = sum(math.prod(a.shape) * a.dtype.itemsize for a in (*args, *outs))

    def inner(*refs):
        body(*refs[:first], *refs[first + passed : first + passed + len(outs)],
             *refs[first + 2 * passed + len(outs) :])

    return pl.pallas_call(
        inner,
        out_shape=list(outs) + [jax.ShapeDtypeStruct(a.shape, a.dtype) for a in after],
        in_specs=specs + anywhere,
        out_specs=[pl.BlockSpec(memory_space=pltpu.VMEM) for _ in outs] + anywhere,
        scratch_shapes=list(scratch),
        input_output_aliases={first + j: len(outs) + j for j in range(passed)},
        compiler_params=pltpu.CompilerParams(vmem_limit_bytes=VMEM_LIMIT),
        cost_estimate=pl.CostEstimate(flops=flops, bytes_accessed=size, transcendentals=0),
    )(*args, *after)


def shape(rows, cols, dtype):
    return jax.ShapeDtypeStruct((rows, cols), dtype)


def border_kernel(send_ref, table_ref, out_ref):
    hot = hot_rows(send_ref[...], table_ref.shape[0])
    out_ref[...] = mm_tn(hot, table_ref[...]).astype(BF)


def live_column(count_ref, b, size):
    row = lax.broadcasted_iota(jnp.int32, (size, 1), 0) + b * size
    return jnp.where(row < count_ref[0], 1.0, 0.0)


def whole_row(ref):
    return jnp.concatenate([ref[b : b + 1, :] for b in range(ref.shape[0])], axis=1)


def per_device(
    node_state,
    edge_state,
    edge_count,
    block_start,
    edge_offset,
    edge_other,
    send_index,
    edge_entry,
    edge_middle,
    edge_outlet,
    edge_gain,
    node_entry,
    node_middle,
    node_outlet,
    node_gain,
    node_cotangent,
    edge_cotangent,
):
    nodes, feat = node_state.shape
    edges = edge_state.shape[0]
    blocks = block_start.shape[0]
    size = edges // blocks
    send = send_index.shape[0]
    lay = Layout(nodes, send)
    remote = 3 * lay.sub - 1
    outward = lay.sub + 1
    own = nodes + send
    half_near, half_own, half_halo = nodes // 2, own // 2, lay.halo // 2
    f = feat

    sends = send_index.reshape(1, send)
    gain_e = edge_gain.reshape(1, f)
    gain_n = node_gain.reshape(1, f)

    (border,) = call(border_kernel, [shape(send, f, BF)], sends, node_state)
    halo = lay.fetch(border)

    def edge_local(
        off_ref, oth_ref, start_ref, node_ref, border_ref, near_ref, far_ref, place_ref, spot_ref
    ):
        near_table = fold(node_ref[...])
        own_table = fold(jnp.concatenate([node_ref[...], border_ref[...]], axis=0))
        for b in range(blocks):
            rows = pl.ds(b * size, size)
            spot = off_ref[rows].reshape(1, size) + start_ref[b]
            place = lay.place(oth_ref[rows].reshape(1, size))
            spot_ref[b : b + 1, :] = spot
            place_ref[b : b + 1, :] = place
            near_ref[rows, :] = gather_folded(spot, column(spot), near_table).astype(BF)
            far_ref[rows, :] = gather_folded(place, column(place), own_table).astype(BF)

    near_rows, far_own, place, spot = call(
        edge_local,
        [
            shape(edges, f, BF),
            shape(edges, f, BF),
            shape(blocks, size, jnp.int32),
            shape(blocks, size, jnp.int32),
        ],
        edge_offset, edge_other, block_start, node_state, border,
        smem=(2,),
        flops=2 * edges * f * (nodes + own),
    )

    def edge_forward(*refs):
        (place_ref, count_ref, edge_ref, far_own_ref, near_ref, entry_ref, middle_ref,
         outlet_ref, gain_ref) = refs[:9]
        halo_refs = refs[9 : 9 + remote]
        (message_ref, far_ref, h1_ref, h2_ref, s1_ref, s2_ref, out_ref) = refs[
            9 + remote : 16 + remote
        ]
        slot_refs = refs[16 + remote : 16 + remote + outward]
        table, pairs = refs[16 + remote + outward :]
        for j in range(remote):
            table[pl.ds(j * send, send), :] = halo_refs[j][...]
        folded = fold(table[...])
        for b in range(blocks):
            rows = pl.ds(b * size, size)
            slot = place_ref[b : b + 1, :] - own
            slot_col = column(slot)
            far = gather_folded(slot, slot_col, folded)
            far = (far + far_own_ref[rows, :].astype(F32)).astype(BF)
            far_ref[rows, :] = far
            inputs = jnp.concatenate([edge_ref[rows, :], near_ref[rows, :], far], axis=1)
            act, slope = silu_pair(mm(inputs, entry_ref[...]))
            h1 = act.astype(BF)
            h1_ref[rows, :] = h1
            s1_ref[rows, :] = slope
            act, slope = silu_pair(mm(h1, middle_ref[...]))
            h2 = act.astype(BF)
            h2_ref[rows, :] = h2
            s2_ref[rows, :] = slope
            output_pre = mm(h2, outlet_ref[...])
            out_ref[rows, :] = output_pre
            normed, _ = layer_norm(output_pre)
            live = live_column(count_ref, b, size)
            state = edge_ref[rows, :].astype(F32)
            new = (state + live * gain_ref[...] * normed).astype(BF)
            message = new.astype(F32) * live
            message_ref[rows, :] = message.astype(BF)
            pairs[rows, :] = halves(message, slot_col, half_halo)
        hot = folded_hot(whole_row(place_ref) - own, half_halo)
        lay.store_slots(unfold(mm(hot, pairs[...])), slot_refs)

    edge_outs = call(
        edge_forward,
        [shape(edges, f, BF)] * 4
        + [shape(edges, f, F32)] * 3
        + lay.slot_shapes(f),
        place, edge_count, edge_state, far_own, near_rows, edge_entry, edge_middle, edge_outlet,
        gain_e, *halo,
        smem=(1,),
        scratch=[pltpu.VMEM((lay.halo, f), BF), pltpu.VMEM((edges, 2 * f), BF)],
        flops=2 * edges * f * (2 * lay.halo + 5 * f),
    )
    message, far_rows, h1, h2, s1, s2, out_pre = edge_outs[:7]
    received = lay.give_back(edge_outs[7], edge_outs[8:-1], edge_outs[-1])

    def local_sums(spot_ref, place_ref, send_ref, near_pairs, far_pairs):
        total = unfold(mm(folded_hot(whole_row(spot_ref), half_near), near_pairs[...]))
        sums = unfold(mm(folded_hot(whole_row(place_ref), half_own), far_pairs[...]))
        slot = sums[nodes:].astype(BF)
        return total + sums[:nodes] + mm(hot_rows(send_ref[...], nodes), slot)

    pair_scratch = [pltpu.VMEM((edges, 2 * f), BF), pltpu.VMEM((edges, 2 * f), BF)]

    def message_sums(
        spot_ref, place_ref, send_ref, count_ref, edge_ref, message_ref, new_ref, out_ref,
        near_pairs, far_pairs,
    ):
        for b in range(blocks):
            rows = pl.ds(b * size, size)
            message = message_ref[rows, :].astype(F32)
            live = live_column(count_ref, b, size) > 0.0
            new_ref[rows, :] = jnp.where(live, message, edge_ref[rows, :].astype(F32)).astype(BF)
            near_pairs[rows, :] = halves(message, column(spot_ref[b : b + 1, :]), half_near)
            far_pairs[rows, :] = halves(message, column(place_ref[b : b + 1, :]), half_own)
        out_ref[...] = local_sums(spot_ref, place_ref, send_ref, near_pairs, far_pairs)

    new_edges, message_part = call(
        message_sums,
        [shape(edges, f, BF), shape(nodes, f, F32)],
        spot, place, sends, edge_count, edge_state, message,
        smem=(3,),
        scratch=pair_scratch,
        flops=2 * edges * f * (nodes + own),
    )

    def join_kernel(send_ref, own_ref, *refs):
        hot = hot_rows(send_ref[...], nodes)
        total = own_ref[...]
        for ref in refs[:-1]:
            total += mm(hot, ref[...])
        refs[-1][...] = total.astype(BF)

    def join(part, arrived):
        (out,) = call(
            join_kernel, [shape(nodes, f, BF)], sends, part, *arrived,
            flops=2 * nodes * send * f * len(arrived),
        )
        return out, swap_axis(out, "inner", 1)

    part, part_other = join(message_part, received)

    def node_kernel(
        part_ref, other_ref, node_ref, cot_ref, send_ref, entry_ref, middle_ref, outlet_ref,
        gain_ref, new_ref, pulls_ref, border_ref, direct_ref, totals_ref, h1_ref, h2_ref,
        first_ref, second_ref, og_ref, gain_grad_ref,
    ):
        totals = (part_ref[...].astype(F32) + other_ref[...].astype(F32)).astype(BF)
        totals_ref[...] = totals
        state = node_ref[...]
        act, slope1 = silu_pair(mm(state, entry_ref[:f, :]) + mm(totals, entry_ref[f:, :]))
        h1n = act.astype(BF)
        h1_ref[...] = h1n
        act, slope2 = silu_pair(mm(h1n, middle_ref[...]))
        h2n = act.astype(BF)
        h2_ref[...] = h2n
        normed, inverse = layer_norm(mm(h2n, outlet_ref[...]))
        new_ref[...] = (state.astype(F32) + gain_ref[...] * normed).astype(BF)
        up = cot_ref[...].astype(F32)
        gain_grad_ref[...] = jnp.sum(up * normed, axis=0, keepdims=True)
        og = norm_backward(up * gain_ref[...], normed, inverse).astype(BF)
        og_ref[...] = og
        second = (mm_nt(og, outlet_ref[...]) * slope2).astype(BF)
        second_ref[...] = second
        first = (mm_nt(second, middle_ref[...]) * slope1).astype(BF)
        first_ref[...] = first
        pulls = mm_nt(first, entry_ref[f:, :]).astype(BF)
        pulls_ref[...] = pulls
        border_ref[...] = mm_tn(hot_rows(send_ref[...], nodes), pulls).astype(BF)
        direct_ref[...] = up + mm_nt(first, entry_ref[:f, :])

    node_outs = call(
        node_kernel,
        [
            shape(nodes, f, BF),
            shape(nodes, f, BF),
            shape(send, f, BF),
            shape(nodes, f, F32),
        ]
        + [shape(nodes, f, BF)] * 6
        + [shape(1, f, F32)],
        part, part_other, node_state, node_cotangent, sends, node_entry, node_middle,
        node_outlet, gain_n,
        flops=2 * nodes * f * f * 8,
    )
    own_new, pulls, pull_border, direct = node_outs[:4]
    node_saved, node_gain_grad = node_outs[4:10], node_outs[10]
    pull_halo = lay.fetch(pull_border)

    def pull_local(
        spot_ref, place_ref, count_ref, pulls_ref, border_ref, cot_ref, node_ref, totals_ref,
        h1_ref, h2_ref, first_ref, second_ref, og_ref, up_ref, weight_ref,
    ):
        near_table = fold(pulls_ref[...])
        own_table = fold(jnp.concatenate([pulls_ref[...], border_ref[...]], axis=0))
        for b in range(blocks):
            rows = pl.ds(b * size, size)
            spot = spot_ref[b : b + 1, :]
            place = place_ref[b : b + 1, :]
            got = gather_folded(spot, column(spot), near_table)
            got += gather_folded(place, column(place), own_table)
            live = live_column(count_ref, b, size)
            up_ref[rows, :] = cot_ref[rows, :].astype(F32) + live * got
        first = first_ref[...]
        weight_ref[:f, :] = (0.5 * mm_tn(node_ref[...], first)).astype(BF)
        weight_ref[f : 2 * f, :] = (0.5 * mm_tn(totals_ref[...], first)).astype(BF)
        weight_ref[2 * f : 3 * f, :] = (0.5 * mm_tn(h1_ref[...], second_ref[...])).astype(BF)
        weight_ref[3 * f :, :] = (0.5 * mm_tn(h2_ref[...], og_ref[...])).astype(BF)

    up_own, node_weights = call(
        pull_local,
        [shape(edges, f, F32), shape(4 * f, f, BF)],
        spot, place, edge_count, pulls, pull_border, edge_cotangent, node_state, *node_saved,
        smem=(2,),
        flops=2 * edges * f * (nodes + own) + 8 * nodes * f * f,
    )

    subs = lax.axis_size("sub")
    doms = lax.axis_size("dom")
    inners = lax.axis_size("inner")
    unit = 16 * inners * subs
    weight_rows = -(-(9 * f + 16) // unit) * unit
    half = weight_rows // 2
    piece = half // subs
    block_total = doms * subs
    edge_scale = 1.0 / math.sqrt(edges * block_total * inners)
    node_scale = 1.0 / math.sqrt(nodes * block_total)

    def edge_backward(*refs):
        (place_ref, count_ref, up_own_ref, out_pre_ref, s1_ref, s2_ref, h1_ref, h2_ref, edge_ref,
         near_ref, far_ref, middle_ref, outlet_ref, gain_ref, node_ref, node_gain_ref) = refs[:16]
        halo_refs = refs[16 : 16 + remote]
        up_ref, first_ref, keep_ref, give_ref, table, second, output, acc = refs[16 + remote :]
        for j in range(remote):
            table[pl.ds(j * send, send), :] = halo_refs[j][...]
        folded = fold(table[...])
        gain_sum = jnp.zeros((1, f), F32)
        for b in range(blocks):
            rows = pl.ds(b * size, size)
            live = live_column(count_ref, b, size)
            slot = place_ref[b : b + 1, :] - own
            up = up_own_ref[rows, :] + live * gather_folded(slot, column(slot), folded)
            up_ref[rows, :] = up
            into = live * up
            normed, inverse = layer_norm(out_pre_ref[rows, :])
            gain_sum += jnp.sum(into * normed, axis=0, keepdims=True)
            og = norm_backward(into * gain_ref[...], normed, inverse).astype(BF)
            output[rows, :] = og
            second_b = (mm_nt(og, outlet_ref[...]) * s2_ref[rows, :]).astype(BF)
            second[rows, :] = second_b
            first_ref[rows, :] = (mm_nt(second_b, middle_ref[...]) * s1_ref[rows, :]).astype(BF)
        first = first_ref[...]
        acc[:f, :] = mm_tn(edge_ref[...], first).astype(BF)
        acc[f : 2 * f, :] = mm_tn(near_ref[...], first).astype(BF)
        acc[2 * f : 3 * f, :] = mm_tn(far_ref[...], first).astype(BF)
        acc[3 * f : 4 * f, :] = mm_tn(h1_ref[...], second[...]).astype(BF)
        acc[4 * f : 5 * f, :] = mm_tn(h2_ref[...], output[...]).astype(BF)
        acc[5 * f : 9 * f, :] = node_ref[...]
        row = lax.broadcasted_iota(jnp.int32, (weight_rows - 9 * f, f), 0)
        gains = jnp.where(row == 0, gain_sum, 0.0)
        gains = jnp.where(row == 1, node_gain_ref[...] * 0.5, gains)
        acc[9 * f :, :] = gains.astype(BF)
        me = lax.axis_index("inner")
        keep_ref[...] = acc[pl.ds(pl.multiple_of(me * half, 16), half), :]
        give_ref[...] = acc[pl.ds(pl.multiple_of((1 - me) * half, 16), half), :]

    up, first_grad, keep, give = call(
        edge_backward,
        [shape(edges, f, F32), shape(edges, f, BF), shape(half, f, BF), shape(half, f, BF)],
        place, edge_count, up_own, out_pre, s1, s2, h1, h2, edge_state, near_rows, far_rows,
        edge_middle, edge_outlet, gain_e, node_weights, node_gain_grad, *pull_halo,
        smem=(1,),
        scratch=[
            pltpu.VMEM((lay.halo, f), BF),
            pltpu.VMEM((edges, f), BF),
            pltpu.VMEM((edges, f), BF),
            pltpu.VMEM((weight_rows, f), BF),
        ],
        flops=2 * edges * f * (lay.halo + 7 * f),
    )
    got = swap_axis(give, "inner", 1)

    def far_slots(place_ref, first_ref, entry_ref, far_ref, *refs):
        slot_refs, pairs = refs[:-1], refs[-1]
        for b in range(blocks):
            rows = pl.ds(b * size, size)
            far = mm_nt(first_ref[rows, :], entry_ref[2 * f :, :])
            far_ref[rows, :] = far.astype(BF)
            pairs[rows, :] = halves(far, column(place_ref[b : b + 1, :] - own), half_halo)
        hot = folded_hot(whole_row(place_ref) - own, half_halo)
        lay.store_slots(unfold(mm(hot, pairs[...])), slot_refs)

    far_outs = call(
        far_slots,
        [shape(edges, f, BF)] + lay.slot_shapes(f),
        place, first_grad, edge_entry,
        scratch=[pltpu.VMEM((edges, 2 * f), BF)],
        flops=2 * edges * f * (lay.halo + f),
    )
    far_grad = far_outs[0]
    back = lay.give_back(far_outs[1], far_outs[2:-1], far_outs[-1])

    def split_kernel(keep_ref, got_ref, *refs):
        out_refs, acc = refs[:-1], refs[-1]
        acc[...] = (keep_ref[...].astype(F32) + got_ref[...].astype(F32)).astype(BF)
        t = lax.axis_index("sub")
        for x in range(subs):
            out_refs[x][...] = acc[pl.ds(pl.multiple_of((t ^ x) * piece, 16), piece), :]

    split = call(
        split_kernel,
        [shape(piece, f, BF)] * subs,
        keep, got,
        scratch=[pltpu.VMEM((half, f), BF)],
    )
    arrived = [split[0]] + [swap_axis(split[x], "sub", x) for x in range(1, subs)]

    def add_kernel(*refs):
        values = [ref[...].astype(F32) for ref in refs[:-1]]
        while len(values) > 1:
            values = [values[j] + values[j + 1] for j in range(0, len(values), 2)]
        refs[-1][...] = values[0].astype(BF)

    def add_all(values, after=()):
        out = call(add_kernel, [shape(piece, f, BF)], *values, after=after)
        return out[0], out[1:]

    total, _ = add_all(arrived)
    stride = 1
    while stride < doms:
        partner = swap_axis(total, "dom", stride)
        if stride == 1:
            total, (far_grad,) = add_all([total, partner], [far_grad])
        else:
            total, _ = add_all([total, partner])
        stride *= 2
    own_pieces = [total] + [swap_axis(total, "sub", x) for x in range(1, subs)]

    def grad_sums(
        spot_ref, place_ref, send_ref, up_ref, first_ref, far_ref, entry_ref, adjoint_ref,
        out_ref, near_pairs, far_pairs,
    ):
        for b in range(blocks):
            rows = pl.ds(b * size, size)
            first = first_ref[rows, :]
            adjoint_ref[rows, :] = (up_ref[rows, :] + mm_nt(first, entry_ref[:f, :])).astype(BF)
            near = mm_nt(first, entry_ref[f : 2 * f, :])
            far = far_ref[rows, :].astype(F32)
            near_pairs[rows, :] = halves(near, column(spot_ref[b : b + 1, :]), half_near)
            far_pairs[rows, :] = halves(far, column(place_ref[b : b + 1, :]), half_own)
        out_ref[...] = local_sums(spot_ref, place_ref, send_ref, near_pairs, far_pairs)

    edge_adjoint, grad_part = call(
        grad_sums,
        [shape(edges, f, BF), shape(nodes, f, F32)],
        spot, place, sends, up, first_grad, far_grad, edge_entry,
        scratch=pair_scratch,
        flops=2 * edges * f * (nodes + own + 2 * f),
    )

    def order_kernel(*refs):
        t = lax.axis_index("sub")
        for x in range(subs):
            refs[-1][pl.ds(pl.multiple_of((t ^ x) * piece, 16), piece), :] = refs[x][...]

    (own_half,) = call(order_kernel, [shape(half, f, BF)], *own_pieces)
    other_half = swap_axis(own_half, "inner", 1)

    def finish_kernel(own_ref, other_ref, edge_ref, node_ref, gain_ref, acc):
        me = lax.axis_index("inner")
        acc[pl.ds(pl.multiple_of(me * half, 16), half), :] = own_ref[...]
        acc[pl.ds(pl.multiple_of((1 - me) * half, 16), half), :] = other_ref[...]
        edge_ref[...] = acc[: 5 * f, :].astype(F32) * edge_scale
        node_ref[...] = acc[5 * f : 9 * f, :].astype(F32) * node_scale
        tail = acc[9 * f : 9 * f + 16, :].astype(F32)
        gain_ref[0:1, :] = tail[0:1, :] * edge_scale
        gain_ref[1:2, :] = tail[1:2, :] * node_scale

    edge_gradient, node_gradient, gain_gradient = call(
        finish_kernel,
        [shape(5 * f, f, F32), shape(4 * f, f, F32), shape(2, f, F32)],
        own_half, other_half,
        scratch=[pltpu.VMEM((weight_rows, f), BF)],
    )

    back_part, back_other = join(grad_part, back)
    node_adjoint = (back_part.astype(F32) + back_other.astype(F32) + direct).astype(BF)
    return (
        own_new,
        new_edges,
        node_adjoint,
        edge_adjoint,
        edge_gradient,
        node_gradient,
        gain_gradient,
    )


def solution(mesh):
    nodes = P(("groups", "dom", "sub"), None)
    edges = P(("groups", "dom", "sub", "inner"), None)
    slots = P(("groups", "dom", "sub", "inner"))
    return jax.shard_map(
        per_device,
        mesh=mesh,
        in_specs=(
            nodes,
            edges,
            slots,
            slots,
            slots,
            slots,
            P(("groups", "dom", "sub")),
            P(),
            P(),
            P(),
            P(),
            P(),
            P(),
            P(),
            P(),
            nodes,
            edges,
        ),
        out_specs=(
            nodes,
            edges,
            nodes,
            edges,
            P("groups", None),
            P("groups", None),
            P("groups", None),
        ),
        check_vma=False,
    )
```

```python
import math

import jax
import jax.numpy as jnp
from jax import lax
from jax.experimental import pallas as pl
from jax.experimental.pallas import tpu as pltpu
from jax.sharding import PartitionSpec as P

EPS = 1e-05
BF = jnp.bfloat16
F32 = jnp.float32
AXES = ("dom", "sub", "inner")
BACK_ORDER = (1, 0, 2)
VMEM_LIMIT = 16 * 1024 * 1024


def mm(left, right):
    return jnp.dot(left, right, preferred_element_type=F32)


def mm_tn(left, right):
    return lax.dot_general(left, right, (((0,), (0,)), ((), ())), preferred_element_type=F32)


def mm_nt(left, right):
    return lax.dot_general(left, right, (((1,), (1,)), ((), ())), preferred_element_type=F32)


def silu_pair(pre_act):
    logistic = jax.nn.sigmoid(pre_act)
    act = pre_act * logistic
    return act, logistic + act * (1.0 - logistic)


def layer_norm(output_pre):
    centred = output_pre - jnp.mean(output_pre, axis=-1, keepdims=True)
    inverse = lax.rsqrt(jnp.mean(centred * centred, axis=-1, keepdims=True) + EPS)
    return centred * inverse, inverse


def norm_backward(scaled, normed, inverse):
    return inverse * (
        scaled
        - jnp.mean(scaled, axis=-1, keepdims=True)
        - normed * jnp.mean(scaled * normed, axis=-1, keepdims=True)
    )


def hot_rows(index_row, rows):
    place = lax.broadcasted_iota(jnp.int32, (rows, index_row.shape[1]), 0)
    return jnp.where(place == index_row, 1.0, 0.0).astype(BF)


def folded_hot(index_row, rows):
    return hot_rows(jnp.where(index_row >= rows, index_row - rows, index_row), rows)


def fold(table):
    rows = table.shape[0] // 2
    return jnp.concatenate([table[:rows], table[rows:]], axis=1)


def unfold(table):
    f = table.shape[1] // 2
    return jnp.concatenate([table[:, :f], table[:, f:]], axis=0)


def gather_folded(index_row, index_col, table):
    rows, f = table.shape[0], table.shape[1] // 2
    got = mm_tn(folded_hot(index_row, rows), table)
    return jnp.where(index_col >= rows, got[:, f:], got[:, :f])


def halves(values, index_col, rows):
    upper = index_col >= rows
    zero = jnp.zeros_like(values)
    return jnp.concatenate(
        [jnp.where(upper, zero, values), jnp.where(upper, values, zero)], axis=1
    ).astype(BF)


def column(row):
    wide = jnp.broadcast_to(row, (8, row.shape[1]))
    return jnp.transpose(wide)[:, :1]


class Layout:
    def __init__(self, nodes, send):
        self.nodes, self.send = nodes, send
        self.sub = lax.axis_size("sub")
        self.dom = lax.axis_size("dom")
        self.halo = (3 * self.sub - 1) * send

    def place(self, other):
        d, t, core = (lax.axis_index(name) for name in AXES)
        slot = jnp.maximum(other - self.nodes, 0)
        layer = slot // (self.sub * self.send)
        rest = slot - layer * (self.sub * self.send)
        peer = rest // self.send
        k = rest - peer * self.send
        upper = (layer == 2).astype(jnp.int32)
        even = 1 - lax.rem(d, 2)
        x = peer ^ t
        pair = x >> 1
        near = upper == even
        mine = near == ((x & 1) == core)
        group = jnp.where(near, self.sub // 2 + pair, pair)
        group += jnp.where(mine, 1, 2 * self.sub)
        group = jnp.where(layer == 1, jnp.where(x > 0, self.sub + x, 0), group)
        row = self.nodes + group * self.send + k
        return jnp.where(other < self.nodes, other, row)

    def permute(self, value, layer, x):
        inner = lax.axis_size("inner")
        pairs = []
        for d in range(self.dom):
            other = (d, d ^ 1, ((d + 1) ^ 1) - 1)[layer]
            if not 0 <= other < self.dom:
                continue
            for t in range(self.sub):
                for i in range(inner):
                    source = (d * self.sub + t) * inner + i
                    pairs.append((source, (other * self.sub + (t ^ x[i])) * inner + i))
        return lax.ppermute(value, AXES, pairs)

    def swaps(self):
        pairs = range(0, self.sub, 2)
        steps = [(2, (x + 1, x)) for x in pairs] + [(1, (x, x + 1)) for x in pairs]
        return steps + [(0, (x, x)) for x in range(1, self.sub)]

    def fetch(self, border):
        return [self.permute(border, layer, x) for layer, x in self.swaps()]

    def fetch_theirs(self, got):
        return [swap_axis(value, "inner", 1) for value in got[: self.sub]]

    def give_back(self, mine, own, theirs):
        got = swap_axis(theirs, "inner", 1)
        send = self.send

        def add_kernel(mine_ref, got_ref, *outs):
            total = (mine_ref[...] + got_ref[...].astype(F32)).astype(BF)
            for x, out in enumerate(outs):
                out[...] = total[x * send : (x + 1) * send]

        rows = [shape(send, mine.shape[1], BF)] * self.sub
        sums = call(add_kernel, rows, mine, got)
        arrived = {}
        order = BACK_ORDER if self.sub == 2 else range(len(self.swaps()))
        for j in order:
            value = (*sums, *own)[j]
            arrived[j] = self.permute(value, *self.swaps()[j])
        return list(arrived.values())

    def slot_shapes(self, f):
        block = self.sub * self.send
        own = [shape(self.send, f, BF)] * (self.sub - 1)
        return [shape(block, f, F32)] + own + [shape(block, f, BF)]

    def store_slots(self, sums, refs):
        block, send = self.sub * self.send, self.send
        refs[0][...] = sums[:block]
        for j in range(self.sub - 1):
            refs[1 + j][...] = sums[block + j * send : block + (j + 1) * send].astype(BF)
        refs[-1][...] = sums[self.halo - block :].astype(BF)


def swap_axis(value, axis, mask):
    count = lax.axis_size(axis)
    return lax.ppermute(value, axis, [(j, j ^ mask) for j in range(count)])


def call(body, outs, *args, smem=(), hbm=(), scratch=(), flops=0, after=()):
    first, passed = len(args), len(after)
    specs = []
    for j in range(first):
        space = pltpu.SMEM if j in smem else pltpu.HBM if j in hbm else pltpu.VMEM
        specs.append(pl.BlockSpec(memory_space=space))
    anywhere = [pl.BlockSpec(memory_space=pl.ANY)] * passed
    size = sum(math.prod(a.shape) * a.dtype.itemsize for a in (*args, *outs))

    def inner(*refs):
        body(*refs[:first], *refs[first + passed : first + passed + len(outs)],
             *refs[first + 2 * passed + len(outs) :])

    return pl.pallas_call(
        inner,
        out_shape=list(outs) + [jax.ShapeDtypeStruct(a.shape, a.dtype) for a in after],
        in_specs=specs + anywhere,
        out_specs=[pl.BlockSpec(memory_space=pltpu.VMEM) for _ in outs] + anywhere,
        scratch_shapes=list(scratch),
        input_output_aliases={first + j: len(outs) + j for j in range(passed)},
        compiler_params=pltpu.CompilerParams(vmem_limit_bytes=VMEM_LIMIT),
        cost_estimate=pl.CostEstimate(flops=flops, bytes_accessed=size, transcendentals=0),
    )(*args, *after)


def shape(rows, cols, dtype):
    return jax.ShapeDtypeStruct((rows, cols), dtype)


def border_kernel(send_ref, table_ref, out_ref):
    hot = hot_rows(send_ref[...], table_ref.shape[0])
    out_ref[...] = mm_tn(hot, table_ref[...]).astype(BF)


def live_column(count_ref, b, size):
    row = lax.broadcasted_iota(jnp.int32, (size, 1), 0) + b * size
    return jnp.where(row < count_ref[0], 1.0, 0.0)


def whole_row(ref):
    return jnp.concatenate([ref[b : b + 1, :] for b in range(ref.shape[0])], axis=1)


def per_device(
    node_state,
    edge_state,
    edge_count,
    block_start,
    edge_offset,
    edge_other,
    send_index,
    edge_entry,
    edge_middle,
    edge_outlet,
    edge_gain,
    node_entry,
    node_middle,
    node_outlet,
    node_gain,
    node_cotangent,
    edge_cotangent,
):
    nodes, feat = node_state.shape
    edges = edge_state.shape[0]
    blocks = block_start.shape[0]
    size = edges // blocks
    send = send_index.shape[0]
    lay = Layout(nodes, send)
    remote = 3 * lay.sub - 1
    outward = lay.sub + 1
    own = nodes + send
    half_near, half_own, half_halo = nodes // 2, own // 2, lay.halo // 2
    f = feat

    sends = send_index.reshape(1, send)
    gain_e = edge_gain.reshape(1, f)
    gain_n = node_gain.reshape(1, f)

    (border,) = call(border_kernel, [shape(send, f, BF)], sends, node_state)
    halo = lay.fetch(border)

    def edge_near(
        off_ref, oth_ref, start_ref, node_ref, gain_ref, near_ref, place_ref, spot_ref,
        gain_out_ref,
    ):
        gain_out_ref[...] = gain_ref[...]
        table = fold(node_ref[...])
        for b in range(blocks):
            rows = pl.ds(b * size, size)
            spot = off_ref[rows].reshape(1, size) + start_ref[b]
            spot_ref[b : b + 1, :] = spot
            place_ref[b : b + 1, :] = lay.place(oth_ref[rows].reshape(1, size))
            near_ref[rows, :] = gather_folded(spot, column(spot), table).astype(BF)

    near_rows, place, spot, gain_e = call(
        edge_near,
        [
            shape(edges, f, BF),
            shape(blocks, size, jnp.int32),
            shape(blocks, size, jnp.int32),
            shape(1, f, F32),
        ],
        edge_offset, edge_other, block_start, node_state, gain_e,
        smem=(2,),
        flops=2 * edges * f * nodes,
    )
    halo += lay.fetch_theirs(halo)

    def edge_far(place_ref, node_ref, border_ref, far_ref):
        table = fold(jnp.concatenate([node_ref[...], border_ref[...]], axis=0))
        for b in range(blocks):
            place = place_ref[b : b + 1, :]
            got = gather_folded(place, column(place), table)
            far_ref[pl.ds(b * size, size), :] = got.astype(BF)

    (far_own,) = call(
        edge_far,
        [shape(edges, f, BF)],
        place, node_state, border,
        flops=20 * edges * f * own,
    )

    def edge_forward(*refs):
        (place_ref, count_ref, edge_ref, far_own_ref, near_ref, entry_ref, middle_ref,
         outlet_ref, gain_ref) = refs[:9]
        halo_refs = refs[9 : 9 + remote]
        (message_ref, far_ref, h1_ref, h2_ref, s1_ref, s2_ref, out_ref) = refs[
            9 + remote : 16 + remote
        ]
        slot_refs = refs[16 + remote : 16 + remote + outward]
        table, pairs = refs[16 + remote + outward :]
        for j in range(remote):
            table[pl.ds(j * send, send), :] = halo_refs[j][...]
        folded = fold(table[...])
        for b in range(blocks):
            rows = pl.ds(b * size, size)
            slot = place_ref[b : b + 1, :] - own
            slot_col = column(slot)
            far = gather_folded(slot, slot_col, folded)
            far = (far + far_own_ref[rows, :].astype(F32)).astype(BF)
            far_ref[rows, :] = far
            inputs = jnp.concatenate([edge_ref[rows, :], near_ref[rows, :], far], axis=1)
            act, slope = silu_pair(mm(inputs, entry_ref[...]))
            h1 = act.astype(BF)
            h1_ref[rows, :] = h1
            s1_ref[rows, :] = slope
            act, slope = silu_pair(mm(h1, middle_ref[...]))
            h2 = act.astype(BF)
            h2_ref[rows, :] = h2
            s2_ref[rows, :] = slope
            output_pre = mm(h2, outlet_ref[...])
            out_ref[rows, :] = output_pre
            normed, _ = layer_norm(output_pre)
            live = live_column(count_ref, b, size)
            state = edge_ref[rows, :].astype(F32)
            new = (state + live * gain_ref[...] * normed).astype(BF)
            message = new.astype(F32) * live
            message_ref[rows, :] = message.astype(BF)
            pairs[rows, :] = halves(message, slot_col, half_halo)
        hot = folded_hot(whole_row(place_ref) - own, half_halo)
        lay.store_slots(unfold(mm(hot, pairs[...])), slot_refs)

    edge_outs = call(
        edge_forward,
        [shape(edges, f, BF)] * 4
        + [shape(edges, f, F32)] * 3
        + lay.slot_shapes(f),
        place, edge_count, edge_state, far_own, near_rows, edge_entry, edge_middle, edge_outlet,
        gain_e, *halo,
        smem=(1,),
        scratch=[pltpu.VMEM((lay.halo, f), BF), pltpu.VMEM((edges, 2 * f), BF)],
        flops=2 * edges * f * (2 * lay.halo + 5 * f),
    )
    message, far_rows, h1, h2, s1, s2, out_pre = edge_outs[:7]
    received = lay.give_back(edge_outs[7], edge_outs[8:-1], edge_outs[-1])

    def local_sums(spot_ref, place_ref, send_ref, near_pairs, far_pairs):
        total = unfold(mm(folded_hot(whole_row(spot_ref), half_near), near_pairs[...]))
        sums = unfold(mm(folded_hot(whole_row(place_ref), half_own), far_pairs[...]))
        slot = sums[nodes:].astype(BF)
        return total + sums[:nodes] + mm(hot_rows(send_ref[...], nodes), slot)

    pair_scratch = [pltpu.VMEM((edges, 2 * f), BF), pltpu.VMEM((edges, 2 * f), BF)]

    def message_sums(
        spot_ref, place_ref, send_ref, count_ref, edge_ref, message_ref, new_ref, out_ref,
        near_pairs, far_pairs,
    ):
        for b in range(blocks):
            rows = pl.ds(b * size, size)
            message = message_ref[rows, :].astype(F32)
            live = live_column(count_ref, b, size) > 0.0
            new_ref[rows, :] = jnp.where(live, message, edge_ref[rows, :].astype(F32)).astype(BF)
            near_pairs[rows, :] = halves(message, column(spot_ref[b : b + 1, :]), half_near)
            far_pairs[rows, :] = halves(message, column(place_ref[b : b + 1, :]), half_own)
        out_ref[...] = local_sums(spot_ref, place_ref, send_ref, near_pairs, far_pairs)

    new_edges, message_part = call(
        message_sums,
        [shape(edges, f, BF), shape(nodes, f, F32)],
        spot, place, sends, edge_count, edge_state, message,
        smem=(3,),
        scratch=pair_scratch,
        flops=2 * edges * f * (nodes + own),
    )

    def join_kernel(send_ref, own_ref, *refs):
        hot = hot_rows(send_ref[...], nodes)
        total = own_ref[...]
        for ref in refs[:-1]:
            total += mm(hot, ref[...])
        refs[-1][...] = total.astype(BF)

    def join(part, arrived):
        (out,) = call(
            join_kernel, [shape(nodes, f, BF)], sends, part, *arrived,
            flops=2 * nodes * send * f * len(arrived),
        )
        return out, swap_axis(out, "inner", 1)

    part, part_other = join(message_part, received)

    def node_kernel(
        part_ref, other_ref, node_ref, cot_ref, send_ref, entry_ref, middle_ref, outlet_ref,
        gain_ref, new_ref, pulls_ref, border_ref, totals_ref, h1_ref, h2_ref, first_ref,
        second_ref, og_ref, gain_grad_ref,
    ):
        totals = (part_ref[...].astype(F32) + other_ref[...].astype(F32)).astype(BF)
        totals_ref[...] = totals
        state = node_ref[...]
        act, slope1 = silu_pair(mm(state, entry_ref[:f, :]) + mm(totals, entry_ref[f:, :]))
        h1n = act.astype(BF)
        h1_ref[...] = h1n
        act, slope2 = silu_pair(mm(h1n, middle_ref[...]))
        h2n = act.astype(BF)
        h2_ref[...] = h2n
        normed, inverse = layer_norm(mm(h2n, outlet_ref[...]))
        new_ref[...] = (state.astype(F32) + gain_ref[...] * normed).astype(BF)
        up = cot_ref[...].astype(F32)
        gain_grad_ref[...] = jnp.sum(up * normed, axis=0, keepdims=True)
        og = norm_backward(up * gain_ref[...], normed, inverse).astype(BF)
        og_ref[...] = og
        second = (mm_nt(og, outlet_ref[...]) * slope2).astype(BF)
        second_ref[...] = second
        first = (mm_nt(second, middle_ref[...]) * slope1).astype(BF)
        first_ref[...] = first
        pulls = mm_nt(first, entry_ref[f:, :]).astype(BF)
        pulls_ref[...] = pulls
        border_ref[...] = mm_tn(hot_rows(send_ref[...], nodes), pulls).astype(BF)

    node_outs = call(
        node_kernel,
        [
            shape(nodes, f, BF),
            shape(nodes, f, BF),
            shape(send, f, BF),
        ]
        + [shape(nodes, f, BF)] * 6
        + [shape(1, f, F32)],
        part, part_other, node_state, node_cotangent, sends, node_entry, node_middle,
        node_outlet, gain_n,
        flops=2 * nodes * f * f * 8,
    )
    new_rows, pulls, pull_border = node_outs[:3]
    node_saved, node_gain_grad = node_outs[3:9], node_outs[9]
    pull_halo = lay.fetch(pull_border)

    def pull_near(
        spot_ref, pulls_ref, node_ref, totals_ref, h1_ref, h2_ref, first_ref, second_ref, og_ref,
        new_ref, got_ref, weight_ref, own_new_ref,
    ):
        table = fold(pulls_ref[...])
        for b in range(blocks):
            spot = spot_ref[b : b + 1, :]
            got = gather_folded(spot, column(spot), table)
            got_ref[pl.ds(b * size, size), :] = got.astype(BF)
        first = first_ref[...]
        weight_ref[:f, :] = (0.5 * mm_tn(node_ref[...], first)).astype(BF)
        weight_ref[f : 2 * f, :] = (0.5 * mm_tn(totals_ref[...], first)).astype(BF)
        weight_ref[2 * f : 3 * f, :] = (0.5 * mm_tn(h1_ref[...], second_ref[...])).astype(BF)
        weight_ref[3 * f :, :] = (0.5 * mm_tn(h2_ref[...], og_ref[...])).astype(BF)
        own_new_ref[...] = new_ref[...]

    got_near, node_weights, own_new = call(
        pull_near,
        [shape(edges, f, BF), shape(4 * f, f, BF), shape(nodes, f, BF)],
        spot, pulls, node_state, *node_saved, new_rows,
        flops=2 * edges * f * nodes + 8 * nodes * f * f,
    )
    pull_halo += lay.fetch_theirs(pull_halo)

    def pull_far(
        place_ref, count_ref, got_ref, pulls_ref, border_ref, cot_ref, first_ref, node_cot_ref,
        entry_ref, up_ref, direct_ref,
    ):
        table = fold(jnp.concatenate([pulls_ref[...], border_ref[...]], axis=0))
        for b in range(blocks):
            rows = pl.ds(b * size, size)
            place = place_ref[b : b + 1, :]
            got = got_ref[rows, :].astype(F32) + gather_folded(place, column(place), table)
            live = live_column(count_ref, b, size)
            up_ref[rows, :] = cot_ref[rows, :].astype(F32) + live * got
        direct_ref[...] = node_cot_ref[...].astype(F32) + mm_nt(first_ref[...], entry_ref[:f, :])

    up_own, direct = call(
        pull_far,
        [shape(edges, f, F32), shape(nodes, f, F32)],
        place, edge_count, got_near, pulls, pull_border, edge_cotangent, node_saved[3],
        node_cotangent, node_entry,
        smem=(1,),
        flops=20 * edges * f * own,
    )

    subs = lax.axis_size("sub")
    doms = lax.axis_size("dom")
    inners = lax.axis_size("inner")
    unit = 16 * inners * subs
    weight_rows = -(-(9 * f + 16) // unit) * unit
    half = weight_rows // 2
    piece = half // subs
    block_total = doms * subs
    edge_scale = 1.0 / math.sqrt(edges * block_total * inners)
    node_scale = 1.0 / math.sqrt(nodes * block_total)

    def edge_backward(*refs):
        (place_ref, count_ref, up_own_ref, out_pre_ref, s1_ref, s2_ref, h1_ref, h2_ref, edge_ref,
         near_ref, far_ref, middle_ref, outlet_ref, gain_ref, node_ref, node_gain_ref) = refs[:16]
        halo_refs = refs[16 : 16 + remote]
        up_ref, first_ref, keep_ref, give_ref, table, second, output, acc = refs[16 + remote :]
        for j in range(remote):
            table[pl.ds(j * send, send), :] = halo_refs[j][...]
        folded = fold(table[...])
        gain_sum = jnp.zeros((1, f), F32)
        for b in range(blocks):
            rows = pl.ds(b * size, size)
            live = live_column(count_ref, b, size)
            slot = place_ref[b : b + 1, :] - own
            up = up_own_ref[rows, :] + live * gather_folded(slot, column(slot), folded)
            up_ref[rows, :] = up
            into = live * up
            normed, inverse = layer_norm(out_pre_ref[rows, :])
            gain_sum += jnp.sum(into * normed, axis=0, keepdims=True)
            og = norm_backward(into * gain_ref[...], normed, inverse).astype(BF)
            output[rows, :] = og
            second_b = (mm_nt(og, outlet_ref[...]) * s2_ref[rows, :]).astype(BF)
            second[rows, :] = second_b
            first_ref[rows, :] = (mm_nt(second_b, middle_ref[...]) * s1_ref[rows, :]).astype(BF)
        first = first_ref[...]
        acc[:f, :] = mm_tn(edge_ref[...], first).astype(BF)
        acc[f : 2 * f, :] = mm_tn(near_ref[...], first).astype(BF)
        acc[2 * f : 3 * f, :] = mm_tn(far_ref[...], first).astype(BF)
        acc[3 * f : 4 * f, :] = mm_tn(h1_ref[...], second[...]).astype(BF)
        acc[4 * f : 5 * f, :] = mm_tn(h2_ref[...], output[...]).astype(BF)
        acc[5 * f : 9 * f, :] = node_ref[...]
        row = lax.broadcasted_iota(jnp.int32, (weight_rows - 9 * f, f), 0)
        gains = jnp.where(row == 0, gain_sum, 0.0)
        gains = jnp.where(row == 1, node_gain_ref[...] * 0.5, gains)
        acc[9 * f :, :] = gains.astype(BF)
        me = lax.axis_index("inner")
        keep_ref[...] = acc[pl.ds(pl.multiple_of(me * half, 16), half), :]
        give_ref[...] = acc[pl.ds(pl.multiple_of((1 - me) * half, 16), half), :]

    up, first_grad, keep, give = call(
        edge_backward,
        [shape(edges, f, F32), shape(edges, f, BF), shape(half, f, BF), shape(half, f, BF)],
        place, edge_count, up_own, out_pre, s1, s2, h1, h2, edge_state, near_rows, far_rows,
        edge_middle, edge_outlet, gain_e, node_weights, node_gain_grad, *pull_halo,
        smem=(1,),
        scratch=[
            pltpu.VMEM((lay.halo, f), BF),
            pltpu.VMEM((edges, f), BF),
            pltpu.VMEM((edges, f), BF),
            pltpu.VMEM((weight_rows, f), BF),
        ],
        flops=2 * edges * f * (lay.halo + 7 * f),
    )
    got = swap_axis(give, "inner", 1)

    def far_slots(place_ref, first_ref, entry_ref, far_ref, *refs):
        slot_refs, pairs = refs[:-1], refs[-1]
        for b in range(blocks):
            rows = pl.ds(b * size, size)
            far = mm_nt(first_ref[rows, :], entry_ref[2 * f :, :])
            far_ref[rows, :] = far.astype(BF)
            pairs[rows, :] = halves(far, column(place_ref[b : b + 1, :] - own), half_halo)
        hot = folded_hot(whole_row(place_ref) - own, half_halo)
        lay.store_slots(unfold(mm(hot, pairs[...])), slot_refs)

    far_outs = call(
        far_slots,
        [shape(edges, f, BF)] + lay.slot_shapes(f),
        place, first_grad, edge_entry,
        scratch=[pltpu.VMEM((edges, 2 * f), BF)],
        flops=2 * edges * f * (lay.halo + f),
    )
    far_grad = far_outs[0]
    back = lay.give_back(far_outs[1], far_outs[2:-1], far_outs[-1])

    def split_kernel(keep_ref, got_ref, *refs):
        out_refs, acc = refs[:-1], refs[-1]
        acc[...] = (keep_ref[...].astype(F32) + got_ref[...].astype(F32)).astype(BF)
        t = lax.axis_index("sub")
        for x in range(subs):
            out_refs[x][...] = acc[pl.ds(pl.multiple_of((t ^ x) * piece, 16), piece), :]

    split = call(
        split_kernel,
        [shape(piece, f, BF)] * subs,
        keep, got,
        scratch=[pltpu.VMEM((half, f), BF)],
    )
    arrived = [split[0]] + [swap_axis(split[x], "sub", x) for x in range(1, subs)]

    def add_kernel(*refs):
        values = [ref[...].astype(F32) for ref in refs[:-1]]
        while len(values) > 1:
            values = [values[j] + values[j + 1] for j in range(0, len(values), 2)]
        refs[-1][...] = values[0].astype(BF)

    def add_all(values, after=()):
        out = call(add_kernel, [shape(piece, f, BF)], *values, after=after)
        return out[0], out[1:]

    total, _ = add_all(arrived)
    stride = 1
    while stride < doms:
        partner = swap_axis(total, "dom", stride)
        if stride == 1:
            total, (far_grad,) = add_all([total, partner], [far_grad])
        else:
            total, _ = add_all([total, partner])
        stride *= 2
    own_pieces = [total] + [swap_axis(total, "sub", x) for x in range(1, subs)]

    def grad_sums(
        spot_ref, place_ref, send_ref, up_ref, first_ref, far_ref, entry_ref, adjoint_ref,
        out_ref, near_pairs, far_pairs,
    ):
        for b in range(blocks):
            rows = pl.ds(b * size, size)
            first = first_ref[rows, :]
            adjoint_ref[rows, :] = (up_ref[rows, :] + mm_nt(first, entry_ref[:f, :])).astype(BF)
            near = mm_nt(first, entry_ref[f : 2 * f, :])
            far = far_ref[rows, :].astype(F32)
            near_pairs[rows, :] = halves(near, column(spot_ref[b : b + 1, :]), half_near)
            far_pairs[rows, :] = halves(far, column(place_ref[b : b + 1, :]), half_own)
        out_ref[...] = local_sums(spot_ref, place_ref, send_ref, near_pairs, far_pairs)

    edge_adjoint, grad_part = call(
        grad_sums,
        [shape(edges, f, BF), shape(nodes, f, F32)],
        spot, place, sends, up, first_grad, far_grad, edge_entry,
        scratch=pair_scratch,
        flops=2 * edges * f * (nodes + own + 2 * f),
    )

    def order_kernel(*refs):
        t = lax.axis_index("sub")
        for x in range(subs):
            refs[-1][pl.ds(pl.multiple_of((t ^ x) * piece, 16), piece), :] = refs[x][...]

    (own_half,) = call(order_kernel, [shape(half, f, BF)], *own_pieces)
    other_half = swap_axis(own_half, "inner", 1)

    def finish_kernel(own_ref, other_ref, edge_ref, node_ref, gain_ref, acc):
        me = lax.axis_index("inner")
        acc[pl.ds(pl.multiple_of(me * half, 16), half), :] = own_ref[...]
        acc[pl.ds(pl.multiple_of((1 - me) * half, 16), half), :] = other_ref[...]
        edge_ref[...] = acc[: 5 * f, :].astype(F32) * edge_scale
        node_ref[...] = acc[5 * f : 9 * f, :].astype(F32) * node_scale
        tail = acc[9 * f : 9 * f + 16, :].astype(F32)
        gain_ref[0:1, :] = tail[0:1, :] * edge_scale
        gain_ref[1:2, :] = tail[1:2, :] * node_scale

    edge_gradient, node_gradient, gain_gradient = call(
        finish_kernel,
        [shape(5 * f, f, F32), shape(4 * f, f, F32), shape(2, f, F32)],
        own_half, other_half,
        scratch=[pltpu.VMEM((weight_rows, f), BF)],
    )

    back_part, back_other = join(grad_part, back)
    node_adjoint = (back_part.astype(F32) + back_other.astype(F32) + direct).astype(BF)
    return (
        own_new,
        new_edges,
        node_adjoint,
        edge_adjoint,
        edge_gradient,
        node_gradient,
        gain_gradient,
    )


def solution(mesh):
    nodes = P(("groups", "dom", "sub"), None)
    edges = P(("groups", "dom", "sub", "inner"), None)
    slots = P(("groups", "dom", "sub", "inner"))
    return jax.shard_map(
        per_device,
        mesh=mesh,
        in_specs=(
            nodes,
            edges,
            slots,
            slots,
            slots,
            slots,
            P(("groups", "dom", "sub")),
            P(),
            P(),
            P(),
            P(),
            P(),
            P(),
            P(),
            P(),
            nodes,
            edges,
        ),
        out_specs=(
            nodes,
            edges,
            nodes,
            edges,
            P("groups", None),
            P("groups", None),
            P("groups", None),
        ),
        check_vma=False,
    )
```

```python
import math

import jax
import jax.numpy as jnp
from jax import lax
from jax.experimental import pallas as pl
from jax.experimental.pallas import tpu as pltpu
from jax.sharding import PartitionSpec as P

EPS = 1e-05
BF = jnp.bfloat16
F32 = jnp.float32
AXES = ("dom", "sub", "inner")
BACK_ORDER = (1, 0, 2)
VMEM_LIMIT = 16 * 1024 * 1024


def mm(left, right):
    return jnp.dot(left, right, preferred_element_type=F32)


def mm_tn(left, right):
    return lax.dot_general(left, right, (((0,), (0,)), ((), ())), preferred_element_type=F32)


def mm_nt(left, right):
    return lax.dot_general(left, right, (((1,), (1,)), ((), ())), preferred_element_type=F32)


def silu_pair(pre_act):
    logistic = jax.nn.sigmoid(pre_act)
    act = pre_act * logistic
    return act, logistic + act * (1.0 - logistic)


def layer_norm(output_pre):
    centred = output_pre - jnp.mean(output_pre, axis=-1, keepdims=True)
    inverse = lax.rsqrt(jnp.mean(centred * centred, axis=-1, keepdims=True) + EPS)
    return centred * inverse, inverse


def norm_backward(scaled, normed, inverse):
    return inverse * (
        scaled
        - jnp.mean(scaled, axis=-1, keepdims=True)
        - normed * jnp.mean(scaled * normed, axis=-1, keepdims=True)
    )


def hot_rows(index_row, rows):
    place = lax.broadcasted_iota(jnp.int32, (rows, index_row.shape[1]), 0)
    return jnp.where(place == index_row, 1.0, 0.0).astype(BF)


def folded_hot(index_row, rows):
    return hot_rows(jnp.where(index_row >= rows, index_row - rows, index_row), rows)


def fold(table):
    rows = table.shape[0] // 2
    return jnp.concatenate([table[:rows], table[rows:]], axis=1)


def unfold(table):
    f = table.shape[1] // 2
    return jnp.concatenate([table[:, :f], table[:, f:]], axis=0)


def gather_folded(index_row, index_col, table):
    rows, f = table.shape[0], table.shape[1] // 2
    got = mm_tn(folded_hot(index_row, rows), table)
    return jnp.where(index_col >= rows, got[:, f:], got[:, :f])


def halves(values, index_col, rows):
    upper = index_col >= rows
    zero = jnp.zeros_like(values)
    return jnp.concatenate(
        [jnp.where(upper, zero, values), jnp.where(upper, values, zero)], axis=1
    ).astype(BF)


def column(row):
    wide = jnp.broadcast_to(row, (8, row.shape[1]))
    return jnp.transpose(wide)[:, :1]


class Layout:
    def __init__(self, nodes, send):
        self.nodes, self.send = nodes, send
        self.sub = lax.axis_size("sub")
        self.dom = lax.axis_size("dom")
        self.halo = (3 * self.sub - 1) * send

    def place(self, other):
        d, t, core = (lax.axis_index(name) for name in AXES)
        slot = jnp.maximum(other - self.nodes, 0)
        layer = slot // (self.sub * self.send)
        rest = slot - layer * (self.sub * self.send)
        peer = rest // self.send
        k = rest - peer * self.send
        upper = (layer == 2).astype(jnp.int32)
        even = 1 - lax.rem(d, 2)
        x = peer ^ t
        pair = x >> 1
        near = upper == even
        mine = near == ((x & 1) == core)
        group = jnp.where(near, self.sub // 2 + pair, pair)
        group += jnp.where(mine, 1, 2 * self.sub)
        group = jnp.where(layer == 1, jnp.where(x > 0, self.sub + x, 0), group)
        row = self.nodes + group * self.send + k
        return jnp.where(other < self.nodes, other, row)

    def permute(self, value, layer, x):
        inner = lax.axis_size("inner")
        pairs = []
        for d in range(self.dom):
            other = (d, d ^ 1, ((d + 1) ^ 1) - 1)[layer]
            if not 0 <= other < self.dom:
                continue
            for t in range(self.sub):
                for i in range(inner):
                    source = (d * self.sub + t) * inner + i
                    pairs.append((source, (other * self.sub + (t ^ x[i])) * inner + i))
        return lax.ppermute(value, AXES, pairs)

    def swaps(self):
        pairs = range(0, self.sub, 2)
        steps = [(2, (x + 1, x)) for x in pairs] + [(1, (x, x + 1)) for x in pairs]
        return steps + [(0, (x, x)) for x in range(1, self.sub)]

    def fetch(self, border):
        return [self.permute(border, layer, x) for layer, x in self.swaps()]

    def fetch_theirs(self, got):
        return [swap_axis(value, "inner", 1) for value in got[: self.sub]]

    def outgoing(self, mine, own, theirs):
        got = swap_axis(theirs, "inner", 1)
        send = self.send

        def add_kernel(mine_ref, got_ref, *outs):
            total = (mine_ref[...] + got_ref[...].astype(F32)).astype(BF)
            for x, out in enumerate(outs):
                out[...] = total[x * send : (x + 1) * send]

        rows = [shape(send, mine.shape[1], BF)] * self.sub
        return list(call(add_kernel, rows, mine, got)) + list(own)

    def give(self, values, which):
        swaps = self.swaps()
        return [self.permute(values[j], *swaps[j]) for j in which]

    def slot_shapes(self, f):
        block = self.sub * self.send
        own = [shape(self.send, f, BF)] * (self.sub - 1)
        return [shape(block, f, F32)] + own + [shape(block, f, BF)]

    def store_slots(self, sums, refs):
        block, send = self.sub * self.send, self.send
        refs[0][...] = sums[:block]
        for j in range(self.sub - 1):
            refs[1 + j][...] = sums[block + j * send : block + (j + 1) * send].astype(BF)
        refs[-1][...] = sums[self.halo - block :].astype(BF)


def swap_axis(value, axis, mask):
    count = lax.axis_size(axis)
    return lax.ppermute(value, axis, [(j, j ^ mask) for j in range(count)])


def call(body, outs, *args, smem=(), hbm=(), scratch=(), flops=0, after=()):
    first, passed = len(args), len(after)
    specs = []
    for j in range(first):
        space = pltpu.SMEM if j in smem else pltpu.HBM if j in hbm else pltpu.VMEM
        specs.append(pl.BlockSpec(memory_space=space))
    anywhere = [pl.BlockSpec(memory_space=pl.ANY)] * passed
    size = sum(math.prod(a.shape) * a.dtype.itemsize for a in (*args, *outs))

    def inner(*refs):
        body(*refs[:first], *refs[first + passed : first + passed + len(outs)],
             *refs[first + 2 * passed + len(outs) :])

    return pl.pallas_call(
        inner,
        out_shape=list(outs) + [jax.ShapeDtypeStruct(a.shape, a.dtype) for a in after],
        in_specs=specs + anywhere,
        out_specs=[pl.BlockSpec(memory_space=pltpu.VMEM) for _ in outs] + anywhere,
        scratch_shapes=list(scratch),
        input_output_aliases={first + j: len(outs) + j for j in range(passed)},
        compiler_params=pltpu.CompilerParams(vmem_limit_bytes=VMEM_LIMIT),
        cost_estimate=pl.CostEstimate(flops=flops, bytes_accessed=size, transcendentals=0),
    )(*args, *after)


def shape(rows, cols, dtype):
    return jax.ShapeDtypeStruct((rows, cols), dtype)


def border_kernel(send_ref, table_ref, out_ref):
    hot = hot_rows(send_ref[...], table_ref.shape[0])
    out_ref[...] = mm_tn(hot, table_ref[...]).astype(BF)


def live_column(count_ref, b, size):
    row = lax.broadcasted_iota(jnp.int32, (size, 1), 0) + b * size
    return jnp.where(row < count_ref[0], 1.0, 0.0)


def whole_row(ref):
    return jnp.concatenate([ref[b : b + 1, :] for b in range(ref.shape[0])], axis=1)


def per_device(
    node_state,
    edge_state,
    edge_count,
    block_start,
    edge_offset,
    edge_other,
    send_index,
    edge_entry,
    edge_middle,
    edge_outlet,
    edge_gain,
    node_entry,
    node_middle,
    node_outlet,
    node_gain,
    node_cotangent,
    edge_cotangent,
):
    nodes, feat = node_state.shape
    edges = edge_state.shape[0]
    blocks = block_start.shape[0]
    size = edges // blocks
    send = send_index.shape[0]
    lay = Layout(nodes, send)
    remote = 3 * lay.sub - 1
    outward = lay.sub + 1
    own = nodes + send
    half_near, half_own, half_halo = nodes // 2, own // 2, lay.halo // 2
    f = feat

    sends = send_index.reshape(1, send)
    gain_e = edge_gain.reshape(1, f)
    gain_n = node_gain.reshape(1, f)

    (border,) = call(border_kernel, [shape(send, f, BF)], sends, node_state)
    halo = lay.fetch(border)

    def edge_near(
        off_ref, oth_ref, start_ref, node_ref, gain_ref, near_ref, place_ref, spot_ref,
        gain_out_ref,
    ):
        gain_out_ref[...] = gain_ref[...]
        table = fold(node_ref[...])
        for b in range(blocks):
            rows = pl.ds(b * size, size)
            spot = off_ref[rows].reshape(1, size) + start_ref[b]
            spot_ref[b : b + 1, :] = spot
            place_ref[b : b + 1, :] = lay.place(oth_ref[rows].reshape(1, size))
            near_ref[rows, :] = gather_folded(spot, column(spot), table).astype(BF)

    near_rows, place, spot, gain_e = call(
        edge_near,
        [
            shape(edges, f, BF),
            shape(blocks, size, jnp.int32),
            shape(blocks, size, jnp.int32),
            shape(1, f, F32),
        ],
        edge_offset, edge_other, block_start, node_state, gain_e,
        smem=(2,),
        flops=2 * edges * f * nodes,
    )
    halo += lay.fetch_theirs(halo)

    def edge_far(place_ref, node_ref, border_ref, far_ref):
        table = fold(jnp.concatenate([node_ref[...], border_ref[...]], axis=0))
        for b in range(blocks):
            place = place_ref[b : b + 1, :]
            got = gather_folded(place, column(place), table)
            far_ref[pl.ds(b * size, size), :] = got.astype(BF)

    (far_own,) = call(
        edge_far,
        [shape(edges, f, BF)],
        place, node_state, border,
        flops=20 * edges * f * own,
    )

    def edge_forward(*refs):
        (place_ref, count_ref, edge_ref, far_own_ref, near_ref, entry_ref, middle_ref,
         outlet_ref, gain_ref) = refs[:9]
        halo_refs = refs[9 : 9 + remote]
        (message_ref, far_ref, h1_ref, h2_ref, s1_ref, s2_ref, out_ref) = refs[
            9 + remote : 16 + remote
        ]
        slot_refs = refs[16 + remote : 16 + remote + outward]
        table, pairs = refs[16 + remote + outward :]
        for j in range(remote):
            table[pl.ds(j * send, send), :] = halo_refs[j][...]
        folded = fold(table[...])
        slots = [place_ref[b : b + 1, :] - own for b in range(blocks)]
        cols = [column(slot) for slot in slots]
        parts = [pl.ds(b * size, size) for b in range(blocks)]
        for slot, col, rows in zip(slots, cols, parts):
            far = gather_folded(slot, col, folded)
            far_ref[rows, :] = (far + far_own_ref[rows, :].astype(F32)).astype(BF)
        for rows in parts:
            inputs = [edge_ref[rows, :], near_ref[rows, :], far_ref[rows, :]]
            act, slope = silu_pair(mm(jnp.concatenate(inputs, axis=1), entry_ref[...]))
            h1_ref[rows, :] = act.astype(BF)
            s1_ref[rows, :] = slope
        for rows in parts:
            act, slope = silu_pair(mm(h1_ref[rows, :], middle_ref[...]))
            h2_ref[rows, :] = act.astype(BF)
            s2_ref[rows, :] = slope
        for rows in parts:
            out_ref[rows, :] = mm(h2_ref[rows, :], outlet_ref[...])
        for b, (col, rows) in enumerate(zip(cols, parts)):
            normed, _ = layer_norm(out_ref[rows, :])
            live = live_column(count_ref, b, size)
            state = edge_ref[rows, :].astype(F32)
            new = (state + live * gain_ref[...] * normed).astype(BF)
            message = new.astype(F32) * live
            message_ref[rows, :] = message.astype(BF)
            pairs[rows, :] = halves(message, col, half_halo)
        hot = folded_hot(whole_row(place_ref) - own, half_halo)
        lay.store_slots(unfold(mm(hot, pairs[...])), slot_refs)

    edge_outs = call(
        edge_forward,
        [shape(edges, f, BF)] * 4
        + [shape(edges, f, F32)] * 3
        + lay.slot_shapes(f),
        place, edge_count, edge_state, far_own, near_rows, edge_entry, edge_middle, edge_outlet,
        gain_e, *halo,
        smem=(1,),
        scratch=[pltpu.VMEM((lay.halo, f), BF), pltpu.VMEM((edges, 2 * f), BF)],
        flops=2 * edges * f * (2 * lay.halo + 5 * f),
    )
    message, far_rows, h1, h2, s1, s2, out_pre = edge_outs[:7]
    outgoing = lay.outgoing(edge_outs[7], edge_outs[8:-1], edge_outs[-1])
    near_first = lay.sub // 2
    other_swaps = [j for j in range(len(outgoing)) if j != near_first]
    received = lay.give(outgoing, [near_first] + other_swaps)

    def local_sums(spot_ref, place_ref, send_ref, near_pairs, far_pairs):
        total = unfold(mm(folded_hot(whole_row(spot_ref), half_near), near_pairs[...]))
        sums = unfold(mm(folded_hot(whole_row(place_ref), half_own), far_pairs[...]))
        slot = sums[nodes:].astype(BF)
        return total + sums[:nodes] + mm(hot_rows(send_ref[...], nodes), slot)

    pair_scratch = [pltpu.VMEM((edges, 2 * f), BF), pltpu.VMEM((edges, 2 * f), BF)]

    def message_sums(
        spot_ref, place_ref, send_ref, count_ref, edge_ref, message_ref, new_ref, out_ref,
        near_pairs, far_pairs,
    ):
        for b in range(blocks):
            rows = pl.ds(b * size, size)
            message = message_ref[rows, :].astype(F32)
            live = live_column(count_ref, b, size) > 0.0
            new_ref[rows, :] = jnp.where(live, message, edge_ref[rows, :].astype(F32)).astype(BF)
            near_pairs[rows, :] = halves(message, column(spot_ref[b : b + 1, :]), half_near)
            far_pairs[rows, :] = halves(message, column(place_ref[b : b + 1, :]), half_own)
        out_ref[...] = local_sums(spot_ref, place_ref, send_ref, near_pairs, far_pairs)

    new_edges, message_part = call(
        message_sums,
        [shape(edges, f, BF), shape(nodes, f, F32)],
        spot, place, sends, edge_count, edge_state, message,
        smem=(3,),
        scratch=pair_scratch,
        flops=2 * edges * f * (nodes + own),
    )

    def join_kernel(send_ref, own_ref, *refs):
        hot = hot_rows(send_ref[...], nodes)
        total = own_ref[...]
        for ref in refs[:-1]:
            total += mm(hot, ref[:send, :])
        refs[-1][...] = total.astype(BF)

    def join(part, arrived):
        (out,) = call(
            join_kernel, [shape(nodes, f, BF)], sends, part, *arrived,
            flops=2 * nodes * send * f * len(arrived),
        )
        return out, swap_axis(out, "inner", 1)

    part, part_other = join(message_part, received)

    def node_kernel(
        part_ref, other_ref, node_ref, cot_ref, send_ref, entry_ref, middle_ref, outlet_ref,
        gain_ref, new_ref, pulls_ref, border_ref, totals_ref, h1_ref, h2_ref, first_ref,
        second_ref, og_ref, gain_grad_ref, slope1, slope2,
    ):
        half_rows = nodes // 2
        parts = [pl.ds(j * half_rows, half_rows) for j in range(2)]
        for rows in parts:
            totals = part_ref[rows, :].astype(F32) + other_ref[rows, :].astype(F32)
            totals_ref[rows, :] = totals.astype(BF)
        for rows in parts:
            inputs = jnp.concatenate([node_ref[rows, :], totals_ref[rows, :]], axis=1)
            act, slope = silu_pair(mm(inputs, entry_ref[...]))
            h1_ref[rows, :] = act.astype(BF)
            slope1[rows, :] = slope
        for rows in parts:
            act, slope = silu_pair(mm(h1_ref[rows, :], middle_ref[...]))
            h2_ref[rows, :] = act.astype(BF)
            slope2[rows, :] = slope
        gain_sum = jnp.zeros((1, f), F32)
        for rows in parts:
            normed, inverse = layer_norm(mm(h2_ref[rows, :], outlet_ref[...]))
            new = node_ref[rows, :].astype(F32) + gain_ref[...] * normed
            new_ref[rows, :] = new.astype(BF)
            up = cot_ref[rows, :].astype(F32)
            gain_sum += jnp.sum(up * normed, axis=0, keepdims=True)
            og_ref[rows, :] = norm_backward(up * gain_ref[...], normed, inverse).astype(BF)
        gain_grad_ref[...] = gain_sum
        for rows in parts:
            grad = mm_nt(og_ref[rows, :], outlet_ref[...])
            second_ref[rows, :] = (grad * slope2[rows, :]).astype(BF)
        for rows in parts:
            grad = mm_nt(second_ref[rows, :], middle_ref[...])
            first_ref[rows, :] = (grad * slope1[rows, :]).astype(BF)
        for rows in parts:
            pulls_ref[rows, :] = mm_nt(first_ref[rows, :], entry_ref[f:, :]).astype(BF)
        border_ref[...] = mm_tn(hot_rows(send_ref[...], nodes), pulls_ref[...]).astype(BF)

    node_outs = call(
        node_kernel,
        [
            shape(nodes, f, BF),
            shape(nodes, f, BF),
            shape(send, f, BF),
        ]
        + [shape(nodes, f, BF)] * 6
        + [shape(1, f, F32)],
        part, part_other, node_state, node_cotangent, sends, node_entry, node_middle,
        node_outlet, gain_n,
        scratch=[pltpu.VMEM((nodes, f), F32), pltpu.VMEM((nodes, f), F32)],
        flops=2 * nodes * f * f * 8,
    )
    new_rows, pulls, pull_border = node_outs[:3]
    node_saved, node_gain_grad = node_outs[3:9], node_outs[9]
    pull_halo = lay.fetch(pull_border)

    def pull_near(
        spot_ref, pulls_ref, node_ref, totals_ref, h1_ref, h2_ref, first_ref, second_ref, og_ref,
        new_ref, got_ref, weight_ref, own_new_ref,
    ):
        table = fold(pulls_ref[...])
        for b in range(blocks):
            spot = spot_ref[b : b + 1, :]
            got = gather_folded(spot, column(spot), table)
            got_ref[pl.ds(b * size, size), :] = got.astype(BF)
        first = first_ref[...]
        weight_ref[:f, :] = (0.5 * mm_tn(node_ref[...], first)).astype(BF)
        weight_ref[f : 2 * f, :] = (0.5 * mm_tn(totals_ref[...], first)).astype(BF)
        weight_ref[2 * f : 3 * f, :] = (0.5 * mm_tn(h1_ref[...], second_ref[...])).astype(BF)
        weight_ref[3 * f :, :] = (0.5 * mm_tn(h2_ref[...], og_ref[...])).astype(BF)
        own_new_ref[...] = new_ref[...]

    got_near, node_weights, own_new = call(
        pull_near,
        [shape(edges, f, BF), shape(4 * f, f, BF), shape(nodes, f, BF)],
        spot, pulls, node_state, *node_saved, new_rows,
        flops=2 * edges * f * nodes + 8 * nodes * f * f,
    )
    pull_halo += lay.fetch_theirs(pull_halo)

    def pull_far(
        place_ref, count_ref, got_ref, pulls_ref, border_ref, cot_ref, first_ref, node_cot_ref,
        entry_ref, up_ref, direct_ref,
    ):
        table = fold(jnp.concatenate([pulls_ref[...], border_ref[...]], axis=0))
        for b in range(blocks):
            rows = pl.ds(b * size, size)
            place = place_ref[b : b + 1, :]
            got = got_ref[rows, :].astype(F32) + gather_folded(place, column(place), table)
            live = live_column(count_ref, b, size)
            up_ref[rows, :] = cot_ref[rows, :].astype(F32) + live * got
        direct_ref[...] = node_cot_ref[...].astype(F32) + mm_nt(first_ref[...], entry_ref[:f, :])

    up_own, direct = call(
        pull_far,
        [shape(edges, f, F32), shape(nodes, f, F32)],
        place, edge_count, got_near, pulls, pull_border, edge_cotangent, node_saved[3],
        node_cotangent, node_entry,
        smem=(1,),
        flops=20 * edges * f * own,
    )

    subs = lax.axis_size("sub")
    doms = lax.axis_size("dom")
    inners = lax.axis_size("inner")
    unit = 16 * inners * subs
    weight_rows = -(-(9 * f + 16) // unit) * unit
    half = weight_rows // 2
    piece = half // subs
    block_total = doms * subs
    edge_scale = 1.0 / math.sqrt(edges * block_total * inners)
    node_scale = 1.0 / math.sqrt(nodes * block_total)

    def edge_backward(*refs):
        (place_ref, count_ref, up_own_ref, out_pre_ref, s1_ref, s2_ref, h1_ref, h2_ref, edge_ref,
         near_ref, far_ref, middle_ref, outlet_ref, gain_ref, node_ref, node_gain_ref) = refs[:16]
        halo_refs = refs[16 : 16 + remote]
        up_ref, first_ref, keep_ref, give_ref, table, second, output, acc = refs[16 + remote :]
        for j in range(remote):
            table[pl.ds(j * send, send), :] = halo_refs[j][...]
        folded = fold(table[...])
        parts = [pl.ds(b * size, size) for b in range(blocks)]
        for b, rows in enumerate(parts):
            live = live_column(count_ref, b, size)
            slot = place_ref[b : b + 1, :] - own
            got = gather_folded(slot, column(slot), folded)
            up_ref[rows, :] = up_own_ref[rows, :] + live * got
        gain_sum = jnp.zeros((1, f), F32)
        for b, rows in enumerate(parts):
            into = live_column(count_ref, b, size) * up_ref[rows, :]
            normed, inverse = layer_norm(out_pre_ref[rows, :])
            gain_sum += jnp.sum(into * normed, axis=0, keepdims=True)
            output[rows, :] = norm_backward(into * gain_ref[...], normed, inverse).astype(BF)
        for rows in parts:
            grad = mm_nt(output[rows, :], outlet_ref[...])
            second[rows, :] = (grad * s2_ref[rows, :]).astype(BF)
        for rows in parts:
            grad = mm_nt(second[rows, :], middle_ref[...])
            first_ref[rows, :] = (grad * s1_ref[rows, :]).astype(BF)
        first = first_ref[...]
        acc[:f, :] = mm_tn(edge_ref[...], first).astype(BF)
        acc[f : 2 * f, :] = mm_tn(near_ref[...], first).astype(BF)
        acc[2 * f : 3 * f, :] = mm_tn(far_ref[...], first).astype(BF)
        acc[3 * f : 4 * f, :] = mm_tn(h1_ref[...], second[...]).astype(BF)
        acc[4 * f : 5 * f, :] = mm_tn(h2_ref[...], output[...]).astype(BF)
        acc[5 * f : 9 * f, :] = node_ref[...]
        row = lax.broadcasted_iota(jnp.int32, (weight_rows - 9 * f, f), 0)
        gains = jnp.where(row == 0, gain_sum, 0.0)
        gains = jnp.where(row == 1, node_gain_ref[...] * 0.5, gains)
        acc[9 * f :, :] = gains.astype(BF)
        me = lax.axis_index("inner")
        keep_ref[...] = acc[pl.ds(pl.multiple_of(me * half, 16), half), :]
        give_ref[...] = acc[pl.ds(pl.multiple_of((1 - me) * half, 16), half), :]

    up, first_grad, keep, give = call(
        edge_backward,
        [shape(edges, f, F32), shape(edges, f, BF), shape(half, f, BF), shape(half, f, BF)],
        place, edge_count, up_own, out_pre, s1, s2, h1, h2, edge_state, near_rows, far_rows,
        edge_middle, edge_outlet, gain_e, node_weights, node_gain_grad, *pull_halo,
        smem=(1,),
        scratch=[
            pltpu.VMEM((lay.halo, f), BF),
            pltpu.VMEM((edges, f), BF),
            pltpu.VMEM((edges, f), BF),
            pltpu.VMEM((weight_rows, f), BF),
        ],
        flops=2 * edges * f * (lay.halo + 7 * f),
    )
    got = swap_axis(give, "inner", 1)

    def far_slots(place_ref, first_ref, entry_ref, far_ref, *refs):
        slot_refs, pairs = refs[:-1], refs[-1]
        for b in range(blocks):
            rows = pl.ds(b * size, size)
            far = mm_nt(first_ref[rows, :], entry_ref[2 * f :, :])
            far_ref[rows, :] = far.astype(BF)
            pairs[rows, :] = halves(far, column(place_ref[b : b + 1, :] - own), half_halo)
        hot = folded_hot(whole_row(place_ref) - own, half_halo)
        lay.store_slots(unfold(mm(hot, pairs[...])), slot_refs)

    far_outs = call(
        far_slots,
        [shape(edges, f, BF)] + lay.slot_shapes(f),
        place, first_grad, edge_entry,
        scratch=[pltpu.VMEM((edges, 2 * f), BF)],
        flops=2 * edges * f * (lay.halo + f),
    )
    far_grad = far_outs[0]
    outgoing = lay.outgoing(far_outs[1], far_outs[2:-1], far_outs[-1])
    back = lay.give(outgoing, other_swaps)

    def kept():
        swapped = lax.axis_index("inner") & lax.axis_index("dom") & 1
        return lax.axis_index("sub") ^ swapped

    def split_kernel(keep_ref, got_ref, *refs):
        out_refs, acc = refs[:-1], refs[-1]
        acc[...] = (keep_ref[...].astype(F32) + got_ref[...].astype(F32)).astype(BF)
        t = kept()
        for x in range(subs):
            out_refs[x][...] = acc[pl.ds(pl.multiple_of((t ^ x) * piece, 16), piece), :]

    split = call(
        split_kernel,
        [shape(piece, f, BF)] * subs,
        keep, got,
        scratch=[pltpu.VMEM((half, f), BF)],
    )
    arrived = [split[0]] + [swap_axis(split[x], "sub", x) for x in range(1, subs)]

    def add_values(values):
        values = [value.astype(F32) for value in values]
        while len(values) > 1:
            values = [values[j] + values[j + 1] for j in range(0, len(values), 2)]
        return values[0].astype(BF)

    def join_pieces(slots_ref, *refs):
        refs[-1][:send, :] = slots_ref[...]
        refs[-1][send:, :] = add_values([ref[...] for ref in refs[:-1]])

    (packed,) = call(
        join_pieces, [shape(send + piece, f, BF)], outgoing[near_first], *arrived
    )
    packed_other = lay.permute(packed, 1, (0, 1))
    back.append(packed_other)

    def add_packed(own_ref, other_ref, out_ref):
        out_ref[...] = add_values([own_ref[send:, :], other_ref[send:, :]])

    def add_pieces(own_ref, other_ref, out_ref):
        out_ref[...] = add_values([own_ref[...], other_ref[...]])

    (total,) = call(add_packed, [shape(piece, f, BF)], packed, packed_other)
    stride = 2
    while stride < doms:
        partner = swap_axis(total, "dom", stride)
        (total,) = call(add_pieces, [shape(piece, f, BF)], total, partner)
        stride *= 2
    own_pieces = [total] + [swap_axis(total, "sub", x) for x in range(1, subs)]

    def grad_sums(
        spot_ref, place_ref, send_ref, up_ref, first_ref, far_ref, entry_ref, adjoint_ref,
        out_ref, near_pairs, far_pairs,
    ):
        for b in range(blocks):
            rows = pl.ds(b * size, size)
            first = first_ref[rows, :]
            adjoint_ref[rows, :] = (up_ref[rows, :] + mm_nt(first, entry_ref[:f, :])).astype(BF)
            near = mm_nt(first, entry_ref[f : 2 * f, :])
            far = far_ref[rows, :].astype(F32)
            near_pairs[rows, :] = halves(near, column(spot_ref[b : b + 1, :]), half_near)
            far_pairs[rows, :] = halves(far, column(place_ref[b : b + 1, :]), half_own)
        out_ref[...] = local_sums(spot_ref, place_ref, send_ref, near_pairs, far_pairs)

    edge_adjoint, grad_part = call(
        grad_sums,
        [shape(edges, f, BF), shape(nodes, f, F32)],
        spot, place, sends, up, first_grad, far_grad, edge_entry,
        scratch=pair_scratch,
        flops=2 * edges * f * (nodes + own + 2 * f),
    )

    def order_kernel(*refs):
        t = kept()
        for x in range(subs):
            refs[-1][pl.ds(pl.multiple_of((t ^ x) * piece, 16), piece), :] = refs[x][...]

    (own_half,) = call(order_kernel, [shape(half, f, BF)], *own_pieces)
    other_half = swap_axis(own_half, "inner", 1)

    def finish_kernel(own_ref, other_ref, edge_ref, node_ref, gain_ref, acc):
        me = lax.axis_index("inner")
        acc[pl.ds(pl.multiple_of(me * half, 16), half), :] = own_ref[...]
        acc[pl.ds(pl.multiple_of((1 - me) * half, 16), half), :] = other_ref[...]
        edge_ref[...] = acc[: 5 * f, :].astype(F32) * edge_scale
        node_ref[...] = acc[5 * f : 9 * f, :].astype(F32) * node_scale
        tail = acc[9 * f : 9 * f + 16, :].astype(F32)
        gain_ref[0:1, :] = tail[0:1, :] * edge_scale
        gain_ref[1:2, :] = tail[1:2, :] * node_scale

    edge_gradient, node_gradient, gain_gradient = call(
        finish_kernel,
        [shape(5 * f, f, F32), shape(4 * f, f, F32), shape(2, f, F32)],
        own_half, other_half,
        scratch=[pltpu.VMEM((weight_rows, f), BF)],
    )

    back_part, back_other = join(grad_part, back)
    node_adjoint = (back_part.astype(F32) + back_other.astype(F32) + direct).astype(BF)
    return (
        own_new,
        new_edges,
        node_adjoint,
        edge_adjoint,
        edge_gradient,
        node_gradient,
        gain_gradient,
    )


def solution(mesh):
    nodes = P(("groups", "dom", "sub"), None)
    edges = P(("groups", "dom", "sub", "inner"), None)
    slots = P(("groups", "dom", "sub", "inner"))
    return jax.shard_map(
        per_device,
        mesh=mesh,
        in_specs=(
            nodes,
            edges,
            slots,
            slots,
            slots,
            slots,
            P(("groups", "dom", "sub")),
            P(),
            P(),
            P(),
            P(),
            P(),
            P(),
            P(),
            P(),
            nodes,
            edges,
        ),
        out_specs=(
            nodes,
            edges,
            nodes,
            edges,
            P("groups", None),
            P("groups", None),
            P("groups", None),
        ),
        check_vma=False,
    )
```

```python
import math

import jax
import jax.numpy as jnp
from jax import lax
from jax.experimental import pallas as pl
from jax.experimental.pallas import tpu as pltpu
from jax.sharding import PartitionSpec as P

EPS = 1e-05
BF = jnp.bfloat16
F32 = jnp.float32
AXES = ("dom", "sub", "inner")
BACK_ORDER = (1, 0, 2)
VMEM_LIMIT = 16 * 1024 * 1024


def mm(left, right):
    return jnp.dot(left, right, preferred_element_type=F32)


def mm_tn(left, right):
    return lax.dot_general(left, right, (((0,), (0,)), ((), ())), preferred_element_type=F32)


def mm_nt(left, right):
    return lax.dot_general(left, right, (((1,), (1,)), ((), ())), preferred_element_type=F32)


def silu_pair(pre_act):
    logistic = jax.nn.sigmoid(pre_act)
    act = pre_act * logistic
    return act, logistic + act * (1.0 - logistic)


def layer_norm(output_pre):
    centred = output_pre - jnp.mean(output_pre, axis=-1, keepdims=True)
    inverse = lax.rsqrt(jnp.mean(centred * centred, axis=-1, keepdims=True) + EPS)
    return centred * inverse, inverse


def norm_backward(scaled, normed, inverse):
    return inverse * (
        scaled
        - jnp.mean(scaled, axis=-1, keepdims=True)
        - normed * jnp.mean(scaled * normed, axis=-1, keepdims=True)
    )


def hot_rows(index_row, rows):
    place = lax.broadcasted_iota(jnp.int32, (rows, index_row.shape[1]), 0)
    return jnp.where(place == index_row, 1.0, 0.0).astype(BF)


def folded_hot(index_row, rows):
    return hot_rows(jnp.where(index_row >= rows, index_row - rows, index_row), rows)


def fold(table):
    rows = table.shape[0] // 2
    return jnp.concatenate([table[:rows], table[rows:]], axis=1)


def unfold(table):
    f = table.shape[1] // 2
    return jnp.concatenate([table[:, :f], table[:, f:]], axis=0)


def gather_folded(index_row, index_col, table):
    rows, f = table.shape[0], table.shape[1] // 2
    got = mm_tn(folded_hot(index_row, rows), table)
    return jnp.where(index_col >= rows, got[:, f:], got[:, :f])


def halves(values, index_col, rows):
    upper = index_col >= rows
    zero = jnp.zeros_like(values)
    return jnp.concatenate(
        [jnp.where(upper, zero, values), jnp.where(upper, values, zero)], axis=1
    ).astype(BF)


def column(row):
    wide = jnp.broadcast_to(row, (8, row.shape[1]))
    return jnp.transpose(wide)[:, :1]


class Layout:
    def __init__(self, nodes, send):
        self.nodes, self.send = nodes, send
        self.sub = lax.axis_size("sub")
        self.dom = lax.axis_size("dom")
        self.halo = (3 * self.sub - 1) * send

    def place(self, other):
        d, t, core = (lax.axis_index(name) for name in AXES)
        slot = jnp.maximum(other - self.nodes, 0)
        layer = slot // (self.sub * self.send)
        rest = slot - layer * (self.sub * self.send)
        peer = rest // self.send
        k = rest - peer * self.send
        upper = (layer == 2).astype(jnp.int32)
        even = 1 - lax.rem(d, 2)
        x = peer ^ t
        pair = x >> 1
        near = upper == even
        mine = near == ((x & 1) == core)
        group = jnp.where(near, self.sub // 2 + pair, pair)
        group += jnp.where(mine, 1, 2 * self.sub)
        group = jnp.where(layer == 1, jnp.where(x > 0, self.sub + x, 0), group)
        row = self.nodes + group * self.send + k
        return jnp.where(other < self.nodes, other, row)

    def permute(self, value, layer, x):
        inner = lax.axis_size("inner")
        pairs = []
        for d in range(self.dom):
            other = (d, d ^ 1, ((d + 1) ^ 1) - 1)[layer]
            if not 0 <= other < self.dom:
                continue
            for t in range(self.sub):
                for i in range(inner):
                    source = (d * self.sub + t) * inner + i
                    pairs.append((source, (other * self.sub + (t ^ x[i])) * inner + i))
        return lax.ppermute(value, AXES, pairs)

    def swaps(self):
        pairs = range(0, self.sub, 2)
        steps = [(2, (x + 1, x)) for x in pairs] + [(1, (x, x + 1)) for x in pairs]
        return steps + [(0, (x, x)) for x in range(1, self.sub)]

    def fetch(self, border):
        return [self.permute(border, layer, x) for layer, x in self.swaps()]

    def fetch_theirs(self, got):
        return [swap_axis(value, "inner", 1) for value in got[: self.sub]]

    def outgoing(self, mine, own, theirs):
        got = swap_axis(theirs, "inner", 1)
        send = self.send

        def add_kernel(mine_ref, got_ref, *outs):
            total = (mine_ref[...] + got_ref[...].astype(F32)).astype(BF)
            for x, out in enumerate(outs):
                out[...] = total[x * send : (x + 1) * send]

        rows = [shape(send, mine.shape[1], BF)] * self.sub
        return list(call(add_kernel, rows, mine, got)) + list(own)

    def give(self, values, which):
        swaps = self.swaps()
        return [self.permute(values[j], *swaps[j]) for j in which]

    def slot_shapes(self, f):
        block = self.sub * self.send
        own = [shape(self.send, f, BF)] * (self.sub - 1)
        return [shape(block, f, F32)] + own + [shape(block, f, BF)]

    def store_slots(self, sums, refs):
        block, send = self.sub * self.send, self.send
        refs[0][...] = sums[:block]
        for j in range(self.sub - 1):
            refs[1 + j][...] = sums[block + j * send : block + (j + 1) * send].astype(BF)
        refs[-1][...] = sums[self.halo - block :].astype(BF)


def swap_axis(value, axis, mask):
    count = lax.axis_size(axis)
    return lax.ppermute(value, axis, [(j, j ^ mask) for j in range(count)])


def call(body, outs, *args, smem=(), hbm=(), scratch=(), flops=0, after=()):
    first, passed = len(args), len(after)
    specs = []
    for j in range(first):
        space = pltpu.SMEM if j in smem else pltpu.HBM if j in hbm else pltpu.VMEM
        specs.append(pl.BlockSpec(memory_space=space))
    anywhere = [pl.BlockSpec(memory_space=pl.ANY)] * passed
    size = sum(math.prod(a.shape) * a.dtype.itemsize for a in (*args, *outs))

    def inner(*refs):
        body(*refs[:first], *refs[first + passed : first + passed + len(outs)],
             *refs[first + 2 * passed + len(outs) :])

    return pl.pallas_call(
        inner,
        out_shape=list(outs) + [jax.ShapeDtypeStruct(a.shape, a.dtype) for a in after],
        in_specs=specs + anywhere,
        out_specs=[pl.BlockSpec(memory_space=pltpu.VMEM) for _ in outs] + anywhere,
        scratch_shapes=list(scratch),
        input_output_aliases={first + j: len(outs) + j for j in range(passed)},
        compiler_params=pltpu.CompilerParams(vmem_limit_bytes=VMEM_LIMIT),
        cost_estimate=pl.CostEstimate(flops=flops, bytes_accessed=size, transcendentals=0),
    )(*args, *after)


def shape(rows, cols, dtype):
    return jax.ShapeDtypeStruct((rows, cols), dtype)


def first_kernel(out_ref):
    out_ref[...] = jnp.zeros(out_ref.shape, F32)


def border_kernel(send_ref, table_ref, first_ref, out_ref):
    hot = hot_rows(send_ref[...], table_ref.shape[0])
    out_ref[...] = mm_tn(hot, table_ref[...]).astype(BF)


def live_column(count_ref, b, size):
    row = lax.broadcasted_iota(jnp.int32, (size, 1), 0) + b * size
    return jnp.where(row < count_ref[0], 1.0, 0.0)


def whole_row(ref):
    return jnp.concatenate([ref[b : b + 1, :] for b in range(ref.shape[0])], axis=1)


def per_device(
    node_state,
    edge_state,
    edge_count,
    block_start,
    edge_offset,
    edge_other,
    send_index,
    edge_entry,
    edge_middle,
    edge_outlet,
    edge_gain,
    node_entry,
    node_middle,
    node_outlet,
    node_gain,
    node_cotangent,
    edge_cotangent,
):
    nodes, feat = node_state.shape
    edges = edge_state.shape[0]
    blocks = block_start.shape[0]
    size = edges // blocks
    send = send_index.shape[0]
    lay = Layout(nodes, send)
    remote = 3 * lay.sub - 1
    outward = lay.sub + 1
    own = nodes + send
    half_near, half_own, half_halo = nodes // 2, own // 2, lay.halo // 2
    f = feat

    sends = send_index.reshape(1, send)
    gain_e = edge_gain.reshape(1, f)
    gain_n = node_gain.reshape(1, f)

    (first,) = call(first_kernel, [shape(8, f, F32)])
    (border,) = call(border_kernel, [shape(send, f, BF)], sends, node_state, first)
    halo = lay.fetch(border)

    def edge_near(
        off_ref, oth_ref, start_ref, node_ref, gain_ref, near_ref, place_ref, spot_ref,
        gain_out_ref,
    ):
        gain_out_ref[...] = gain_ref[...]
        table = fold(node_ref[...])
        for b in range(blocks):
            rows = pl.ds(b * size, size)
            spot = off_ref[rows].reshape(1, size) + start_ref[b]
            spot_ref[b : b + 1, :] = spot
            place_ref[b : b + 1, :] = lay.place(oth_ref[rows].reshape(1, size))
            near_ref[rows, :] = gather_folded(spot, column(spot), table).astype(BF)

    near_rows, place, spot, gain_e = call(
        edge_near,
        [
            shape(edges, f, BF),
            shape(blocks, size, jnp.int32),
            shape(blocks, size, jnp.int32),
            shape(1, f, F32),
        ],
        edge_offset, edge_other, block_start, node_state, gain_e,
        smem=(2,),
        flops=2 * edges * f * nodes,
    )
    halo += lay.fetch_theirs(halo)

    def edge_far(place_ref, node_ref, border_ref, far_ref):
        table = fold(jnp.concatenate([node_ref[...], border_ref[...]], axis=0))
        for b in range(blocks):
            place = place_ref[b : b + 1, :]
            got = gather_folded(place, column(place), table)
            far_ref[pl.ds(b * size, size), :] = got.astype(BF)

    (far_own,) = call(
        edge_far,
        [shape(edges, f, BF)],
        place, node_state, border,
        flops=20 * edges * f * own,
    )

    def edge_forward(*refs):
        (place_ref, count_ref, edge_ref, far_own_ref, near_ref, entry_ref, middle_ref,
         outlet_ref, gain_ref) = refs[:9]
        halo_refs = refs[9 : 9 + remote]
        (message_ref, far_ref, h1_ref, h2_ref, s1_ref, s2_ref, out_ref) = refs[
            9 + remote : 16 + remote
        ]
        slot_refs = refs[16 + remote : 16 + remote + outward]
        table, pairs = refs[16 + remote + outward :]
        for j in range(remote):
            table[pl.ds(j * send, send), :] = halo_refs[j][...]
        folded = fold(table[...])
        slots = [place_ref[b : b + 1, :] - own for b in range(blocks)]
        cols = [column(slot) for slot in slots]
        parts = [pl.ds(b * size, size) for b in range(blocks)]
        for slot, col, rows in zip(slots, cols, parts):
            far = gather_folded(slot, col, folded)
            far_ref[rows, :] = (far + far_own_ref[rows, :].astype(F32)).astype(BF)
        for rows in parts:
            inputs = [edge_ref[rows, :], near_ref[rows, :], far_ref[rows, :]]
            act, slope = silu_pair(mm(jnp.concatenate(inputs, axis=1), entry_ref[...]))
            h1_ref[rows, :] = act.astype(BF)
            s1_ref[rows, :] = slope
        for rows in parts:
            act, slope = silu_pair(mm(h1_ref[rows, :], middle_ref[...]))
            h2_ref[rows, :] = act.astype(BF)
            s2_ref[rows, :] = slope
        for rows in parts:
            out_ref[rows, :] = mm(h2_ref[rows, :], outlet_ref[...])
        for b, (col, rows) in enumerate(zip(cols, parts)):
            normed, _ = layer_norm(out_ref[rows, :])
            live = live_column(count_ref, b, size)
            state = edge_ref[rows, :].astype(F32)
            new = (state + live * gain_ref[...] * normed).astype(BF)
            message = new.astype(F32) * live
            message_ref[rows, :] = message.astype(BF)
            pairs[rows, :] = halves(message, col, half_halo)
        hot = folded_hot(whole_row(place_ref) - own, half_halo)
        lay.store_slots(unfold(mm(hot, pairs[...])), slot_refs)

    edge_outs = call(
        edge_forward,
        [shape(edges, f, BF)] * 4
        + [shape(edges, f, F32)] * 3
        + lay.slot_shapes(f),
        place, edge_count, edge_state, far_own, near_rows, edge_entry, edge_middle, edge_outlet,
        gain_e, *halo,
        smem=(1,),
        scratch=[pltpu.VMEM((lay.halo, f), BF), pltpu.VMEM((edges, 2 * f), BF)],
        flops=2 * edges * f * (2 * lay.halo + 5 * f),
    )
    message, far_rows, h1, h2, s1, s2, out_pre = edge_outs[:7]
    outgoing = lay.outgoing(edge_outs[7], edge_outs[8:-1], edge_outs[-1])
    near_first = lay.sub // 2
    other_swaps = [j for j in range(len(outgoing)) if j != near_first]
    received = lay.give(outgoing, [near_first] + other_swaps)

    def local_sums(spot_ref, place_ref, send_ref, near_pairs, far_pairs):
        total = unfold(mm(folded_hot(whole_row(spot_ref), half_near), near_pairs[...]))
        sums = unfold(mm(folded_hot(whole_row(place_ref), half_own), far_pairs[...]))
        slot = sums[nodes:].astype(BF)
        return total + sums[:nodes] + mm(hot_rows(send_ref[...], nodes), slot)

    pair_scratch = [pltpu.VMEM((edges, 2 * f), BF), pltpu.VMEM((edges, 2 * f), BF)]

    def message_sums(
        spot_ref, place_ref, send_ref, count_ref, edge_ref, message_ref, new_ref, out_ref,
        near_pairs, far_pairs,
    ):
        for b in range(blocks):
            rows = pl.ds(b * size, size)
            message = message_ref[rows, :].astype(F32)
            live = live_column(count_ref, b, size) > 0.0
            new_ref[rows, :] = jnp.where(live, message, edge_ref[rows, :].astype(F32)).astype(BF)
            near_pairs[rows, :] = halves(message, column(spot_ref[b : b + 1, :]), half_near)
            far_pairs[rows, :] = halves(message, column(place_ref[b : b + 1, :]), half_own)
        out_ref[...] = local_sums(spot_ref, place_ref, send_ref, near_pairs, far_pairs)

    new_edges, message_part = call(
        message_sums,
        [shape(edges, f, BF), shape(nodes, f, F32)],
        spot, place, sends, edge_count, edge_state, message,
        smem=(3,),
        scratch=pair_scratch,
        flops=2 * edges * f * (nodes + own),
    )

    def join_kernel(send_ref, own_ref, *refs):
        hot = hot_rows(send_ref[...], nodes)
        total = own_ref[...]
        for ref in refs[:-1]:
            total += mm(hot, ref[:send, :])
        refs[-1][...] = total.astype(BF)

    def join(part, arrived):
        (out,) = call(
            join_kernel, [shape(nodes, f, BF)], sends, part, *arrived,
            flops=2 * nodes * send * f * len(arrived),
        )
        return out, swap_axis(out, "inner", 1)

    part, part_other = join(message_part, received)

    def node_kernel(
        part_ref, other_ref, node_ref, cot_ref, send_ref, entry_ref, middle_ref, outlet_ref,
        gain_ref, new_ref, pulls_ref, border_ref, totals_ref, h1_ref, h2_ref, first_ref,
        second_ref, og_ref, gain_grad_ref, slope1, slope2,
    ):
        part_rows = nodes // 4
        parts = [pl.ds(j * part_rows, part_rows) for j in range(4)]
        for rows in parts:
            totals = part_ref[rows, :].astype(F32) + other_ref[rows, :].astype(F32)
            totals_ref[rows, :] = totals.astype(BF)
        for rows in parts:
            inputs = jnp.concatenate([node_ref[rows, :], totals_ref[rows, :]], axis=1)
            act, slope = silu_pair(mm(inputs, entry_ref[...]))
            h1_ref[rows, :] = act.astype(BF)
            slope1[rows, :] = slope
        for rows in parts:
            act, slope = silu_pair(mm(h1_ref[rows, :], middle_ref[...]))
            h2_ref[rows, :] = act.astype(BF)
            slope2[rows, :] = slope
        gain_sum = jnp.zeros((1, f), F32)
        for rows in parts:
            normed, inverse = layer_norm(mm(h2_ref[rows, :], outlet_ref[...]))
            new = node_ref[rows, :].astype(F32) + gain_ref[...] * normed
            new_ref[rows, :] = new.astype(BF)
            up = cot_ref[rows, :].astype(F32)
            gain_sum += jnp.sum(up * normed, axis=0, keepdims=True)
            og_ref[rows, :] = norm_backward(up * gain_ref[...], normed, inverse).astype(BF)
        gain_grad_ref[...] = gain_sum
        for rows in parts:
            grad = mm_nt(og_ref[rows, :], outlet_ref[...])
            second_ref[rows, :] = (grad * slope2[rows, :]).astype(BF)
        for rows in parts:
            grad = mm_nt(second_ref[rows, :], middle_ref[...])
            first_ref[rows, :] = (grad * slope1[rows, :]).astype(BF)
        for rows in parts:
            pulls_ref[rows, :] = mm_nt(first_ref[rows, :], entry_ref[f:, :]).astype(BF)
        border_ref[...] = mm_tn(hot_rows(send_ref[...], nodes), pulls_ref[...]).astype(BF)

    node_outs = call(
        node_kernel,
        [
            shape(nodes, f, BF),
            shape(nodes, f, BF),
            shape(send, f, BF),
        ]
        + [shape(nodes, f, BF)] * 6
        + [shape(1, f, F32)],
        part, part_other, node_state, node_cotangent, sends, node_entry, node_middle,
        node_outlet, gain_n,
        scratch=[pltpu.VMEM((nodes, f), F32), pltpu.VMEM((nodes, f), F32)],
        flops=2 * nodes * f * f * 8,
    )
    new_rows, pulls, pull_border = node_outs[:3]
    node_saved, node_gain_grad = node_outs[3:9], node_outs[9]
    pull_halo = lay.fetch(pull_border)

    def pull_near(
        spot_ref, pulls_ref, node_ref, totals_ref, h1_ref, h2_ref, first_ref, second_ref, og_ref,
        new_ref, got_ref, weight_ref, own_new_ref,
    ):
        table = fold(pulls_ref[...])
        for b in range(blocks):
            spot = spot_ref[b : b + 1, :]
            got = gather_folded(spot, column(spot), table)
            got_ref[pl.ds(b * size, size), :] = got.astype(BF)
        first = first_ref[...]
        weight_ref[:f, :] = (0.5 * mm_tn(node_ref[...], first)).astype(BF)
        weight_ref[f : 2 * f, :] = (0.5 * mm_tn(totals_ref[...], first)).astype(BF)
        weight_ref[2 * f : 3 * f, :] = (0.5 * mm_tn(h1_ref[...], second_ref[...])).astype(BF)
        weight_ref[3 * f :, :] = (0.5 * mm_tn(h2_ref[...], og_ref[...])).astype(BF)
        own_new_ref[...] = new_ref[...]

    got_near, node_weights, own_new = call(
        pull_near,
        [shape(edges, f, BF), shape(4 * f, f, BF), shape(nodes, f, BF)],
        spot, pulls, node_state, *node_saved, new_rows,
        flops=2 * edges * f * nodes + 8 * nodes * f * f,
    )
    pull_halo += lay.fetch_theirs(pull_halo)

    def pull_far(
        place_ref, count_ref, got_ref, pulls_ref, border_ref, cot_ref, first_ref, node_cot_ref,
        entry_ref, up_ref, direct_ref,
    ):
        table = fold(jnp.concatenate([pulls_ref[...], border_ref[...]], axis=0))
        for b in range(blocks):
            rows = pl.ds(b * size, size)
            place = place_ref[b : b + 1, :]
            got = got_ref[rows, :].astype(F32) + gather_folded(place, column(place), table)
            live = live_column(count_ref, b, size)
            up_ref[rows, :] = cot_ref[rows, :].astype(F32) + live * got
        direct_ref[...] = node_cot_ref[...].astype(F32) + mm_nt(first_ref[...], entry_ref[:f, :])

    up_own, direct = call(
        pull_far,
        [shape(edges, f, F32), shape(nodes, f, F32)],
        place, edge_count, got_near, pulls, pull_border, edge_cotangent, node_saved[3],
        node_cotangent, node_entry,
        smem=(1,),
        flops=20 * edges * f * own,
    )

    subs = lax.axis_size("sub")
    doms = lax.axis_size("dom")
    inners = lax.axis_size("inner")
    unit = 16 * inners * subs
    weight_rows = -(-(9 * f + 16) // unit) * unit
    half = weight_rows // 2
    piece = half // subs
    block_total = doms * subs
    edge_scale = 1.0 / math.sqrt(edges * block_total * inners)
    node_scale = 1.0 / math.sqrt(nodes * block_total)

    def edge_backward(*refs):
        (place_ref, count_ref, up_own_ref, out_pre_ref, s1_ref, s2_ref, h1_ref, h2_ref, edge_ref,
         near_ref, far_ref, middle_ref, outlet_ref, gain_ref, node_ref, node_gain_ref) = refs[:16]
        halo_refs = refs[16 : 16 + remote]
        up_ref, first_ref, keep_ref, give_ref, table, second, output, acc = refs[16 + remote :]
        for j in range(remote):
            table[pl.ds(j * send, send), :] = halo_refs[j][...]
        folded = fold(table[...])
        parts = [pl.ds(b * size, size) for b in range(blocks)]
        for b, rows in enumerate(parts):
            live = live_column(count_ref, b, size)
            slot = place_ref[b : b + 1, :] - own
            got = gather_folded(slot, column(slot), folded)
            up_ref[rows, :] = up_own_ref[rows, :] + live * got
        gain_sum = jnp.zeros((1, f), F32)
        for b, rows in enumerate(parts):
            into = live_column(count_ref, b, size) * up_ref[rows, :]
            normed, inverse = layer_norm(out_pre_ref[rows, :])
            gain_sum += jnp.sum(into * normed, axis=0, keepdims=True)
            output[rows, :] = norm_backward(into * gain_ref[...], normed, inverse).astype(BF)
        for rows in parts:
            grad = mm_nt(output[rows, :], outlet_ref[...])
            second[rows, :] = (grad * s2_ref[rows, :]).astype(BF)
        for rows in parts:
            grad = mm_nt(second[rows, :], middle_ref[...])
            first_ref[rows, :] = (grad * s1_ref[rows, :]).astype(BF)
        first = first_ref[...]
        inputs = jnp.concatenate([edge_ref[...], near_ref[...], far_ref[...]], axis=1)
        acc[: 3 * f, :] = mm_tn(inputs, first).astype(BF)
        acc[3 * f : 4 * f, :] = mm_tn(h1_ref[...], second[...]).astype(BF)
        acc[4 * f : 5 * f, :] = mm_tn(h2_ref[...], output[...]).astype(BF)
        acc[5 * f : 9 * f, :] = node_ref[...]
        row = lax.broadcasted_iota(jnp.int32, (weight_rows - 9 * f, f), 0)
        gains = jnp.where(row == 0, gain_sum, 0.0)
        gains = jnp.where(row == 1, node_gain_ref[...] * 0.5, gains)
        acc[9 * f :, :] = gains.astype(BF)
        me = lax.axis_index("inner")
        keep_ref[...] = acc[pl.ds(pl.multiple_of(me * half, 16), half), :]
        give_ref[...] = acc[pl.ds(pl.multiple_of((1 - me) * half, 16), half), :]

    up, first_grad, keep, give = call(
        edge_backward,
        [shape(edges, f, F32), shape(edges, f, BF), shape(half, f, BF), shape(half, f, BF)],
        place, edge_count, up_own, out_pre, s1, s2, h1, h2, edge_state, near_rows, far_rows,
        edge_middle, edge_outlet, gain_e, node_weights, node_gain_grad, *pull_halo,
        smem=(1,),
        scratch=[
            pltpu.VMEM((lay.halo, f), BF),
            pltpu.VMEM((edges, f), BF),
            pltpu.VMEM((edges, f), BF),
            pltpu.VMEM((weight_rows, f), BF),
        ],
        flops=2 * edges * f * (lay.halo + 7 * f),
    )
    got = swap_axis(give, "inner", 1)

    def far_slots(place_ref, first_ref, entry_ref, far_ref, *refs):
        slot_refs, pairs = refs[:-1], refs[-1]
        for b in range(blocks):
            rows = pl.ds(b * size, size)
            far = mm_nt(first_ref[rows, :], entry_ref[2 * f :, :])
            far_ref[rows, :] = far.astype(BF)
            pairs[rows, :] = halves(far, column(place_ref[b : b + 1, :] - own), half_halo)
        hot = folded_hot(whole_row(place_ref) - own, half_halo)
        lay.store_slots(unfold(mm(hot, pairs[...])), slot_refs)

    far_outs = call(
        far_slots,
        [shape(edges, f, BF)] + lay.slot_shapes(f),
        place, first_grad, edge_entry,
        scratch=[pltpu.VMEM((edges, 2 * f), BF)],
        flops=2 * edges * f * (lay.halo + f),
    )
    far_grad = far_outs[0]
    outgoing = lay.outgoing(far_outs[1], far_outs[2:-1], far_outs[-1])
    back = lay.give(outgoing, other_swaps)

    def kept():
        swapped = lax.axis_index("inner") & lax.axis_index("dom") & 1
        return lax.axis_index("sub") ^ swapped

    def split_kernel(keep_ref, got_ref, *refs):
        out_refs, acc = refs[:-1], refs[-1]
        acc[...] = (keep_ref[...].astype(F32) + got_ref[...].astype(F32)).astype(BF)
        t = kept()
        for x in range(subs):
            out_refs[x][...] = acc[pl.ds(pl.multiple_of((t ^ x) * piece, 16), piece), :]

    split = call(
        split_kernel,
        [shape(piece, f, BF)] * subs,
        keep, got,
        scratch=[pltpu.VMEM((half, f), BF)],
    )
    arrived = [split[0]] + [swap_axis(split[x], "sub", x) for x in range(1, subs)]

    def add_values(values):
        values = [value.astype(F32) for value in values]
        while len(values) > 1:
            values = [values[j] + values[j + 1] for j in range(0, len(values), 2)]
        return values[0].astype(BF)

    def join_pieces(slots_ref, *refs):
        refs[-1][:send, :] = slots_ref[...]
        refs[-1][send:, :] = add_values([ref[...] for ref in refs[:-1]])

    (packed,) = call(
        join_pieces, [shape(send + piece, f, BF)], outgoing[near_first], *arrived
    )
    packed_other = lay.permute(packed, 1, (0, 1))
    back.append(packed_other)

    def add_packed(own_ref, other_ref, out_ref):
        out_ref[...] = add_values([own_ref[send:, :], other_ref[send:, :]])

    def add_pieces(own_ref, other_ref, out_ref):
        out_ref[...] = add_values([own_ref[...], other_ref[...]])

    (total,) = call(add_packed, [shape(piece, f, BF)], packed, packed_other)
    stride = 2
    while stride < doms:
        partner = swap_axis(total, "dom", stride)
        (total,) = call(add_pieces, [shape(piece, f, BF)], total, partner)
        stride *= 2
    own_pieces = [total] + [swap_axis(total, "sub", x) for x in range(1, subs)]

    def grad_sums(
        spot_ref, place_ref, send_ref, up_ref, first_ref, far_ref, entry_ref, adjoint_ref,
        out_ref, near_pairs, far_pairs,
    ):
        for b in range(blocks):
            rows = pl.ds(b * size, size)
            first = first_ref[rows, :]
            adjoint_ref[rows, :] = (up_ref[rows, :] + mm_nt(first, entry_ref[:f, :])).astype(BF)
            near = mm_nt(first, entry_ref[f : 2 * f, :])
            far = far_ref[rows, :].astype(F32)
            near_pairs[rows, :] = halves(near, column(spot_ref[b : b + 1, :]), half_near)
            far_pairs[rows, :] = halves(far, column(place_ref[b : b + 1, :]), half_own)
        out_ref[...] = local_sums(spot_ref, place_ref, send_ref, near_pairs, far_pairs)

    edge_adjoint, grad_part = call(
        grad_sums,
        [shape(edges, f, BF), shape(nodes, f, F32)],
        spot, place, sends, up, first_grad, far_grad, edge_entry,
        scratch=pair_scratch,
        flops=2 * edges * f * (nodes + own + 2 * f),
    )

    def order_kernel(*refs):
        t = kept()
        for x in range(subs):
            refs[-1][pl.ds(pl.multiple_of((t ^ x) * piece, 16), piece), :] = refs[x][...]

    (own_half,) = call(order_kernel, [shape(half, f, BF)], *own_pieces)
    other_half = swap_axis(own_half, "inner", 1)

    def finish_kernel(own_ref, other_ref, edge_ref, node_ref, gain_ref, acc):
        me = lax.axis_index("inner")
        acc[pl.ds(pl.multiple_of(me * half, 16), half), :] = own_ref[...]
        acc[pl.ds(pl.multiple_of((1 - me) * half, 16), half), :] = other_ref[...]
        edge_ref[...] = acc[: 5 * f, :].astype(F32) * edge_scale
        node_ref[...] = acc[5 * f : 9 * f, :].astype(F32) * node_scale
        tail = acc[9 * f : 9 * f + 16, :].astype(F32)
        gain_ref[0:1, :] = tail[0:1, :] * edge_scale
        gain_ref[1:2, :] = tail[1:2, :] * node_scale

    edge_gradient, node_gradient, gain_gradient = call(
        finish_kernel,
        [shape(5 * f, f, F32), shape(4 * f, f, F32), shape(2, f, F32)],
        own_half, other_half,
        scratch=[pltpu.VMEM((weight_rows, f), BF)],
    )

    back_part, back_other = join(grad_part, back)
    node_adjoint = (back_part.astype(F32) + back_other.astype(F32) + direct).astype(BF)
    return (
        own_new,
        new_edges,
        node_adjoint,
        edge_adjoint,
        edge_gradient,
        node_gradient,
        gain_gradient,
    )


def solution(mesh):
    nodes = P(("groups", "dom", "sub"), None)
    edges = P(("groups", "dom", "sub", "inner"), None)
    slots = P(("groups", "dom", "sub", "inner"))
    return jax.shard_map(
        per_device,
        mesh=mesh,
        in_specs=(
            nodes,
            edges,
            slots,
            slots,
            slots,
            slots,
            P(("groups", "dom", "sub")),
            P(),
            P(),
            P(),
            P(),
            P(),
            P(),
            P(),
            P(),
            nodes,
            edges,
        ),
        out_specs=(
            nodes,
            edges,
            nodes,
            edges,
            P("groups", None),
            P("groups", None),
            P("groups", None),
        ),
        check_vma=False,
    )
```
